32 devices in a mesh: blk: 16 (over z, y, x), grp: 2 (over core).
Axes of the slice: x: 2, y: 2, z: 4, core: 2. Of those that a mesh axis runs over, the one named last changes fastest.
Arguments:
- query_tokens: bfloat16 [1024, 32, 768], P(('blk', 'grp')), may hold values from -6 to 6
- passage_tokens: bfloat16 [64, 512, 768], P(('blk', 'grp')), may hold values from -6 to 6
- lengths: int32 [64, 4], P(('blk', 'grp')), may hold values from 1 to 256, 512 in all within a row
- labels: int32 [1024], P(('blk', 'grp')), may hold values from 0 to 255
- attn_in: bfloat16 [2, 768, 2304], replicated, may hold values from -0.21875 to 0.21875
- attn_out: bfloat16 [2, 768, 768], replicated, may hold values from -1.75 to 1.75
- ffn_in: bfloat16 [2, 768, 3072], replicated, may hold values from -0.21875 to 0.21875
- ffn_out: bfloat16 [2, 3072, 768], replicated, may hold values from -0.109375 to 0.109375
- gains: float32 [2, 2, 768], replicated, may hold values from 0.5 to 1.5
- biases: float32 [2, 6, 768], replicated, may hold values from -1.2 to 1.2
- ffn_bias: float32 [2, 3072], replicated, may hold values from -1.2 to 1.2
Outputs:
- query_losses: float32 [1024], P(('blk', 'grp'))
- query_out: bfloat16 [1024, 32, 768], P(('blk', 'grp'))
- passage_out: bfloat16 [64, 512, 768], P(('blk', 'grp'))
- query_grad: float32 [1024, 32, 768], P(('blk', 'grp'))
- passage_grad: float32 [64, 512, 768], P(('blk', 'grp'))
- grad_attn_in: float32 [2, 768, 2304], P(None, 'blk')
- grad_attn_out: float32 [2, 768, 768], P(None, 'blk')
- grad_ffn_in: float32 [2, 768, 3072], P(None, 'blk')
- grad_ffn_out: float32 [2, 3072, 768], P(None, 'blk')
- grad_gains: float32 [2, 2, 768], P(None, None, 'blk')
- grad_biases: float32 [2, 6, 768], P(None, None, 'blk')
- grad_ffn_bias: float32 [2, 3072], P(None, 'blk')
The draws below stay inside these ranges and needn't reach their ends.
Inputs may be any that keep to these rules, and one draw needn't show every extreme that they name: In each row the lengths sum to 512, and the longest is exactly 256.
All inputs are finite; a program needn't handle non-finite values.
Results may differ from the reference program's by a relative error of at most 0.024.
Values may be sent and summed in bfloat16 or wider, within the bound.
A program may use at most 256 MiB of HBM per device.

```python
import math
import jax
import jax.numpy as jnp
import numpy as np
from jax import lax

D = 768
HEAD_DIM = 64
FF = 3072
QLEN = 32
PLEN = 512
NPASS = 4
MOST = 256
QDEV = 32
NQ_ALL = 1024
NPR = 64
NP_ALL = 256


def set_ends(array, key, smallest, high):
    index_at = [jax.random.randint(jax.random.fold_in(key, axis), (), 0, length) for axis, length in enumerate(array.shape)]
    widest = array.shape.index(max(array.shape))
    neighbour = index_at[:widest] + [(index_at[widest] + 1) % array.shape[widest]] + index_at[widest + 1:]
    return array.at[tuple(index_at)].set(smallest).at[tuple(neighbour)].set(high)


def levels(own_key, dims, pieces, smallest, top_value):
    def one(dim, parts):
        steps = jax.random.uniform(jax.random.fold_in(jax.random.fold_in(own_key, 6), dim), (parts,), jnp.float32, smallest / len(pieces), top_value / len(pieces))
        return jnp.repeat(jnp.exp(steps), dims[dim] // parts).reshape((-1,) + (1,) * (len(dims) - dim - 1))

    factor_of = one(*pieces[0])
    for cut in pieces[1:]:
        factor_of = factor_of * one(*cut)
    return factor_of


def split_up(count, total, most, skew):
    portions = [(1 << 20) // math.isqrt(grade ** skew) + 1 for grade in range(2, count + 1)]
    rest, given = total - most - (count - 1), [1] * (count - 1)
    while rest > 0:
        free = [i for i in range(count - 1) if given[i] < most]
        pool, remaining = sum([portions[i] for i in free]), rest
        for i in free:
            more = min(most - given[i], max(1, remaining * portions[i] // pool), rest)
            given[i] = given[i] + more
            rest = rest - more
    return np.array([most] + given)


def ragged_sizes(own_key, amount, total, reach, skew):
    if amount == 2:
        one = jax.random.randint(own_key, (), max(1, total - reach), min(reach, total - 1) + 1)
        return jnp.stack([one, total - one])
    sizes = jnp.asarray(split_up(amount, total, reach, skew), jnp.int32)
    couples = (amount - 1) // 2
    source_of, sink = sizes[1:1 + 2 * couples:2], sizes[2:2 + 2 * couples:2]
    margin = jnp.minimum(source_of - 1, reach - sink)
    moved = jax.random.randint(jax.random.fold_in(own_key, 1), (couples,), 0, 1 << 20) % (margin + 1)
    sizes = sizes.at[1:1 + 2 * couples:2].set(source_of - moved).at[2:2 + 2 * couples:2].set(sink + moved)
    return sizes[jax.random.permutation(jax.random.fold_in(own_key, 2), amount)]


def scatter_about(stream_key, extent, scale, limit, pieces=(), held_as=jnp.bfloat16):
    loudness = levels(stream_key, extent, pieces, -0.22, 0.18) if pieces else 1.0
    values = jax.random.normal(stream_key, extent, jnp.float32) * scale * loudness
    return jnp.minimum(jnp.maximum(values, -limit), limit).astype(held_as)


def setup_inputs(seed: int = 0) -> dict:
    streams_of = jax.random.split(jax.random.key(seed), 12)
    return {
        "query_tokens": scatter_about(streams_of[0], (NQ_ALL, QLEN, D), 1.0, 6.0, ((0, 32),)),
        "passage_tokens": scatter_about(streams_of[1], (NPR, PLEN, D), 1.0, 6.0, ((0, 32),)),
        "lengths": jax.vmap(lambda own: ragged_sizes(own, NPASS, PLEN, MOST, 2))(jax.random.split(streams_of[2], NPR)).reshape((NPR, NPASS)).astype(jnp.int32),
        "labels": set_ends(jax.random.randint(streams_of[3], (NQ_ALL,), 0, NP_ALL), jax.random.fold_in(streams_of[3], 1), 0, NP_ALL - 1).astype(jnp.int32),
        "attn_in": scatter_about(streams_of[4], (2, D, 3 * D), D ** -0.5, 0.21875),
        "attn_out": scatter_about(streams_of[5], (2, D, D), (max(D // 64, 1)) ** -0.5, 1.75),
        "ffn_in": scatter_about(streams_of[6], (2, D, FF), D ** -0.5, 0.21875),
        "ffn_out": scatter_about(streams_of[7], (2, FF, D), FF ** -0.5, 0.109375),
        "gains": jnp.clip(1.0 + 0.1 * jax.random.normal(streams_of[8], (2, 2, D), jnp.float32), 0.5, 1.5),
        "biases": scatter_about(streams_of[9], (2, 6, D), 0.2, 1.2, (), jnp.float32),
        "ffn_bias": scatter_about(streams_of[10], (2, FF), 0.2, 1.2, (), jnp.float32),
    }


EPSILON = 1e-05
SCORE_SCALE = 0.08
KEY_SCALE = 0.125
HIGHEST = lax.Precision.HIGHEST

@jax.custom_vjp
def low(v):
    return lax.optimization_barrier(v.astype(jnp.bfloat16)).astype(jnp.float32)

@jax.custom_vjp
def low_back(v):
    return v

def low_keep(v):
    return (low(v), None)

def low_pass(kept, grad):
    return (grad,)

def back_keep(v):
    return (v, None)

def back_low(kept, grad):
    return (low(grad),)
low.defvjp(low_keep, low_pass)
low_back.defvjp(back_keep, back_low)

def layer_norm(residual, gain_vec, shift_vec):
    centre = residual - lax.optimization_barrier(jnp.mean(residual, -1, keepdims=True))
    spread = lax.optimization_barrier(jnp.mean(centre * centre, -1, keepdims=True))
    return centre * lax.rsqrt(spread + EPSILON) * gain_vec + shift_vec

def tower_layer(inputs, segment, params):
    attn_in, attn_out, ffn_in, ffn_out, gains, biases, ffn_bias = params
    length = inputs.shape[0]
    zeros_vec = jnp.zeros_like(biases[0])
    joined = jnp.dot(inputs, attn_in, precision=HIGHEST) + jnp.concatenate([biases[0], zeros_vec, biases[1]])
    joined = low(low_back(joined)).reshape(length, 3, -1, HEAD_DIM)
    query_part = joined[:, 0]
    key_part = joined[:, 1]
    value_part = joined[:, 2]
    scores = jnp.einsum('qhd,khd->hqk', query_part, key_part, precision=HIGHEST) * KEY_SCALE
    same_seg = segment[:, None] == segment[None, :]
    scores = low_back(jnp.where(same_seg[None], scores, -1000000000.0))
    attention = low(jax.nn.softmax(scores, -1))
    mixed = jnp.einsum('hqk,khd->qhd', attention, value_part, precision=HIGHEST).reshape(length, -1)
    mixed = low(low_back(mixed))
    first_sum = inputs + low_back(jnp.dot(mixed, attn_out, precision=HIGHEST) + biases[2])
    hidden = low(layer_norm(first_sum, gains[0], biases[3]))
    inner = low_back(jnp.dot(hidden, ffn_in, precision=HIGHEST) + ffn_bias)
    active = low(jax.nn.gelu(inner))
    second_sum = hidden + low_back(jnp.dot(active, ffn_out, precision=HIGHEST) + biases[4])
    return low(layer_norm(second_sum, gains[1], biases[5]))

def query_group(group_block, params):
    flat_seg = jnp.zeros((QLEN,), jnp.int32)
    return jax.vmap(lambda single: tower_layer(single, flat_seg, params))(group_block)

def passage_row(single, segment, params):
    return tower_layer(single, segment, params)

def encode(weights, queries, passages, segment, starts, labels):
    query_params = tuple((matrix[0] for matrix in weights))
    passage_params = tuple((matrix[1] for matrix in weights))
    grouped = queries.reshape(-1, QDEV, QLEN, D)
    query_out = lax.map(lambda group_block: jax.checkpoint(query_group)(group_block, query_params), grouped)
    query_out = query_out.reshape(-1, QLEN, D)
    passage_out = lax.map(lambda row_pair: jax.checkpoint(passage_row)(row_pair[0], row_pair[1], passage_params), (passages, segment))
    query_vectors = query_out[:, 0]
    row_index = jnp.arange(passages.shape[0], dtype=jnp.int32)[:, None]
    passage_vectors = passage_out[row_index, starts].reshape(-1, D)
    logits = low_back(SCORE_SCALE * jnp.dot(query_vectors, passage_vectors.T, precision=HIGHEST))
    norm_log = jax.nn.logsumexp(logits, -1)
    positive = jnp.take_along_axis(logits, labels[:, None], 1)[:, 0]
    return (query_out, passage_out, norm_log - positive)

def reference(query_tokens, passage_tokens, lengths, labels, attn_in, attn_out, ffn_in, ffn_out, gains, biases, ffn_bias):
    ends = jnp.cumsum(lengths, -1).astype(jnp.int32)
    starts = (ends - lengths).astype(jnp.int32)
    places = jnp.arange(PLEN, dtype=jnp.int32)
    segment = lax.optimization_barrier(jnp.sum((places[None, :, None] >= ends[:, None, :]).astype(jnp.int32), -1)).astype(jnp.int32)
    weights = tuple((matrix.astype(jnp.float32) for matrix in (attn_in, attn_out, ffn_in, ffn_out, gains, biases, ffn_bias)))
    queries = query_tokens.astype(jnp.float32)
    passages = passage_tokens.astype(jnp.float32)

    def forward(weight_set, query_in, passage_in):
        return encode(weight_set, query_in, passage_in, segment, starts, labels)
    (query_out, passage_out, losses), pullback = jax.vjp(forward, weights, queries, passages)
    weight_grads, query_grad, passage_grad = pullback((jnp.zeros_like(query_out), jnp.zeros_like(passage_out), jnp.ones_like(losses)))
    return (losses, query_out.astype(jnp.bfloat16), passage_out.astype(jnp.bfloat16), query_grad, passage_grad, weight_grads[0], weight_grads[1], weight_grads[2], weight_grads[3], weight_grads[4], weight_grads[5], weight_grads[6])
```

```python
import functools
import jax
import jax.numpy as jnp
from jax import lax
from jax.experimental import pallas as pl
from jax.experimental.pallas import tpu as pltpu
from jax.sharding import PartitionSpec as P

MESH = pl.DeviceIdType.MESH
HEAD_DIM = 64
HEADS = 12
EPSILON = 1e-05
SCORE_SCALE = 0.08
KEY_SCALE = 0.125
NEG = -1000000000.0
F32 = jnp.float32
BF16 = jnp.bfloat16
VMEM_LIMIT = 60 * 1024 * 1024


def dot(a, b):
    return lax.dot_general(a, b, (((1,), (0,)), ((), ())), preferred_element_type=F32)


def dot_nt(a, b):
    return lax.dot_general(a, b, (((1,), (1,)), ((), ())), preferred_element_type=F32)


def dot_tn(a, b):
    return lax.dot_general(a, b, (((0,), (0,)), ((), ())), preferred_element_type=F32)


def iota(shape, dim):
    return lax.broadcasted_iota(jnp.int32, shape, dim)


def head_row(h):
    return iota((1, 768), 1) // HEAD_DIM == h


def expand_heads(rows):
    return jnp.concatenate(
        [jnp.where(head_row(h), rows, 0.0) for h in range(HEADS)], 0
    )


def fold_heads(rows, count):
    out = jnp.where(head_row(0), rows[:count], 0.0)
    for h in range(1, HEADS):
        out = out + jnp.where(head_row(h), rows[h * count:(h + 1) * count], 0.0)
    return out


def norm_stats(residual):
    centre = residual - jnp.mean(residual, -1, keepdims=True)
    inverse = lax.rsqrt(jnp.mean(centre * centre, -1, keepdims=True) + EPSILON)
    return centre * inverse, inverse


def gelu(v):
    return 0.5 * v * (1.0 + jnp.tanh(0.7978845608028654 * (v + 0.044715 * (v * v * v))))


def split3(v):
    hi = v.astype(BF16).astype(F32)
    rest = v - hi
    mid = rest.astype(BF16).astype(F32)
    return hi, mid, rest - mid


def lane_pack(columns, count):
    lane = iota((count, 128), 1)
    out = jnp.zeros((count, 128), F32)
    for j, column in enumerate(columns):
        out = jnp.where(lane == j, column, out)
    return out


def front_kernel(
    lens_ref, labels_ref, gains_ref, biases_ref, ffnb_ref,
    xq_hbm, xp_hbm, win_hbm, wout_hbm, fin_hbm, fout_hbm,
    kvq_ref, kvp_ref, pq_ref, pp_ref, pay_ref, slices_ref, zt_ref,
    innq_ref, innp_ref, invq_ref, invp_ref,
    x_s, win_s, wout_s, fin_s, fout_s, sem,
):
    copies = []
    for t, x_hbm in enumerate((xq_hbm, xp_hbm)):
        copies.append([
            pltpu.make_async_copy(x_hbm, x_s.at[t], sem.at[t, 0]),
            pltpu.make_async_copy(win_hbm.at[t], win_s.at[t], sem.at[t, 1]),
            pltpu.make_async_copy(wout_hbm.at[t], wout_s.at[t], sem.at[t, 2]),
            pltpu.make_async_copy(fin_hbm.at[t], fin_s.at[t], sem.at[t, 3]),
            pltpu.make_async_copy(fout_hbm.at[t], fout_s.at[t], sem.at[t, 4]),
        ])
    for c in copies[0][:2] + copies[1][:2] + copies[0][2:] + copies[1][2:]:
        c.start()

    tokens = x_s.shape[1]
    col_q = iota((32, tokens), 1)
    row_q = iota((32, tokens), 0)
    sel_q = col_q == row_q * 32
    own_q = col_q // 32 == row_q
    col_p = iota((8, tokens), 1)
    row_p = iota((8, tokens), 0)
    lo = jnp.zeros((8, tokens), jnp.int32)
    hi = jnp.zeros((8, tokens), jnp.int32)
    for r in range(2):
        acc = jnp.int32(r * 512)
        for c in range(4):
            length = lens_ref[r, c]
            lo = jnp.where(row_p == r * 4 + c, acc, lo)
            acc = acc + length
            hi = jnp.where(row_p == r * 4 + c, acc, hi)
    sel_p = col_p == lo
    own_p = (col_p >= lo) & (col_p < hi)

    picks = []
    for t, (kv_ref, sel, count) in enumerate(((kvq_ref, sel_q, 32), (kvp_ref, sel_p, 8))):
        copies[t][0].wait()
        copies[t][1].wait()
        value_bias = biases_ref[t, 1:2, :]

        def kv_step(m, _, t=t, kv_ref=kv_ref, value_bias=value_bias):
            rows = pl.ds(pl.multiple_of(m * 256, 256), 256)
            x = x_s[t, rows, :]
            kv_ref[rows, 0:768] = dot(x, win_s[t, :, 768:1536]).astype(BF16)
            kv_ref[rows, 768:1536] = (dot(x, win_s[t, :, 1536:2304]) + value_bias).astype(BF16)
            return 0

        lax.fori_loop(0, tokens // 256, kv_step, 0)
        pick = jnp.where(sel, 1.0, 0.0).astype(BF16)
        xc = dot(pick, x_s[t])
        qc = (dot(xc.astype(BF16), win_s[t, :, 0:768]) + biases_ref[t, 0:1, :]).astype(BF16)
        picks.append((xc, qc))

    done = []
    for t, (kv_ref, own, count, p_ref, inn_ref, inv_ref) in enumerate((
        (kvq_ref, own_q, 32, pq_ref, innq_ref, invq_ref),
        (kvp_ref, own_p, 8, pp_ref, innp_ref, invp_ref),
    )):
        xc, qc = picks[t]
        spread = expand_heads(qc.astype(F32)).astype(BF16)
        scores = dot_nt(spread, kv_ref[:, 0:768]) * KEY_SCALE
        own12 = jnp.concatenate([jnp.where(own, 0.0, NEG)] * HEADS, 0)
        scores = scores + own12
        weight = jnp.exp(scores - jnp.max(scores, -1, keepdims=True))
        soft = weight * (1.0 / jnp.sum(weight, -1, keepdims=True))
        p_ref[...] = soft
        soft16 = soft.astype(BF16)
        mixed = fold_heads(dot(soft16, kv_ref[:, 768:1536]), count).astype(BF16)
        z = dot(soft16, x_s[t])
        copies[t][2].wait()
        first = xc + (dot(mixed, wout_s[t]) + biases_ref[t, 2:3, :])
        n1, inv1 = norm_stats(first)
        hidden = (n1 * gains_ref[t, 0:1, :] + biases_ref[t, 3:4, :]).astype(BF16)
        copies[t][3].wait()
        inner = dot(hidden, fin_s[t]) + ffnb_ref[t:t + 1, :]
        inn_ref[...] = inner
        active = gelu(inner).astype(BF16)
        copies[t][4].wait()
        second = hidden.astype(F32) + (dot(active, fout_s[t]) + biases_ref[t, 4:5, :])
        n2, inv2 = norm_stats(second)
        vec = (n2 * gains_ref[t, 1:2, :] + biases_ref[t, 5:6, :]).astype(BF16)
        inv_ref[...] = lane_pack([inv1, inv2], count)
        if t == 0:
            zt_ref[:, 0:384] = z.T.astype(BF16)
        else:
            wide = jnp.concatenate([z, jnp.zeros((32, 768), F32)], 0)
            zt_ref[:, 384:512] = wide.T.astype(BF16)
        done.append((xc, qc, mixed, hidden, vec, inv1, inv2))

    xq, qq, mq, hq, vq, i1q, i2q = done[0]
    xp, qp, mp, hp, vp, i1p, i2p = done[1]
    lab = labels_ref[...].astype(F32)
    eye = iota((32, 32), 0) == iota((32, 32), 1)
    lab_col = jnp.sum(jnp.where(eye, lab, 0.0), 1, keepdims=True)
    lab_hi = jnp.floor(lab_col * (1.0 / 256.0))
    lab_lo = lab_col - 256.0 * lab_hi
    ext_q = lane_pack([*split3(i1q), *split3(i2q), lab_hi, lab_lo], 32)
    ext_p = lane_pack([*split3(i1p), *split3(i2p)], 8)
    ext = jnp.concatenate(
        [ext_p] + [ext_q[8 * a:8 * a + 8] for a in range(4)] + [jnp.zeros((8, 128), F32)], 1
    )
    pay_ref[0:32, :] = hq
    pay_ref[32:64, :] = vq
    pay_ref[64:96, :] = jnp.concatenate(
        [hp.astype(F32), vp.astype(F32), qp.astype(F32), ext], 0
    ).astype(BF16)
    pay_ref[96:128, :] = qq
    both = jnp.concatenate([mq.astype(F32), xq, mp.astype(F32), xp], 0)
    slices_ref[...] = jnp.zeros(slices_ref.shape, BF16)
    for b in range(16):
        slices_ref[b, :, 0:48] = both[:, 48 * b:48 * b + 48].astype(BF16)


def front(xq, xp, lengths, labels, weights):
    attn_in, attn_out, ffn_in, ffn_out, gains, biases, ffn_bias = weights
    tokens = xq.shape[0]
    vm = pl.BlockSpec(memory_space=pltpu.VMEM)
    hb = pl.BlockSpec(memory_space=pl.ANY)
    sds = jax.ShapeDtypeStruct
    return pl.pallas_call(
        front_kernel,
        out_shape=[
            sds((tokens, 1536), BF16), sds((tokens, 1536), BF16),
            sds((384, tokens), F32), sds((96, tokens), F32),
            sds((128, 768), BF16), sds((16, 80, 128), BF16), sds((768, 512), BF16),
            sds((32, 3072), F32), sds((8, 3072), F32), sds((32, 128), F32), sds((8, 128), F32),
        ],
        in_specs=[pl.BlockSpec(memory_space=pltpu.SMEM), vm, vm, vm, vm] + [hb] * 6,
        out_specs=[vm] * 11,
        scratch_shapes=[
            pltpu.VMEM((2, tokens, 768), BF16),
            pltpu.VMEM((2, 768, 2304), BF16), pltpu.VMEM((2, 768, 768), BF16),
            pltpu.VMEM((2, 768, 3072), BF16), pltpu.VMEM((2, 3072, 768), BF16),
            pltpu.SemaphoreType.DMA((2, 5)),
        ],
        compiler_params=pltpu.CompilerParams(vmem_limit_bytes=VMEM_LIMIT),
        name="front",
    )(lengths, labels.reshape(1, -1), gains, biases, ffn_bias, xq, xp, attn_in, attn_out, ffn_in, ffn_out)


def place():
    me = lax.axis_index("blk")
    return me, lax.axis_index("grp")


def remote(src, dst, send, recv, peer):
    return pltpu.make_async_remote_copy(
        src_ref=src, dst_ref=dst, send_sem=send, recv_sem=recv, device_id=peer, device_id_type=MESH
    )


def barrier_all(me, g):
    barrier = pltpu.get_barrier_semaphore()
    for i in range(1, 16):
        pl.semaphore_signal(barrier, inc=1, device_id=(lax.rem(me + i, 16), g), device_id_type=MESH)
    pl.semaphore_signal(barrier, inc=1, device_id=(me, 1 - g), device_id_type=MESH)
    pl.semaphore_wait(barrier, 16)


def gather_phases(me, g, pay, ga, ss, rs):
    z, yx = me // 4, lax.rem(me, 4)
    xpeer = me + 1 - 2 * lax.rem(me, 2)
    ypeer = me + 2 - 4 * (lax.rem(me, 4) // 2)
    yx_x, yx_y = lax.rem(xpeer, 4), lax.rem(ypeer, 4)
    first, second, third = [], [], []
    for d in range(1, 4):
        peer = lax.rem(z + d, 4) * 4 + yx
        first.append(remote(pay, ga.at[z, yx], ss.at[d - 1], rs.at[d - 1], (peer, g)))
    second.append(remote(ga.at[:, yx], ga.at[:, yx], ss.at[3], rs.at[3], (xpeer, g)))
    second.append(remote(ga.at[:, yx], ga.at[:, yx], ss.at[4], rs.at[4], (ypeer, g)))
    third.append(remote(ga.at[0:2, yx_x], ga.at[0:2, yx_x], ss.at[5], rs.at[5], (ypeer, g)))
    third.append(remote(ga.at[2:4, yx_y], ga.at[2:4, yx_y], ss.at[6], rs.at[6], (xpeer, g)))
    return first, second, third


def main_kernel(
    lens_ref, gains_ref, biases_ref, ffnb_ref, xq_ref, xp_ref, kvq_ref, kvp_ref,
    win_hbm, wout_hbm, fin_hbm, fout_hbm, pay_ref, slices_ref, zt_ref,
    outq_ref, outp_ref, ga_ref, gs_ref, rsl_ref, rzt_ref,
    x_s, q_s, mix_s, wq_s, wout_s, fin_s, fout_s, bias_s,
    sem, lsem, ss, rs, as_, ar,
):
    step = pl.program_id(0)
    tower = step // 4
    me, g = place()
    z, yx = me // 4, lax.rem(me, 4)

    copies = []
    for t in range(2):
        copies.append([
            pltpu.make_async_copy(win_hbm.at[t, :, 0:768], wq_s.at[t], sem.at[t, 0]),
            pltpu.make_async_copy(wout_hbm.at[t], wout_s.at[t], sem.at[t, 1]),
            pltpu.make_async_copy(fin_hbm.at[t], fin_s.at[t], sem.at[t, 2]),
            pltpu.make_async_copy(fout_hbm.at[t], fout_s.at[t], sem.at[t, 3]),
        ])

    first, second, third = gather_phases(me, g, pay_ref, ga_ref, ss, rs)
    fourth = [remote(ga_ref.at[:, :, 32:96], gs_ref, ss.at[7], rs.at[7], (me, 1 - g))]
    swaps = []
    for i in range(1, 16):
        peer = lax.rem(me + i, 16)
        swaps.append(remote(slices_ref.at[peer], rsl_ref.at[me], as_.at[0, i], ar.at[0, i], (peer, g)))
        swaps.append(remote(zt_ref.at[peer], rzt_ref.at[me], as_.at[1, i], ar.at[1, i], (peer, g)))
    locals_ = [
        pltpu.make_async_copy(pay_ref, ga_ref.at[z, yx], lsem.at[0]),
        pltpu.make_async_copy(slices_ref.at[me], rsl_ref.at[me], lsem.at[1]),
        pltpu.make_async_copy(zt_ref.at[me], rzt_ref.at[me], lsem.at[2]),
    ]

    @pl.when(step == 0)
    def _():
        for group in copies:
            for c in group:
                c.start()
        for c in locals_:
            c.start()
        barrier_all(me, g)
        for c in first:
            c.start()

    @pl.when(step == 2)
    def _():
        locals_[0].wait()
        for c in first:
            c.wait()
        for c in second:
            c.start()
        for c in swaps:
            c.start()

    @pl.when(step == 4)
    def _():
        for c in second:
            c.wait()
        for c in third:
            c.start()

    @pl.when(step == 6)
    def _():
        for c in third:
            c.wait()
        for c in fourth:
            c.start()

    @pl.when(step == 0)
    def _():
        copies[0][0].wait()

    @pl.when(step == 4)
    def _():
        copies[1][0].wait()

    @pl.when(step < 4)
    def _():
        x_s[...] = xq_ref[...]

    @pl.when(step >= 4)
    def _():
        x_s[...] = xp_ref[...]

    q_s[...] = (dot(x_s[...], wq_s[tower]) + biases_ref[tower, 0:1, :]).astype(BF16)
    low_half = iota((1, 128), 1) < HEAD_DIM

    @pl.when(step < 4)
    def _():
        same = iota((128, 128), 0) // 32 == iota((128, 128), 1) // 32
        mask = jnp.where(same, 0.0, NEG)
        mask2 = jnp.concatenate([mask, mask], 0)
        for part in range(2):
            rows = slice(part * 128, part * 128 + 128)
            for j in range(HEADS // 2):
                lanes = slice(128 * j, 128 * j + 128)
                q = q_s[rows, lanes]
                k = kvq_ref[rows, lanes]
                v = kvq_ref[rows, 768 + 128 * j:768 + 128 * j + 128]
                zero = jnp.zeros_like(q)
                q2 = jnp.concatenate([jnp.where(low_half, q, zero), jnp.where(low_half, zero, q)], 0)
                s = dot_nt(q2, k) * KEY_SCALE + mask2
                e = jnp.exp(s - jnp.max(s, -1, keepdims=True))
                total = jnp.sum(e, -1, keepdims=True)
                o = dot(e.astype(BF16), v) * (1.0 / total)
                mix_s[rows, lanes] = jnp.where(low_half, o[:128], o[128:]).astype(BF16)

    @pl.when(step >= 4)
    def _():
        row = (step - 4) // 2
        base = lax.rem(step, 2) * 256
        qpos = iota((256, 512), 0) + base
        kpos = iota((256, 512), 1)
        qseg = jnp.zeros((256, 512), jnp.int32)
        kseg = jnp.zeros((256, 512), jnp.int32)
        end = jnp.int32(0)
        for c in range(3):
            end = end + lens_ref[row, c]
            qseg = qseg + jnp.where(qpos >= end, 1, 0)
            kseg = kseg + jnp.where(kpos >= end, 1, 0)
        mask = jnp.where(qseg == kseg, 0.0, NEG)
        bias_s[0:256, :] = mask
        bias_s[256:512, :] = mask
        for j in range(HEADS // 2):
            lanes = slice(128 * j, 128 * j + 128)
            q = q_s[:, lanes]
            k = kvp_ref[:, lanes]
            v = kvp_ref[:, 768 + 128 * j:768 + 128 * j + 128]
            zero = jnp.zeros_like(q)
            q2 = jnp.concatenate([jnp.where(low_half, q, zero), jnp.where(low_half, zero, q)], 0)
            s = dot_nt(q2, k) * KEY_SCALE + bias_s[...]
            e = jnp.exp(s - jnp.max(s, -1, keepdims=True))
            total = jnp.sum(e, -1, keepdims=True)
            o = dot(e.astype(BF16), v) * (1.0 / total)
            mix_s[:, lanes] = jnp.where(low_half, o[:256], o[256:]).astype(BF16)

    for when, t in ((0, 0), (4, 1)):
        @pl.when(step == when)
        def _(t=t):
            for c in copies[t][1:]:
                c.wait()

    first_sum = x_s[...].astype(F32) + (dot(mix_s[...], wout_s[tower]) + biases_ref[tower, 2:3, :])
    n1, _ = norm_stats(first_sum)
    hidden = (n1 * gains_ref[tower, 0:1, :] + biases_ref[tower, 3:4, :]).astype(BF16)
    second_sum = hidden.astype(F32) + biases_ref[tower, 4:5, :]
    for c in range(4):
        cols = slice(768 * c, 768 * c + 768)
        inner = dot(hidden, fin_s[tower, :, cols]) + ffnb_ref[tower, :, cols]
        second_sum = second_sum + dot(gelu(inner).astype(BF16), fout_s[tower, cols, :])
    n2, _ = norm_stats(second_sum)
    out = (n2 * gains_ref[tower, 1:2, :] + biases_ref[tower, 5:6, :]).astype(BF16)

    @pl.when(step < 4)
    def _():
        outq_ref[...] = out

    @pl.when(step >= 4)
    def _():
        outp_ref[...] = out

    @pl.when(step == 7)
    def _():
        for c in locals_[1:]:
            c.wait()
        for c in swaps:
            c.wait()
        for c in fourth:
            c.wait()


def main(xq, xp, lengths, weights, kvq, kvp, pay, slices, zt):
    attn_in, attn_out, ffn_in, ffn_out, gains, biases, ffn_bias = weights
    tokens = xq.shape[0]
    vm = pl.BlockSpec(memory_space=pltpu.VMEM)
    hb = pl.BlockSpec(memory_space=pl.ANY)
    sds = jax.ShapeDtypeStruct
    q_row = pl.BlockSpec((256, 768), lambda i: (jnp.minimum(i, 3), 0))
    p_row = pl.BlockSpec((256, 768), lambda i: (jnp.maximum(i - 4, 0), 0))
    return pl.pallas_call(
        main_kernel,
        grid=(8,),
        out_shape=[
            sds((tokens, 768), BF16), sds((tokens, 768), BF16),
            sds((4, 4, 128, 768), BF16), sds((4, 4, 64, 768), BF16),
            sds((16, 80, 128), BF16), sds((16, 48, 512), BF16),
        ],
        in_specs=[
            pl.BlockSpec(memory_space=pltpu.SMEM), vm, vm, vm, q_row, p_row,
            pl.BlockSpec((256, 1536), lambda i: (jnp.minimum(i, 3), 0)),
            pl.BlockSpec((512, 1536), lambda i: (jnp.maximum(i - 4, 0) // 2, 0)),
            hb, hb, hb, hb, hb, hb, hb,
        ],
        out_specs=[q_row, p_row, hb, hb, hb, hb],
        scratch_shapes=[
            pltpu.VMEM((256, 768), BF16), pltpu.VMEM((256, 768), BF16), pltpu.VMEM((256, 768), BF16),
            pltpu.VMEM((2, 768, 768), BF16), pltpu.VMEM((2, 768, 768), BF16),
            pltpu.VMEM((2, 768, 3072), BF16), pltpu.VMEM((2, 3072, 768), BF16),
            pltpu.VMEM((512, 512), F32),
            pltpu.SemaphoreType.DMA((2, 4)), pltpu.SemaphoreType.DMA((3,)),
            pltpu.SemaphoreType.DMA((8,)), pltpu.SemaphoreType.DMA((8,)),
            pltpu.SemaphoreType.DMA((2, 16)), pltpu.SemaphoreType.DMA((2, 16)),
        ],
        compiler_params=pltpu.CompilerParams(
            collective_id=1, has_side_effects=True, vmem_limit_bytes=VMEM_LIMIT,
            dimension_semantics=("arbitrary",),
        ),
        name="main",
    )(lengths, gains, biases, ffn_bias.reshape(2, 1, 3072), xq, xp, kvq, kvp,
      attn_in, attn_out, ffn_in, ffn_out, pay, slices, zt.reshape(16, 48, 512))


def norm_back(up, gain, normed, inverse):
    u = up * gain
    return inverse * (
        u - jnp.mean(u, -1, keepdims=True) - normed * jnp.mean(u * normed, -1, keepdims=True)
    )


def gelu_pair(v):
    sq = v * v
    th = jnp.tanh(0.7978845608028654 * (v + 0.044715 * (v * sq)))
    half = 0.5 * (1.0 + th)
    slope = half + 0.5 * v * (1.0 - th * th) * (0.7978845608028654 * (1.0 + 0.134145 * sq))
    return v * half, slope


def decode_inv(ext):
    return ext[:, 0:1] + ext[:, 1:2] + ext[:, 2:3], ext[:, 3:4] + ext[:, 4:5] + ext[:, 5:6]


def ext_rows(block):
    e_p = block[:, :, 0:128].reshape(128, 128)
    e_q = jnp.concatenate([block[:, :, 128 * a:128 * a + 128] for a in range(1, 5)], 1)
    return e_p, e_q.reshape(512, 128)


def back_kernel(
    ga_ref, gs_ref, pay_ref, innq_ref, innp_ref, invq_ref, invp_ref, gains_ref, biases_ref,
    x_q_hbm, x_p_hbm, kvq_hbm, kvp_hbm, pq_hbm, pp_hbm, wout_hbm, fin_hbm, fout_hbm,
    loss_ref, upq_ref, upp_ref, dpq_ref, dpp_ref, gmq_ref, gmp_ref, gfq_ref, gfp_ref,
    gq_ref, yt_ref,
    loss_s, x_s, kv_s, pq_s, pp_s, wout_s, fin_s, fout_s, sem,
):
    me, g = place()
    copies = [
        [
            pltpu.make_async_copy(fout_hbm.at[t], fout_s.at[t], sem.at[t, 0]),
            pltpu.make_async_copy(fin_hbm.at[t], fin_s.at[t], sem.at[t, 1]),
            pltpu.make_async_copy(wout_hbm.at[t], wout_s.at[t], sem.at[t, 2]),
            pltpu.make_async_copy((kvq_hbm, kvp_hbm)[t], kv_s.at[t], sem.at[t, 3]),
            pltpu.make_async_copy((pq_hbm, pp_hbm)[t], (pq_s, pp_s)[t], sem.at[t, 4]),
            pltpu.make_async_copy((x_q_hbm, x_p_hbm)[t], x_s.at[t], sem.at[t, 5]),
        ]
        for t in range(2)
    ]
    for pair in zip(*copies):
        for c in pair:
            c.start()

    qv = jnp.concatenate([ga_ref[:, 32:64].reshape(512, 768), gs_ref[:, 0:32].reshape(512, 768)], 0)
    pv_own = ga_ref[:, 64:80].astype(F32)[:, 8:16].reshape(128, 768)
    pv_sib = gs_ref[:, 32:48].astype(F32)[:, 8:16].reshape(128, 768)
    pv = jnp.concatenate([pv_own, pv_sib], 0).astype(BF16)
    ext_own = ga_ref[:, 80:96].astype(F32)[:, 8:16]
    ext_sib = gs_ref[:, 48:64].astype(F32)[:, 8:16]
    _, eq_own = ext_rows(ext_own)
    _, eq_sib = ext_rows(ext_sib)
    eq = jnp.concatenate([eq_own, eq_sib], 0)
    label = (eq[:, 6:7] * 256.0 + eq[:, 7:8]).astype(jnp.int32)
    col = iota((1, 256), 1)
    within = lax.rem(col, 128)
    side = jnp.where(col < 128, g, 1 - g)
    ids = (within // 8) * 16 + side * 8 + lax.rem(within, 8)
    logits = SCORE_SCALE * dot_nt(qv, pv)
    top = jnp.max(logits, -1, keepdims=True)
    norm_log = top + jnp.log(jnp.sum(jnp.exp(logits - top), -1, keepdims=True))
    hit = label == ids
    positive = jnp.sum(jnp.where(hit, logits, 0.0), -1, keepdims=True)
    grad = (jnp.exp(logits - norm_log) - jnp.where(hit, 1.0, 0.0)).astype(BF16)
    loss_s[...] = jnp.broadcast_to((norm_log - positive)[:512], (512, 128))
    loss_ref[...] = loss_s[pl.ds(pl.multiple_of(me * 32, 32), 32), :]
    upq_ref[...] = SCORE_SCALE * dot(grad[:512], pv)
    upp_ref[...] = SCORE_SCALE * dot_tn(grad[:, 0:128], qv)

    low = pay_ref[64:80, :].astype(F32)
    gq_rows = []
    for t, (count, up, hidden, vec, inn_ref, inv_ref, p_s, dp_ref, gm_ref, gf_ref) in enumerate((
        (32, upq_ref[pl.ds(pl.multiple_of(me * 32, 32), 32), :], pay_ref[0:32, :].astype(F32),
         pay_ref[32:64, :].astype(F32), innq_ref, invq_ref, pq_s, dpq_ref, gmq_ref, gfq_ref),
        (8, upp_ref[pl.ds(pl.multiple_of(me * 8, 8), 8), :], low[0:8], low[8:16],
         innp_ref, invp_ref, pp_s, dpp_ref, gmp_ref, gfp_ref),
    )):
        g0, g1 = gains_ref[t, 0:1, :], gains_ref[t, 1:2, :]
        n2 = (vec - biases_ref[t, 5:6, :]) / g1
        n1 = (hidden - biases_ref[t, 3:4, :]) / g0
        grad_second = norm_back(up, g1, n2, inv_ref[:, 1:2])
        grad_ffn = grad_second.astype(BF16)
        copies[t][0].wait()
        grad_active = dot_nt(grad_ffn, fout_s[t])
        _, slope = gelu_pair(inn_ref[...])
        grad_inner = (grad_active * slope).astype(BF16)
        copies[t][1].wait()
        grad_hidden = grad_second + dot_nt(grad_inner, fin_s[t])
        grad_first = norm_back(grad_hidden, g0, n1, inv_ref[:, 0:1])
        gf_ref[...] = grad_first
        copies[t][2].wait()
        gm = dot_nt(grad_first.astype(BF16), wout_s[t]).astype(BF16)
        gm_ref[...] = gm
        copies[t][3].wait()
        copies[t][4].wait()
        copies[t][5].wait()
        wide = expand_heads(gm.astype(F32)).astype(BF16)
        dp = dot_nt(wide, kv_s[t, :, 768:1536])
        soft = p_s[...]
        ds = (soft * (dp - jnp.sum(soft * dp, -1, keepdims=True))).astype(BF16)
        n = HEADS * count
        dp_ref[0:n, :] = ds
        dp_ref[n:2 * n, :] = soft.astype(BF16)
        gq_rows.append(fold_heads(dot(ds, kv_s[t, :, 0:768]), count) * KEY_SCALE)
        y = dot(ds, x_s[t]) * KEY_SCALE
        if t == 0:
            yt_ref[:, 0:384] = y.T.astype(BF16)
        else:
            yt_ref[:, 384:512] = jnp.concatenate([y, jnp.zeros((32, 768), F32)], 0).T.astype(BF16)
    gq_ref[...] = jnp.concatenate(gq_rows + [jnp.zeros((8, 768), F32)], 0).astype(BF16)


def back(ga, gs, pay, innq, innp, invq, invp, xq, xp, kvq, kvp, pq, pp, weights):
    attn_in, attn_out, ffn_in, ffn_out, gains, biases, ffn_bias = weights
    tokens = xq.shape[0]
    vm = pl.BlockSpec(memory_space=pltpu.VMEM)
    hb = pl.BlockSpec(memory_space=pl.ANY)
    sds = jax.ShapeDtypeStruct
    return pl.pallas_call(
        back_kernel,
        out_shape=[
            sds((32, 128), F32), sds((512, 768), F32), sds((128, 768), F32),
            sds((768, tokens), BF16), sds((192, tokens), BF16),
            sds((32, 768), BF16), sds((8, 768), BF16), sds((32, 768), F32), sds((8, 768), F32),
            sds((48, 768), BF16), sds((768, 512), BF16),
        ],
        in_specs=[vm] * 9 + [hb] * 9,
        out_specs=[vm] * 11,
        scratch_shapes=[
            pltpu.VMEM((512, 128), F32),
            pltpu.VMEM((2, tokens, 768), BF16), pltpu.VMEM((2, tokens, 1536), BF16),
            pltpu.VMEM((384, tokens), F32), pltpu.VMEM((96, tokens), F32),
            pltpu.VMEM((2, 768, 768), BF16), pltpu.VMEM((2, 768, 3072), BF16),
            pltpu.VMEM((2, 3072, 768), BF16),
            pltpu.SemaphoreType.DMA((2, 6)),
        ],
        compiler_params=pltpu.CompilerParams(vmem_limit_bytes=VMEM_LIMIT),
        name="back",
    )(ga.reshape(16, 128, 768), gs.reshape(16, 64, 768), pay, innq, innp, invq, invp, gains, biases,
      xq, xp, kvq, kvp, pq, pp, attn_out, ffn_in, ffn_out)


QR, PR = 512, 128


def last_kernel(
    lens_ref, gains_ref, biases_ref, ffnb_ref, upq_ref, upp_ref, gmq_ref, gmp_ref, gfq_ref, gfp_ref,
    gq_ref, pay_ref,
    yt_hbm, ga_hbm, rsl_hbm, rzt_hbm, dpq_hbm, dpp_hbm, win_hbm, wout_hbm, fin_hbm, fout_hbm,
    dxq_hbm, dxp_hbm, pwin_ref, pwout_ref, pfin_ref, pfout_ref, psum_ref, pffb_ref,
    swin_ref, swout_ref, sfin_ref, sfout_ref, ssum_ref, sffb_ref,
    rgq_s, ryt_s, ga_s, rsl_s, rzt_s, dpq_s, dpp_s, wout_s, fin_s, fout_s,
    act_s, gin_s, gffn_s, gat_s, gm_s, tr_s, dx_s, dxp_s, acc_s,
    sem, lsem, ss, rs, as_, ar, xs, xr,
):
    me, g = place()
    z, yx = me // 4, lax.rem(me, 4)
    first, second, third = gather_phases(me, g, gq_ref, rgq_s, ss, rs)
    swaps = []
    for i in range(1, 16):
        peer = lax.rem(me + i, 16)
        swaps.append(remote(yt_hbm.at[peer], ryt_s.at[me], as_.at[i], ar.at[i], (peer, g)))
    own = [
        pltpu.make_async_copy(gq_ref, rgq_s.at[z, yx], lsem.at[0]),
        pltpu.make_async_copy(yt_hbm.at[me], ryt_s.at[me], lsem.at[1]),
    ]
    sib = (me, 1 - g)
    early = [
        remote(pwout_ref, swout_ref, xs.at[0], xr.at[0], sib),
        remote(pfin_ref, sfin_ref, xs.at[1], xr.at[1], sib),
        remote(pfout_ref, sfout_ref, xs.at[2], xr.at[2], sib),
        remote(pffb_ref, sffb_ref, xs.at[3], xr.at[3], sib),
    ]
    late = [
        remote(pwin_ref, swin_ref, xs.at[4], xr.at[4], sib),
        remote(psum_ref, ssum_ref, xs.at[5], xr.at[5], sib),
    ]
    load_ga = pltpu.make_async_copy(ga_hbm, ga_s, sem.at[0])
    load_fin = [pltpu.make_async_copy(fin_hbm.at[t], fin_s.at[t], sem.at[1 + t]) for t in range(2)]
    load_fout = [pltpu.make_async_copy(fout_hbm.at[t], fout_s.at[t], sem.at[3 + t]) for t in range(2)]
    load_wout = pltpu.make_async_copy(wout_hbm, wout_s, sem.at[5])
    load_rest = [
        pltpu.make_async_copy(rsl_hbm, rsl_s, sem.at[6]),
        pltpu.make_async_copy(rzt_hbm, rzt_s, sem.at[7]),
        pltpu.make_async_copy(dpq_hbm, dpq_s, sem.at[8]),
        pltpu.make_async_copy(dpp_hbm, dpp_s, sem.at[9]),
    ]
    load_win = pltpu.make_async_copy(win_hbm, fin_s.at[:, :, 0:2304], sem.at[10])
    for c in [load_ga, load_fin[0], load_fout[0], load_wout, load_fin[1], load_fout[1]] + load_rest + own:
        c.start()
    barrier_all(me, g)
    for c in first + swaps:
        c.start()

    ext_p, ext_q = None, None
    load_ga.wait()
    load_wout.wait()
    ext = ga_s[:, 80:96].astype(F32)[:, 8:16]
    ext_p, ext_q = ext_rows(ext)
    psum_ref[...] = jnp.zeros(psum_ref.shape, F32)
    pffb_ref[...] = jnp.zeros(pffb_ref.shape, F32)

    def chain(t, up, hidden, vec, inv1, inv2, rows, count):
        g0, g1 = gains_ref[t, 0:1, :], gains_ref[t, 1:2, :]
        n2 = (vec.astype(F32) - biases_ref[t, 5:6, :]) / g1
        n1 = (hidden.astype(F32) - biases_ref[t, 3:4, :]) / g0
        grad_second = norm_back(up, g1, n2, inv2)
        grad_ffn = grad_second.astype(BF16)
        gffn_s[rows, :] = grad_ffn
        grad_hidden = grad_second
        for c in range(4):
            cols = slice(768 * c, 768 * c + 768)
            inner = dot(hidden, fin_s[t, :, cols]) + ffnb_ref[t, :, cols]
            active, slope = gelu_pair(inner)
            act_s[rows, cols] = active.astype(BF16)
            grad_inner = (dot_nt(grad_ffn, fout_s[t, cols, :]) * slope).astype(BF16)
            gin_s[rows, cols] = grad_inner
            pffb_ref[t, 0:1, cols] += jnp.sum(grad_inner.astype(F32), 0, keepdims=True)
            grad_hidden = grad_hidden + dot_nt(grad_inner, fin_s[t, :, cols])
        grad_first = norm_back(grad_hidden, g0, n1, inv1)
        grad_attn = grad_first.astype(BF16)
        gat_s[rows, :] = grad_attn
        gm = dot_nt(grad_attn, wout_s[t]).astype(BF16)
        gm_s[rows, :] = gm
        total = lambda v: jnp.sum(v, 0, keepdims=True)
        psum_ref[t, 0:8, :] += jnp.concatenate([
            total(grad_hidden * n1), total(up * n2), jnp.zeros((1, 768), F32),
            total(gm.astype(F32)), total(grad_attn.astype(F32)), total(grad_hidden),
            total(grad_ffn.astype(F32)), total(up),
        ], 0)

    i1q, i2q = decode_inv(ext_q)
    i1p, i2p = decode_inv(ext_p)
    for blk in range(2):
        if blk == 0:
            load_fin[0].wait()
            load_fout[0].wait()
        lo = blk * 256
        chain(
            0, upq_ref[lo:lo + 256, :],
            ga_s[8 * blk:8 * blk + 8, 0:32].reshape(256, 768),
            ga_s[8 * blk:8 * blk + 8, 32:64].reshape(256, 768),
            i1q[lo:lo + 256], i2q[lo:lo + 256], slice(lo, lo + 256), 256,
        )
        if blk == 0:
            own[0].wait()
            for c in first:
                c.wait()
            for c in second:
                c.start()
    load_fin[1].wait()
    load_fout[1].wait()
    hv = ga_s[:, 64:80].astype(F32)
    chain(
        1, upp_ref[...], hv[:, 0:8].reshape(128, 768).astype(BF16),
        hv[:, 8:16].reshape(128, 768).astype(BF16), i1p, i2p, slice(QR, QR + PR), 128,
    )
    load_win.start()
    for c in second:
        c.wait()
    for c in third:
        c.start()

    for c in load_rest:
        c.wait()
    for t, rows in enumerate((slice(0, QR), slice(QR, QR + PR))):
        count = rows.stop - rows.start
        fo_at = pl.multiple_of((me // 2) * 384, 128)
        tr_s[:, 0:count] = act_s[rows, pl.ds(fo_at, 384)].astype(F32).T.astype(BF16)
        fo_row = pl.multiple_of(lax.rem(me, 2) * 192, 16)
        pfout_ref[t] = dot(tr_s[pl.ds(fo_row, 192), 0:count], gffn_s[rows, :])
        fi_at = pl.multiple_of((me // 8) * 384, 128)
        if t == 0:
            hid = ga_s[:, 0:32, pl.ds(fi_at, 384)].reshape(QR, 384)
        else:
            hid = ga_s[:, 64:80, pl.ds(fi_at, 384)].astype(F32)[:, 0:8].reshape(PR, 384)
        tr_s[:, 0:count] = hid.astype(F32).T.astype(BF16)
        fi_row = pl.multiple_of(lax.rem(me, 8) * 48, 16)
        pfin_ref[t] = dot(tr_s[pl.ds(fi_row, 48), 0:count], gin_s[rows, :])
        if t == 0:
            mx = rsl_s[:, 0:32].reshape(QR, 128)
        else:
            mx = rsl_s[:, 64:80].astype(F32)[:, 0:8].reshape(PR, 128).astype(BF16)
        pwout_ref[t] = dot_tn(mx, gat_s[rows, :])[0:48]
    for c in early:
        c.start()

    lane4 = iota((1, 256), 1) // HEAD_DIM

    def spread4(rows, j):
        part = rows[:, 256 * j:256 * j + 256]
        return jnp.concatenate([jnp.where(lane4 == h, part, 0.0) for h in range(4)], 0).astype(BF16)

    def low_rank(t_ref, read_q, read_p, out_col):
        acc_s[...] = jnp.zeros(acc_s.shape, F32)

        def source(i, _):
            rows_q = read_q(i).astype(F32)
            for j in range(3):
                acc_s[0, :, 256 * j:256 * j + 256] += dot(
                    t_ref[i, :, 128 * j:128 * j + 128], spread4(rows_q, j)
                )
            wide = jnp.concatenate([expand_heads(read_p(i)), jnp.zeros((32, 768), F32)], 0)
            acc_s[1] += dot(t_ref[i, :, 384:512], wide.astype(BF16))
            return 0

        lax.fori_loop(0, 16, source, 0)
        pwin_ref[:, :, out_col:out_col + 768] = acc_s[...]

    def gm_p(i):
        pair = gm_s[pl.ds(pl.multiple_of(QR + (i // 2) * 16, 16), 16), :].astype(F32)
        return jnp.where(lax.rem(i, 2) == 0, pair[0:8], pair[8:16])

    low_rank(rzt_s, lambda i: gm_s[pl.ds(pl.multiple_of(i * 32, 32), 32), :], gm_p, 1536)

    load_win.wait()
    copies = []
    for t, (count, dp_s, gm_ref, gf_ref, dx, dx_hbm) in enumerate((
        (32, dpq_s, gmq_ref, gfq_ref, dx_s, dxq_hbm), (8, dpp_s, gmp_ref, gfp_ref, dxp_s, dxp_hbm),
    )):
        n = HEADS * count
        if t == 0:
            q = pay_ref[96:128, :].astype(F32)
            gq = gq_ref[0:32, :]
        else:
            q = pay_ref[80:96, :].astype(F32)[0:8]
            gq = gq_ref[32:48, :].astype(F32)[0:8].astype(BF16)
        u = (dot_nt(expand_heads(q).astype(BF16), fin_s[t, :, 768:1536]) * KEY_SCALE).astype(BF16)
        w = dot_nt(expand_heads(gm_ref[...].astype(F32)).astype(BF16), fin_s[t, :, 1536:2304]).astype(BF16)
        uw = jnp.concatenate([u, w], 0)
        extra = dot_nt(gq, fin_s[t, :, 0:768]) + gf_ref[...]
        e_hi = extra.astype(BF16)
        e_lo = (extra - e_hi.astype(F32)).astype(BF16)
        for m in range(4):
            colr = iota((count, 256), 1) + 256 * m
            rowr = iota((count, 256), 0)
            if t == 0:
                sel = colr == rowr * 32
            else:
                start = jnp.zeros((count, 256), jnp.int32)
                for r in range(2):
                    at = jnp.int32(r * 512)
                    for c in range(4):
                        start = jnp.where(rowr == r * 4 + c, at, start)
                        at = at + lens_ref[r, c]
                sel = colr == start
            sel16 = jnp.where(sel, 1.0, 0.0).astype(BF16)
            dx[256 * m:256 * m + 256, :] = (
                dot_tn(dp_s[:, 256 * m:256 * m + 256], uw) + dot_tn(sel16, e_hi) + dot_tn(sel16, e_lo)
            )
        c = pltpu.make_async_copy(dx, dx_hbm, lsem.at[2 + t])
        c.start()
        copies.append(c)

    for c in third:
        c.wait()
    for c in swaps:
        c.wait()
    own[1].wait()

    def q_p(i):
        return ga_s[i, 80:96, :].astype(F32)[0:8]

    low_rank(ryt_s, lambda i: ga_s[i, 96:128, :], q_p, 768)
    rg_q = rgq_s[:, :, 0:32].reshape(QR, 768)
    rg_p = rgq_s[:, :, 32:48].astype(F32)[:, :, 0:8].reshape(PR, 768)
    pwin_ref[0, :, 0:768] = dot_tn(rsl_s[:, 32:64].reshape(QR, 128), rg_q)[0:48]
    x_p = rsl_s[:, 64:80].astype(F32)[:, 8:16].reshape(PR, 128).astype(BF16)
    pwin_ref[1, :, 0:768] = dot_tn(x_p, rg_p.astype(BF16))[0:48]
    psum_ref[0, 2:3, :] = jnp.sum(rg_q.astype(F32), 0, keepdims=True)
    psum_ref[1, 2:3, :] = jnp.sum(rg_p, 0, keepdims=True)
    for c in late:
        c.start()
    for c in early + late + copies:
        c.wait()


def last(lengths, weights, upq, upp, gmq, gmp, gfq, gfp, gq, pay, yt, ga, rsl, rzt, dpq, dpp):
    attn_in, attn_out, ffn_in, ffn_out, gains, biases, ffn_bias = weights
    tokens = dpq.shape[1]
    vm = pl.BlockSpec(memory_space=pltpu.VMEM)
    hb = pl.BlockSpec(memory_space=pl.ANY)
    sds = jax.ShapeDtypeStruct
    parts = [
        sds((2, 48, 2304), F32), sds((2, 48, 768), F32), sds((2, 48, 3072), F32),
        sds((2, 192, 768), F32), sds((2, 8, 768), F32), sds((2, 8, 3072), F32),
    ]
    return pl.pallas_call(
        last_kernel,
        out_shape=[sds((tokens, 768), F32), sds((tokens, 768), F32)] + parts + parts,
        in_specs=[pl.BlockSpec(memory_space=pltpu.SMEM)] + [vm] * 11 + [hb] * 10,
        out_specs=[hb, hb] + [vm] * 6 + [vm] * 6,
        scratch_shapes=[
            pltpu.VMEM((4, 4, 48, 768), BF16), pltpu.VMEM((16, 48, 512), BF16),
            pltpu.VMEM((16, 128, 768), BF16), pltpu.VMEM((16, 80, 128), BF16),
            pltpu.VMEM((16, 48, 512), BF16), pltpu.VMEM((768, tokens), BF16),
            pltpu.VMEM((192, tokens), BF16), pltpu.VMEM((2, 768, 768), BF16),
            pltpu.VMEM((2, 768, 3072), BF16), pltpu.VMEM((2, 3072, 768), BF16),
            pltpu.VMEM((640, 3072), BF16), pltpu.VMEM((640, 3072), BF16),
            pltpu.VMEM((640, 768), BF16), pltpu.VMEM((640, 768), BF16), pltpu.VMEM((640, 768), BF16),
            pltpu.VMEM((384, 512), BF16), pltpu.VMEM((tokens, 768), F32), pltpu.VMEM((tokens, 768), F32),
            pltpu.VMEM((2, 48, 768), F32),
            pltpu.SemaphoreType.DMA((11,)), pltpu.SemaphoreType.DMA((4,)),
            pltpu.SemaphoreType.DMA((7,)), pltpu.SemaphoreType.DMA((7,)),
            pltpu.SemaphoreType.DMA((16,)), pltpu.SemaphoreType.DMA((16,)),
            pltpu.SemaphoreType.DMA((6,)), pltpu.SemaphoreType.DMA((6,)),
        ],
        compiler_params=pltpu.CompilerParams(
            collective_id=2, has_side_effects=True, vmem_limit_bytes=62 * 1024 * 1024
        ),
        name="last",
    )(lengths, gains, biases, ffn_bias.reshape(2, 1, 3072), upq, upp, gmq, gmp, gfq, gfp, gq, pay,
      yt.reshape(16, 48, 512), ga.reshape(16, 128, 768), rsl, rzt, dpq, dpp,
      attn_in, attn_out, ffn_in, ffn_out)


def fast_shards(query_tokens, passage_tokens, lengths, labels, *weights):
    xq = query_tokens.reshape(-1, 768)
    xp = passage_tokens.reshape(-1, 768)
    kvq, kvp, pq, pp, pay, slices, zt, innq, innp, invq, invp = front(xq, xp, lengths, labels, weights)
    outq, outp, ga, gs, rsl, rzt = main(xq, xp, lengths, weights, kvq, kvp, pay, slices, zt)
    loss, upq, upp, dpq, dpp, gmq, gmp, gfq, gfp, gq, yt = back(
        ga, gs, pay, innq, innp, invq, invp, xq, xp, kvq, kvp, pq, pp, weights
    )
    dxq, dxp, *parts = last(
        lengths, weights, upq, upp, gmq, gmp, gfq, gfp, gq, pay, yt, ga, rsl, rzt, dpq, dpp
    )
    win, wout, fin, fout, sums, ffb = [a + b for a, b in zip(parts[:6], parts[6:])]
    me = lax.axis_index("blk")
    mine = lax.dynamic_slice_in_dim(sums, me * 48, 48, 2)
    ffb_mine = lax.dynamic_slice_in_dim(ffb[:, 0], me * 192, 192, 1)
    return (
        loss[:, 0],
        outq.reshape(query_tokens.shape),
        outp.reshape(passage_tokens.shape),
        dxq.reshape(query_tokens.shape),
        dxp.reshape(passage_tokens.shape),
        win, wout, fin, fout, mine[:, 0:2], mine[:, 2:8], ffb_mine,
    )


def layer_norm(residual, gain_vec, shift_vec):
    centre = residual - jnp.mean(residual, -1, keepdims=True)
    inverse = lax.rsqrt(jnp.mean(centre * centre, -1, keepdims=True) + EPSILON)
    return centre * inverse * gain_vec + shift_vec


def plain_norm_back(residual, gain_vec, upstream):
    centre = residual - jnp.mean(residual, -1, keepdims=True)
    inverse = lax.rsqrt(jnp.mean(centre * centre, -1, keepdims=True) + EPSILON)
    normed = centre * inverse
    scaled = upstream * gain_vec
    grad_res = inverse * (
        scaled
        - jnp.mean(scaled, -1, keepdims=True)
        - normed * jnp.mean(scaled * normed, -1, keepdims=True)
    )
    return (grad_res, jnp.sum(upstream * normed, 0), jnp.sum(upstream, 0))


def cls_index(starts, seq_len):
    return (jnp.arange(starts.shape[0], dtype=jnp.int32)[:, None] * seq_len + starts).reshape(-1)


def forward(tokens, segment, starts, params):
    attn_in, attn_out, ffn_in, ffn_out, gains, biases, ffn_bias = params
    batch_size, seq_len, feature = tokens.shape
    head_count = feature // HEAD_DIM
    flat_tokens = tokens.reshape(batch_size * seq_len, feature)
    zeros_vec = jnp.zeros_like(biases[0])
    joined = jnp.dot(flat_tokens, attn_in, preferred_element_type=jnp.float32) + jnp.concatenate(
        [biases[0], zeros_vec, biases[1]]
    )
    joined = joined.astype(jnp.bfloat16)
    shaped = joined.reshape(batch_size, seq_len, 3, head_count, HEAD_DIM)
    scores = (
        jnp.einsum(
            "bqhd,bkhd->bhqk", shaped[:, :, 0], shaped[:, :, 1], preferred_element_type=jnp.float32
        )
        * KEY_SCALE
    )
    same_seg = segment[:, :, None] == segment[:, None, :]
    scores = jnp.where(same_seg[:, None], scores, -1000000000.0)
    attention = jax.nn.softmax(scores, -1).astype(jnp.bfloat16)
    mixed = jnp.einsum(
        "bhqk,bkhd->bqhd", attention, shaped[:, :, 2], preferred_element_type=jnp.float32
    )
    mixed = mixed.reshape(batch_size * seq_len, feature).astype(jnp.bfloat16)
    first_sum = flat_tokens.astype(jnp.float32) + (
        jnp.dot(mixed, attn_out, preferred_element_type=jnp.float32) + biases[2]
    )
    hidden = layer_norm(first_sum, gains[0], biases[3]).astype(jnp.bfloat16)
    inner = jnp.dot(hidden, ffn_in, preferred_element_type=jnp.float32) + ffn_bias
    active = jax.nn.gelu(inner).astype(jnp.bfloat16)
    second_sum = hidden.astype(jnp.float32) + (
        jnp.dot(active, ffn_out, preferred_element_type=jnp.float32) + biases[4]
    )
    output = layer_norm(second_sum, gains[1], biases[5]).astype(jnp.bfloat16)
    picked = cls_index(starts, seq_len)
    kept = (
        flat_tokens,
        joined,
        mixed[picked],
        first_sum[picked],
        hidden[picked],
        inner[picked],
        active[picked],
        second_sum[picked],
    )
    return (output, picked, kept)


def backward(kept, segment, starts, params, upstream):
    attn_in, attn_out, ffn_in, ffn_out, gains, biases, ffn_bias = params
    flat_tokens, joined, mixed_cls, first_cls, hidden_cls, inner_cls, active_cls, second_cls = kept
    batch_size, seq_len = segment.shape
    per_row = starts.shape[1]
    feature = flat_tokens.shape[1]
    head_count = feature // HEAD_DIM
    grad_second, gain_two, shift_two = plain_norm_back(second_cls, gains[1], upstream)
    grad_ffn = grad_second.astype(jnp.bfloat16)
    grad_down = jnp.dot(active_cls.T, grad_ffn, preferred_element_type=jnp.float32)
    grad_active = jnp.dot(grad_ffn, ffn_out.T, preferred_element_type=jnp.float32)
    grad_inner = jax.vjp(jax.nn.gelu, inner_cls)[1](grad_active)[0].astype(jnp.bfloat16)
    grad_up = jnp.dot(hidden_cls.T, grad_inner, preferred_element_type=jnp.float32)
    grad_hidden = grad_second + jnp.dot(grad_inner, ffn_in.T, preferred_element_type=jnp.float32)
    grad_first, gain_one, shift_one = plain_norm_back(first_cls, gains[0], grad_hidden)
    grad_attn = grad_first.astype(jnp.bfloat16)
    grad_outproj = jnp.dot(mixed_cls.T, grad_attn, preferred_element_type=jnp.float32)
    grad_mixed = jnp.dot(grad_attn, attn_out.T, preferred_element_type=jnp.float32).astype(
        jnp.bfloat16
    )
    grad_mixed = grad_mixed.reshape(batch_size, per_row, head_count, HEAD_DIM)
    shaped = joined.reshape(batch_size, seq_len, 3, head_count, HEAD_DIM)
    key_part = shaped[:, :, 1]
    value_part = shaped[:, :, 2]
    picked = cls_index(starts, seq_len)
    query_cls = joined[picked, :feature].reshape(batch_size, per_row, head_count, HEAD_DIM)
    own_seg = jnp.take_along_axis(segment, starts, 1)
    scores = (
        jnp.einsum("bchd,bkhd->bhck", query_cls, key_part, preferred_element_type=jnp.float32)
        * KEY_SCALE
    )
    scores = jnp.where((own_seg[:, :, None] == segment[:, None, :])[:, None], scores, -1000000000.0)
    attention = jax.nn.softmax(scores, -1)
    grad_attention = jnp.einsum(
        "bchd,bkhd->bhck", grad_mixed, value_part, preferred_element_type=jnp.float32
    )
    grad_scores = attention * (
        grad_attention - jnp.sum(attention * grad_attention, -1, keepdims=True)
    )
    grad_scores = grad_scores.astype(jnp.bfloat16)
    grad_query = (
        jnp.einsum("bhck,bkhd->bchd", grad_scores, key_part, preferred_element_type=jnp.float32)
        * KEY_SCALE
    ).astype(jnp.bfloat16)
    grad_key = (
        jnp.einsum("bhck,bchd->bkhd", grad_scores, query_cls, preferred_element_type=jnp.float32)
        * KEY_SCALE
    ).astype(jnp.bfloat16)
    grad_value = jnp.einsum(
        "bhck,bchd->bkhd",
        attention.astype(jnp.bfloat16),
        grad_mixed,
        preferred_element_type=jnp.float32,
    ).astype(jnp.bfloat16)
    places = jnp.arange(seq_len, dtype=jnp.int32)
    selector = (starts[:, :, None] == places[None, None, :]).astype(jnp.bfloat16)
    grad_query_full = jnp.einsum(
        "bcl,bchd->blhd", selector, grad_query, preferred_element_type=jnp.float32
    ).astype(jnp.bfloat16)
    grad_joined = jnp.stack([grad_query_full, grad_key, grad_value], 2).reshape(
        batch_size * seq_len, 3 * feature
    )
    grad_inproj = jnp.dot(flat_tokens.T, grad_joined, preferred_element_type=jnp.float32)
    grad_tokens = (
        jnp.dot(grad_joined, attn_in.T, preferred_element_type=jnp.float32)
        .at[picked]
        .add(grad_first)
    )
    bias_grads = jnp.stack(
        [
            jnp.sum(grad_query.astype(jnp.float32), (0, 1)).reshape(feature),
            jnp.sum(grad_value.astype(jnp.float32), (0, 1)).reshape(feature),
            jnp.sum(grad_attn.astype(jnp.float32), 0),
            shift_one,
            jnp.sum(grad_ffn.astype(jnp.float32), 0),
            shift_two,
        ]
    )
    gain_grads = jnp.stack([gain_one, gain_two])
    hidden_bias = jnp.sum(grad_inner.astype(jnp.float32), 0)
    grads = (grad_inproj, grad_outproj, grad_up, grad_down, gain_grads, bias_grads, hidden_bias)
    row_data = (hidden_cls, grad_inner, active_cls, grad_ffn)
    return (grads, grad_tokens.reshape(batch_size, seq_len, feature), row_data)


def shards(
    query_tokens,
    passage_tokens,
    lengths,
    labels,
    attn_in,
    attn_out,
    ffn_in,
    ffn_out,
    gains,
    biases,
    ffn_bias,
):
    layers = (attn_in, attn_out, ffn_in, ffn_out, gains, biases, ffn_bias)
    query_params = tuple((matrix[0] for matrix in layers))
    passage_params = tuple((matrix[1] for matrix in layers))
    query_count, query_len, feature = query_tokens.shape
    passage_len = passage_tokens.shape[1]
    query_segment = jnp.zeros((query_count, query_len), jnp.int32)
    query_starts = jnp.zeros((query_count, 1), jnp.int32)
    ends = jnp.cumsum(lengths, -1)
    passage_starts = ends - lengths
    places = jnp.arange(passage_len, dtype=jnp.int32)
    passage_segment = jnp.sum((places[None, :, None] >= ends[:, None, :]).astype(jnp.int32), -1)
    query_out, query_pick, query_kept = forward(
        query_tokens, query_segment, query_starts, query_params
    )
    passage_out, passage_pick, passage_kept = forward(
        passage_tokens, passage_segment, passage_starts, passage_params
    )
    query_vec = query_out[query_pick]
    passage_vec = passage_out[passage_pick]
    passage_count = passage_vec.shape[0]
    float_labels = labels.astype(jnp.float32)
    group_vec = lax.all_gather(passage_vec, "grp", axis=0, tiled=True)
    portion = lax.all_gather(group_vec, "blk", axis=0, tiled=True)
    running_max = jnp.full((query_count,), -1e30, jnp.float32)
    score_block = SCORE_SCALE * jnp.dot(query_vec, portion.T, preferred_element_type=jnp.float32)
    column_ids = jnp.arange(portion.shape[0], dtype=jnp.int32)
    new_max = jnp.maximum(running_max, jnp.max(score_block, -1))
    running_sum = jnp.sum(jnp.exp(score_block - new_max[:, None]), -1)
    hits = column_ids[None, :] == labels[:, None]
    positive = jnp.sum(jnp.where(hits, score_block, 0.0), -1)
    running_max, running_sum, positive = (new_max, running_sum, positive)
    norm_log = running_max + jnp.log(running_sum)
    portion = lax.all_gather(group_vec, "blk", axis=0, tiled=True)
    score_block = SCORE_SCALE * jnp.dot(query_vec, portion.T, preferred_element_type=jnp.float32)
    column_ids = jnp.arange(portion.shape[0], dtype=jnp.int32)
    hits = (column_ids[None, :] == labels[:, None]).astype(jnp.float32)
    grad_block = (jnp.exp(score_block - norm_log[:, None]) - hits).astype(jnp.bfloat16)
    query_up = SCORE_SCALE * jnp.dot(grad_block, portion, preferred_element_type=jnp.float32)
    own_ids = (
        lax.axis_index(("blk", "grp")) * passage_count + jnp.arange(passage_count, dtype=jnp.int32)
    ).astype(jnp.float32)
    remote_vec = lax.all_gather(query_vec.astype(jnp.float32), ("blk", "grp"), axis=0, tiled=True)
    remote_log = lax.all_gather(norm_log, ("blk", "grp"), axis=0, tiled=True)
    remote_label = lax.all_gather(float_labels, ("blk", "grp"), axis=0, tiled=True)
    remote_low = remote_vec.astype(jnp.bfloat16)
    score_block = SCORE_SCALE * jnp.dot(
        remote_low, passage_vec.T, preferred_element_type=jnp.float32
    )
    hits = (remote_label[:, None] == own_ids[None, :]).astype(jnp.float32)
    grad_block = (jnp.exp(score_block - remote_log[:, None]) - hits).astype(jnp.bfloat16)
    passage_up = SCORE_SCALE * jnp.dot(grad_block.T, remote_low, preferred_element_type=jnp.float32)
    query_losses = norm_log - positive
    query_grads, query_back, query_rows = backward(
        query_kept, query_segment, query_starts, query_params, query_up
    )
    passage_grads, passage_back, passage_rows = backward(
        passage_kept, passage_segment, passage_starts, passage_params, passage_up
    )
    stacked = tuple(
        (
            jnp.stack([first_part, second_part])
            for first_part, second_part in zip(query_grads, passage_grads)
        )
    )
    grad_win, grad_wout, grad_up, grad_down, grad_gain, grad_bias, grad_hidden_bias = stacked
    shares = (
        lax.psum_scatter(
            grad_win.astype(jnp.bfloat16), "blk", scatter_dimension=1, tiled=True
        ).astype(jnp.float32),
        lax.psum_scatter(
            grad_wout.astype(jnp.bfloat16), "blk", scatter_dimension=1, tiled=True
        ).astype(jnp.float32),
        lax.psum_scatter(
            grad_up.astype(jnp.bfloat16), "blk", scatter_dimension=1, tiled=True
        ).astype(jnp.float32),
        lax.psum_scatter(
            grad_down.astype(jnp.bfloat16), "blk", scatter_dimension=1, tiled=True
        ).astype(jnp.float32),
        lax.psum_scatter(
            grad_gain.astype(jnp.bfloat16), "blk", scatter_dimension=2, tiled=True
        ).astype(jnp.float32),
        lax.psum_scatter(
            grad_bias.astype(jnp.bfloat16), "blk", scatter_dimension=2, tiled=True
        ).astype(jnp.float32),
        lax.psum_scatter(
            grad_hidden_bias.astype(jnp.bfloat16), "blk", scatter_dimension=1, tiled=True
        ).astype(jnp.float32),
    )
    grad_win, grad_wout, grad_up, grad_down, grad_gain, grad_bias, grad_hidden_bias = (
        lax.psum(shares[0].astype(jnp.bfloat16), "grp").astype(jnp.float32),
        lax.psum(shares[1].astype(jnp.bfloat16), "grp").astype(jnp.float32),
        lax.psum(shares[2].astype(jnp.bfloat16), "grp").astype(jnp.float32),
        lax.psum(shares[3].astype(jnp.bfloat16), "grp").astype(jnp.float32),
        lax.psum(shares[4].astype(jnp.bfloat16), "grp").astype(jnp.float32),
        lax.psum(shares[5].astype(jnp.bfloat16), "grp").astype(jnp.float32),
        lax.psum(shares[6].astype(jnp.bfloat16), "grp").astype(jnp.float32),
    )
    query_shaped = query_out.reshape(query_count, query_len, feature)
    passage_shaped = passage_out.reshape(passage_tokens.shape)
    return (
        query_losses,
        query_shaped,
        passage_shaped,
        query_back,
        passage_back,
        grad_win,
        grad_wout,
        grad_up,
        grad_down,
        grad_gain,
        grad_bias,
        grad_hidden_bias,
    )


def solution(mesh):
    placed = (
        P(("blk", "grp"), None, None),
        P(("blk", "grp"), None, None),
        P(("blk", "grp"), None),
        P(("blk", "grp")),
        P(),
        P(),
        P(),
        P(),
        P(),
        P(),
        P(),
    )
    small = dict(mesh.shape) == {"blk": 16, "grp": 2}
    return jax.shard_map(
        fast_shards if small else shards,
        mesh=mesh,
        in_specs=placed,
        out_specs=(
            P(("blk", "grp")),
            P(("blk", "grp"), None, None),
            P(("blk", "grp"), None, None),
            P(("blk", "grp"), None, None),
            P(("blk", "grp"), None, None),
            P(None, "blk", None),
            P(None, "blk", None),
            P(None, "blk", None),
            P(None, "blk", None),
            P(None, None, "blk"),
            P(None, None, "blk"),
            P(None, "blk"),
        ),
        check_vma=False,
    )
```

```python
import functools
import jax
import jax.numpy as jnp
from jax import lax
from jax.experimental import pallas as pl
from jax.experimental.pallas import tpu as pltpu
from jax.sharding import PartitionSpec as P

MESH = pl.DeviceIdType.MESH
HEAD_DIM = 64
HEADS = 12
EPSILON = 1e-05
SCORE_SCALE = 0.08
KEY_SCALE = 0.125
NEG = -1000000000.0
F32 = jnp.float32
BF16 = jnp.bfloat16
VMEM_LIMIT = 60 * 1024 * 1024


def dot(a, b):
    return lax.dot_general(a, b, (((1,), (0,)), ((), ())), preferred_element_type=F32)


def dot_nt(a, b):
    return lax.dot_general(a, b, (((1,), (1,)), ((), ())), preferred_element_type=F32)


def dot_tn(a, b):
    return lax.dot_general(a, b, (((0,), (0,)), ((), ())), preferred_element_type=F32)


def iota(shape, dim):
    return lax.broadcasted_iota(jnp.int32, shape, dim)


def head_row(h):
    return iota((1, 768), 1) // HEAD_DIM == h


def expand_heads(rows):
    return jnp.concatenate(
        [jnp.where(head_row(h), rows, 0.0) for h in range(HEADS)], 0
    )


def fold_heads(rows, count):
    out = jnp.where(head_row(0), rows[:count], 0.0)
    for h in range(1, HEADS):
        out = out + jnp.where(head_row(h), rows[h * count:(h + 1) * count], 0.0)
    return out


def norm_stats(residual):
    centre = residual - jnp.mean(residual, -1, keepdims=True)
    inverse = lax.rsqrt(jnp.mean(centre * centre, -1, keepdims=True) + EPSILON)
    return centre * inverse, inverse


def gelu(v):
    return 0.5 * v * (1.0 + jnp.tanh(0.7978845608028654 * (v + 0.044715 * (v * v * v))))


def split3(v):
    hi = v.astype(BF16).astype(F32)
    rest = v - hi
    mid = rest.astype(BF16).astype(F32)
    return hi, mid, rest - mid


def lane_pack(columns, count):
    lane = iota((count, 128), 1)
    out = jnp.zeros((count, 128), F32)
    for j, column in enumerate(columns):
        out = jnp.where(lane == j, column, out)
    return out


def norm_back(up, gain, normed, inverse):
    u = up * gain
    return inverse * (
        u - jnp.mean(u, -1, keepdims=True) - normed * jnp.mean(u * normed, -1, keepdims=True)
    )


def gelu_pair(v):
    sq = v * v
    th = jnp.tanh(0.7978845608028654 * (v + 0.044715 * (v * sq)))
    half = 0.5 * (1.0 + th)
    slope = half + 0.5 * v * (1.0 - th * th) * (0.7978845608028654 * (1.0 + 0.134145 * sq))
    return v * half, slope


def decode_inv(ext):
    return ext[:, 0:1] + ext[:, 1:2] + ext[:, 2:3], ext[:, 3:4] + ext[:, 4:5] + ext[:, 5:6]


def ext_rows(block):
    e_p = block[:, :, 0:128].reshape(128, 128)
    e_q = jnp.concatenate([block[:, :, 128 * a:128 * a + 128] for a in range(1, 5)], 1)
    return e_p, e_q.reshape(512, 128)


def place():
    return lax.axis_index("blk"), lax.axis_index("grp")


def remote(src, dst, send, recv, peer):
    return pltpu.make_async_remote_copy(
        src_ref=src, dst_ref=dst, send_sem=send, recv_sem=recv, device_id=peer, device_id_type=MESH
    )


def greet(me, g):
    barrier = pltpu.get_barrier_semaphore()
    for i in range(1, 16):
        pl.semaphore_signal(barrier, inc=1, device_id=(lax.rem(me + i, 16), g), device_id_type=MESH)
    pl.semaphore_signal(barrier, inc=1, device_id=(me, 1 - g), device_id_type=MESH)


def greeted():
    pl.semaphore_wait(pltpu.get_barrier_semaphore(), 16)


def gather_phases(me, g, pay, ga, ss, rs, base, lo, hi):
    z, yx = me // 4, lax.rem(me, 4)
    xpeer = me + 1 - 2 * lax.rem(me, 2)
    ypeer = me + 2 - 4 * (lax.rem(me, 4) // 2)
    yx_x, yx_y = lax.rem(xpeer, 4), lax.rem(ypeer, 4)
    rows = slice(lo, hi)
    first, second, third = [], [], []

    def add(phase, src, dst, k, peer):
        phase.append(remote(src, dst, ss.at[base + k], rs.at[base + k], (peer, g)))

    for d in range(1, 4):
        peer = lax.rem(z + d, 4) * 4 + yx
        add(first, pay.at[rows], ga.at[z, yx, rows], d - 1, peer)
    add(second, ga.at[:, yx, rows], ga.at[:, yx, rows], 3, xpeer)
    add(second, ga.at[:, yx, rows], ga.at[:, yx, rows], 4, ypeer)
    add(third, ga.at[0:2, yx_x, rows], ga.at[0:2, yx_x, rows], 5, ypeer)
    add(third, ga.at[2:4, yx_y, rows], ga.at[2:4, yx_y, rows], 6, xpeer)
    return first, second, third


def forward_kernel(
    lens_ref, labels_ref, gains_ref, biases_ref, ffnb_ref,
    xq_hbm, xp_hbm, win_hbm, wout_hbm, fin_hbm, fout_hbm,
    out_hbm, ga_hbm, rsw_ref, part_hbm, uw_hbm, dspq_hbm, dspp_hbm,
    loss_ref, upq_ref, upp_ref, gq_ref, yt_ref, ext_ref,
    x_s, q_s, kv_s, win_s, wout_s, fin_s, fout_s, pq_s, pp_s, out_s, mix_s, bias_s,
    pay_s, swap_s, ga_ref, gs_ref, innq_ref, innp_ref, invq_ref, invp_ref, qq_ref, zq_ref, loss_s,
    sem, lsem, osem, ss, rs, as_, ar,
):
    me, g = place()
    z, yx = me // 4, lax.rem(me, 4)
    greet(me, g)
    copies = []
    for t, x_hbm in enumerate((xq_hbm, xp_hbm)):
        copies.append([
            pltpu.make_async_copy(x_hbm, x_s.at[t], sem.at[t, 0]),
            pltpu.make_async_copy(win_hbm.at[t], win_s.at[t], sem.at[t, 1]),
            pltpu.make_async_copy(wout_hbm.at[t], wout_s.at[t], sem.at[t, 2]),
            pltpu.make_async_copy(fin_hbm.at[t], fin_s.at[t], sem.at[t, 3]),
            pltpu.make_async_copy(fout_hbm.at[t], fout_s.at[t], sem.at[t, 4]),
        ])
    for c in copies[0][:2] + copies[1][:2] + copies[0][2:] + copies[1][2:]:
        c.start()
    a1, b1, c1 = gather_phases(me, g, pay_s, ga_ref, ss, rs, 0, 0, 64)
    a2, b2, c2 = gather_phases(me, g, pay_s, ga_ref, ss, rs, 7, 64, 96)
    last_hop = [remote(ga_ref.at[:, :, 0:64], gs_ref, ss.at[14], rs.at[14], (me, 1 - g))]
    swaps = []
    for i in range(1, 16):
        peer = lax.rem(me + i, 16)
        swaps.append(remote(swap_s.at[peer], rsw_ref.at[me], as_.at[i], ar.at[i], (peer, g)))
    own_copy = [
        pltpu.make_async_copy(pay_s, ga_ref.at[z, yx], lsem.at[0]),
        pltpu.make_async_copy(swap_s.at[me], rsw_ref.at[me], lsem.at[1]),
    ]

    tokens = x_s.shape[1]
    col_q = iota((32, tokens), 1)
    row_q = iota((32, tokens), 0)
    sel_q = col_q == row_q * 32
    own_q = col_q // 32 == row_q
    col_p = iota((8, tokens), 1)
    row_p = iota((8, tokens), 0)
    lo = jnp.zeros((8, tokens), jnp.int32)
    hi = jnp.zeros((8, tokens), jnp.int32)
    for r in range(2):
        acc = jnp.int32(r * 512)
        for c in range(4):
            length = lens_ref[r, c]
            lo = jnp.where(row_p == r * 4 + c, acc, lo)
            acc = acc + length
            hi = jnp.where(row_p == r * 4 + c, acc, hi)
    sel_p = col_p == lo
    own_p = (col_p >= lo) & (col_p < hi)

    picks = []
    for t, sel in enumerate((sel_q, sel_p)):
        copies[t][0].wait()
        copies[t][1].wait()
        query_bias = biases_ref[0, t:t + 1, :]
        value_bias = biases_ref[1, t:t + 1, :]

        def kv_step(m, _, t=t, query_bias=query_bias, value_bias=value_bias):
            rows = pl.ds(pl.multiple_of(m * 256, 256), 256)
            x = x_s[t, rows, :]
            kv_s[t, rows, 0:768] = dot(x, win_s[t, :, 768:1536]).astype(BF16)
            kv_s[t, rows, 768:1536] = (dot(x, win_s[t, :, 1536:2304]) + value_bias).astype(BF16)
            q_s[t, rows, :] = (dot(x, win_s[t, :, 0:768]) + query_bias).astype(BF16)
            return 0

        lax.fori_loop(0, tokens // 256, kv_step, 0)
        pick = jnp.where(sel, 1.0, 0.0).astype(BF16)
        picks.append((dot(pick, x_s[t]), dot(pick, q_s[t])))

    done = []
    for t, (own, count, p_s, inn_ref, inv_ref) in enumerate((
        (own_q, 32, pq_s, innq_ref, invq_ref), (own_p, 8, pp_s, innp_ref, invp_ref),
    )):
        xc, qc = picks[t]
        scores = dot_nt(expand_heads(qc).astype(BF16), kv_s[t, :, 0:768]) * KEY_SCALE
        own12 = jnp.concatenate([jnp.where(own, 0.0, NEG)] * HEADS, 0)
        scores = scores + own12
        weight = jnp.exp(scores - jnp.max(scores, -1, keepdims=True))
        soft = weight * (1.0 / jnp.sum(weight, -1, keepdims=True))
        p_s[...] = soft
        soft16 = soft.astype(BF16)
        mixed = fold_heads(dot(soft16, kv_s[t, :, 768:1536]), count).astype(BF16)
        zsum = dot(soft16, x_s[t])
        copies[t][2].wait()
        first = xc + (dot(mixed, wout_s[t]) + biases_ref[2, t:t + 1, :])
        n1, inv1 = norm_stats(first)
        hidden = (n1 * gains_ref[t, 0:1, :] + biases_ref[3, t:t + 1, :]).astype(BF16)
        copies[t][3].wait()
        inner = dot(hidden, fin_s[t]) + ffnb_ref[t:t + 1, :]
        inn_ref[...] = inner
        active = gelu(inner).astype(BF16)
        copies[t][4].wait()
        second = hidden.astype(F32) + (dot(active, fout_s[t]) + biases_ref[4, t:t + 1, :])
        n2, inv2 = norm_stats(second)
        vec = (n2 * gains_ref[t, 1:2, :] + biases_ref[5, t:t + 1, :]).astype(BF16)
        inv_ref[...] = lane_pack([inv1, inv2], count)
        if t == 0:
            zq_ref[...] = zsum.astype(BF16)
        else:
            wide = jnp.concatenate([zsum, jnp.zeros((32, 768), F32)], 0)
            swap_s[:, 48:96, :] = wide.T.astype(BF16).reshape(16, 48, 128)
        done.append((xc, qc, mixed, hidden, vec, inv1, inv2))

    xq, qq, mq, hq, vq, i1q, i2q = done[0]
    xp, qp, mp, hp, vp, i1p, i2p = done[1]
    lab = labels_ref[...].astype(F32)
    eye = iota((32, 32), 0) == iota((32, 32), 1)
    lab_col = jnp.sum(jnp.where(eye, lab, 0.0), 1, keepdims=True)
    lab_hi = jnp.floor(lab_col * (1.0 / 256.0))
    lab_lo = lab_col - 256.0 * lab_hi
    ext_q = lane_pack([*split3(i1q), *split3(i2q), lab_hi, lab_lo], 32)
    ext_p = lane_pack([*split3(i1p), *split3(i2p)], 8)
    ext = jnp.concatenate(
        [ext_p] + [ext_q[8 * a:8 * a + 8] for a in range(4)] + [jnp.zeros((8, 128), F32)], 1
    )
    pay_s[0:32, :] = vq
    pay_s[32:64, :] = jnp.concatenate([hp.astype(F32), vp.astype(F32), qp, ext], 0).astype(BF16)
    pay_s[64:96, :] = hq
    qq_ref[...] = qq.astype(BF16)
    greeted()
    own_copy[0].start()
    for c in a1 + a2:
        c.start()
    m48 = jnp.concatenate([mq.astype(F32), mp.astype(F32), jnp.zeros((8, 768), F32)], 0)
    x48 = jnp.concatenate([xq, xp, jnp.zeros((8, 768), F32)], 0)
    swap_s[:, 0:48, :] = jnp.zeros((16, 48, 128), BF16)
    for b in range(16):
        swap_s[b, 0:48, 0:48] = m48[:, 48 * b:48 * b + 48].astype(BF16)
        swap_s[b, 0:48, 64:112] = x48[:, 48 * b:48 * b + 48].astype(BF16)
    for c in own_copy[1:]:
        c.start()

    low_half = iota((1, 128), 1) < HEAD_DIM

    def tile(step, _):
        tower = step // 4
        rows = pl.ds(pl.multiple_of(lax.rem(step, 4) * 256, 256), 256)

        def on(k, waits, starts):
            @pl.when(step == k)
            def _():
                for c in waits:
                    c.wait()
                for c in starts:
                    c.start()

        on(1, own_copy[0:1] + a1, b1)
        on(2, a2, b2 + swaps)
        on(3, b1, c1)
        on(4, b2, c2)
        on(5, c1, last_hop)

        @pl.when(step < 4)
        def _():
            same = iota((128, 128), 0) // 32 == iota((128, 128), 1) // 32
            mask = jnp.where(same, 0.0, NEG)
            mask2 = jnp.concatenate([mask, mask], 0)
            for part in range(2):
                at = pl.ds(pl.multiple_of(lax.rem(step, 4) * 256 + part * 128, 128), 128)
                for j in range(HEADS // 2):
                    lanes = slice(128 * j, 128 * j + 128)
                    q = q_s[0, at, lanes]
                    k = kv_s[0, at, lanes]
                    v = kv_s[0, at, 768 + 128 * j:768 + 128 * j + 128]
                    zero = jnp.zeros_like(q)
                    q2 = jnp.concatenate([jnp.where(low_half, q, zero), jnp.where(low_half, zero, q)], 0)
                    s = dot_nt(q2, k) * KEY_SCALE + mask2
                    e = jnp.exp(s - jnp.max(s, -1, keepdims=True))
                    total = jnp.sum(e, -1, keepdims=True)
                    o = dot(e.astype(BF16), v) * (1.0 / total)
                    mix_s[part * 128:part * 128 + 128, lanes] = jnp.where(low_half, o[:128], o[128:]).astype(BF16)

        @pl.when(step >= 4)
        def _():
            row = (step - 4) // 2
            base = lax.rem(step, 2) * 256
            keys = pl.ds(pl.multiple_of(row * 512, 512), 512)
            qpos = iota((256, 512), 0) + base
            kpos = iota((256, 512), 1)
            qseg = jnp.zeros((256, 512), jnp.int32)
            kseg = jnp.zeros((256, 512), jnp.int32)
            end = jnp.int32(0)
            for c in range(3):
                end = end + lens_ref[row, c]
                qseg = qseg + jnp.where(qpos >= end, 1, 0)
                kseg = kseg + jnp.where(kpos >= end, 1, 0)
            mask = jnp.where(qseg == kseg, 0.0, NEG)
            bias_s[...] = mask
            for j in range(HEADS // 2):
                lanes = slice(128 * j, 128 * j + 128)
                q = q_s[1, rows, lanes]
                k = kv_s[1, keys, lanes]
                v = kv_s[1, keys, 768 + 128 * j:768 + 128 * j + 128]
                zero = jnp.zeros_like(q)
                q2 = jnp.concatenate([jnp.where(low_half, q, zero), jnp.where(low_half, zero, q)], 0)
                s = dot_nt(q2, k) * KEY_SCALE
                s = jnp.concatenate([s[:256] + bias_s[...], s[256:] + bias_s[...]], 0)
                e = jnp.exp(s - jnp.max(s, -1, keepdims=True))
                total = jnp.sum(e, -1, keepdims=True)
                o = dot(e.astype(BF16), v) * (1.0 / total)
                mix_s[:, lanes] = jnp.where(low_half, o[:256], o[256:]).astype(BF16)

        first_sum = x_s[tower, rows, :].astype(F32) + (
            dot(mix_s[...], wout_s[tower]) + biases_ref[2, pl.ds(tower, 1), :]
        )
        n1, _ = norm_stats(first_sum)
        hidden = (n1 * gains_ref[tower, 0:1, :] + biases_ref[3, pl.ds(tower, 1), :]).astype(BF16)
        second_sum = hidden.astype(F32) + biases_ref[4, pl.ds(tower, 1), :]
        for c in range(4):
            cols = slice(768 * c, 768 * c + 768)
            inner = dot(hidden, fin_s[tower, :, cols]) + ffnb_ref[pl.ds(tower, 1), cols]
            second_sum = second_sum + dot(gelu(inner).astype(BF16), fout_s[tower, cols, :])
        n2, _ = norm_stats(second_sum)
        slot = lax.rem(step, 2)

        @pl.when(step >= 2)
        def _():
            pltpu.make_async_copy(out_s.at[slot], out_hbm.at[tower, rows], osem.at[slot]).wait()

        out_s[slot] = (
            n2 * gains_ref[tower, 1:2, :] + biases_ref[5, pl.ds(tower, 1), :]
        ).astype(BF16)
        pltpu.make_async_copy(out_s.at[slot], out_hbm.at[tower, rows], osem.at[slot]).start()
        return 0

    lax.fori_loop(0, 8, tile, 0)
    for c in c2 + last_hop + swaps + own_copy[1:]:
        c.wait()
    for i in range(2):
        pltpu.make_async_copy(out_s.at[i], out_hbm.at[1, 0:256], osem.at[i]).wait()
    ga = ga_ref.reshape(16, 96, 768)
    gs = gs_ref.reshape(16, 64, 768)
    save_ga = pltpu.make_async_copy(ga_ref, ga_hbm, osem.at[2])
    save_ga.start()

    save_part = pltpu.make_async_copy(q_s.at[:, 0:768], part_hbm, osem.at[3])
    save_dsp = [
        pltpu.make_async_copy(kv_s.at[0, 0:768, 0:tokens], dspq_hbm, osem.at[5]),
        pltpu.make_async_copy(kv_s.at[1, 0:192, 0:tokens], dspp_hbm, osem.at[6]),
    ]
    save_uw = pltpu.make_async_copy(x_s.at[0, 0:960], uw_hbm, osem.at[4])

    qv = jnp.concatenate([ga[:, 0:32].reshape(512, 768), gs[:, 0:32].reshape(512, 768)], 0)
    pv_own = ga[:, 32:48].astype(F32)[:, 8:16].reshape(128, 768)
    pv_sib = gs[:, 32:48].astype(F32)[:, 8:16].reshape(128, 768)
    pv = jnp.concatenate([pv_own, pv_sib], 0).astype(BF16)
    ext_own = ga[:, 48:64].astype(F32)[:, 8:16]
    ext_sib = gs[:, 48:64].astype(F32)[:, 8:16]
    _, eq_own = ext_rows(ext_own)
    _, eq_sib = ext_rows(ext_sib)
    eq = jnp.concatenate([eq_own, eq_sib], 0)
    label = (eq[:, 6:7] * 256.0 + eq[:, 7:8]).astype(jnp.int32)
    col = iota((1, 256), 1)
    within = lax.rem(col, 128)
    side = jnp.where(col < 128, g, 1 - g)
    ids = (within // 8) * 16 + side * 8 + lax.rem(within, 8)
    logits = SCORE_SCALE * dot_nt(qv, pv)
    top = jnp.max(logits, -1, keepdims=True)
    norm_log = top + jnp.log(jnp.sum(jnp.exp(logits - top), -1, keepdims=True))
    hit = label == ids
    positive = jnp.sum(jnp.where(hit, logits, 0.0), -1, keepdims=True)
    grad = (jnp.exp(logits - norm_log) - jnp.where(hit, 1.0, 0.0)).astype(BF16)
    loss_s[...] = jnp.broadcast_to((norm_log - positive)[:512], (512, 128))
    own_loss = loss_s[pl.ds(pl.multiple_of(me * 32, 32), 32), 0:32]
    diagonal = iota((32, 32), 0) == iota((32, 32), 1)
    loss_ref[...] = jnp.sum(jnp.where(diagonal, own_loss, 0.0), 0, keepdims=True)
    upq_ref[...] = SCORE_SCALE * dot(grad[:512], pv)
    upp_ref[...] = SCORE_SCALE * dot_tn(grad[:, 0:128], qv)

    mine = ga[me]
    low = mine[32:64].astype(F32)
    gq_rows, keep = [], []
    for t, (count, up, hidden, vec, q, inn_ref, inv_ref, p_s) in enumerate((
        (32, upq_ref[pl.ds(pl.multiple_of(me * 32, 32), 32), :], mine[64:96].astype(F32),
         mine[0:32].astype(F32), qq_ref[...].astype(F32), innq_ref, invq_ref, pq_s),
        (8, upp_ref[pl.ds(pl.multiple_of(me * 8, 8), 8), :], low[0:8], low[8:16], low[16:24],
         innp_ref, invp_ref, pp_s),
    )):
        g0, g1 = gains_ref[t, 0:1, :], gains_ref[t, 1:2, :]
        n2 = (vec - biases_ref[5, t:t + 1, :]) / g1
        n1 = (hidden - biases_ref[3, t:t + 1, :]) / g0
        grad_second = norm_back(up, g1, n2, inv_ref[:, 1:2])
        grad_ffn = grad_second.astype(BF16)
        grad_active = dot_nt(grad_ffn, fout_s[t])
        _, slope = gelu_pair(inn_ref[...])
        grad_inner = (grad_active * slope).astype(BF16)
        grad_hidden = grad_second + dot_nt(grad_inner, fin_s[t])
        grad_first = norm_back(grad_hidden, g0, n1, inv_ref[:, 0:1])
        gm = dot_nt(grad_first.astype(BF16), wout_s[t]).astype(BF16)
        wide = expand_heads(gm.astype(F32)).astype(BF16)
        dp = dot_nt(wide, kv_s[t, :, 768:1536])
        soft = p_s[...]
        ds = (soft * (dp - jnp.sum(soft * dp, -1, keepdims=True))).astype(BF16)
        gq = fold_heads(dot(ds, kv_s[t, :, 0:768]), count) * KEY_SCALE
        gq_rows.append(gq)
        y = dot(ds, x_s[t]) * KEY_SCALE
        if t == 0:
            spread = expand_heads(q).astype(BF16)
            q_s[0, 0:768, :] = dot_tn(y.astype(BF16), spread).astype(BF16)
            q_s[1, 0:768, :] = dot_tn(zq_ref[...], wide).astype(BF16)
            save_part.start()
        else:
            yt_ref[...] = jnp.concatenate([y, jnp.zeros((32, 768), F32)], 0).T.astype(BF16)
        at = 768 * t
        n = HEADS * count
        u = dot_nt(expand_heads(q).astype(BF16), win_s[t, :, 768:1536]) * KEY_SCALE
        x_s[0, at:at + n, :] = u.astype(BF16)
        if t == 0:
            x_s[0, 384:768, :] = dot_nt(wide, win_s[t, :, 1536:2304]).astype(BF16)
        else:
            x_s[0, 864:960, :] = dot_nt(wide, win_s[t, :, 1536:2304]).astype(BF16)
        kv_s[t, 0:n, 0:tokens] = ds
        kv_s[t, n:2 * n, 0:tokens] = soft.astype(BF16)
        save_dsp[t].start()
        extra = dot_nt(gq.astype(BF16), win_s[t, :, 0:768]) + grad_first
        ext_ref[32 * t:32 * t + count, :] = extra
    gq_ref[...] = jnp.concatenate(gq_rows + [jnp.zeros((8, 768), F32)], 0).astype(BF16)
    save_uw.start()
    for c in [save_ga, save_part, save_uw] + save_dsp:
        c.wait()


def run_forward(xq, xp, lengths, labels, weights):
    attn_in, attn_out, ffn_in, ffn_out, gains, biases, ffn_bias = weights
    tokens = xq.shape[0]
    vm = pl.BlockSpec(memory_space=pltpu.VMEM)
    hb = pl.BlockSpec(memory_space=pl.ANY)
    sds = jax.ShapeDtypeStruct
    return pl.pallas_call(
        forward_kernel,
        out_shape=[
            sds((2, tokens, 768), BF16), sds((4, 4, 96, 768), BF16), sds((16, 96, 128), BF16),
            sds((2, 768, 768), BF16), sds((960, 768), BF16),
            sds((768, tokens), BF16), sds((192, tokens), BF16),
            sds((1, 32), F32), sds((512, 768), F32), sds((128, 768), F32),
            sds((48, 768), BF16), sds((768, 128), BF16),
            sds((40, 768), F32),
        ],
        in_specs=[pl.BlockSpec(memory_space=pltpu.SMEM), vm, vm, vm, vm] + [hb] * 6,
        out_specs=[hb] * 7 + [vm] * 6,
        scratch_shapes=[
            pltpu.VMEM((2, tokens, 768), BF16), pltpu.VMEM((2, tokens, 768), BF16),
            pltpu.VMEM((2, tokens, 1536), BF16),
            pltpu.VMEM((2, 768, 2304), BF16), pltpu.VMEM((2, 768, 768), BF16),
            pltpu.VMEM((2, 768, 3072), BF16), pltpu.VMEM((2, 3072, 768), BF16),
            pltpu.VMEM((384, tokens), F32), pltpu.VMEM((96, tokens), F32),
            pltpu.VMEM((2, 256, 768), BF16), pltpu.VMEM((256, 768), BF16),
            pltpu.VMEM((256, 512), F32),
            pltpu.VMEM((96, 768), BF16), pltpu.VMEM((16, 96, 128), BF16),
            pltpu.VMEM((4, 4, 96, 768), BF16), pltpu.VMEM((4, 4, 64, 768), BF16),
            pltpu.VMEM((32, 3072), F32), pltpu.VMEM((8, 3072), F32),
            pltpu.VMEM((32, 128), F32), pltpu.VMEM((8, 128), F32),
            pltpu.VMEM((32, 768), BF16), pltpu.VMEM((384, 768), BF16), pltpu.VMEM((512, 128), F32),
            pltpu.SemaphoreType.DMA((2, 5)), pltpu.SemaphoreType.DMA((2,)), pltpu.SemaphoreType.DMA((7,)),
            pltpu.SemaphoreType.DMA((15,)), pltpu.SemaphoreType.DMA((15,)),
            pltpu.SemaphoreType.DMA((16,)), pltpu.SemaphoreType.DMA((16,)),
        ],
        compiler_params=pltpu.CompilerParams(
            collective_id=1, has_side_effects=True, vmem_limit_bytes=63 * 1024 * 1024
        ),
        name="forward",
    )(lengths, labels.reshape(1, -1), gains, biases, ffn_bias, xq, xp, attn_in, attn_out, ffn_in, ffn_out)


QR, PR = 512, 128


def last_kernel(
    gains_ref, biases_ref, ffnb_ref, upq_ref, upp_ref, gq_ref, yt_ref,
    part_hbm, ga_hbm, rsw_hbm, wout_hbm, fin_hbm, fout_hbm,
    pwin_ref, pwout_ref, pfin_ref, pfout_ref, psum_ref, pffb_ref,
    swin_ref, swout_ref, sfin_ref, sfout_ref, ssum_ref, sffb_ref,
    rgq_s, ryt_s, ga_s, rsw_s, own_s, sib_s, r1_s, s2_s, r2_s, wout_s, fin_s, fout_s,
    act_s, gin_s, gffn_s, gat_s, gm_s, tr_s, acc_s,
    sem, lsem, ss, rs, as_, ar, xs, xr, ks, kr,
):
    me, g = place()
    greet(me, g)
    z, yx = me // 4, lax.rem(me, 4)
    first, second, third = gather_phases(me, g, gq_ref, rgq_s, ss, rs, 0, 0, 48)
    swaps = []
    for i in range(1, 16):
        peer = lax.rem(me + i, 16)
        swaps.append(remote(yt_ref.at[peer], ryt_s.at[me], as_.at[i], ar.at[i], (peer, g)))
    own = [
        pltpu.make_async_copy(gq_ref, rgq_s.at[z, yx], lsem.at[0]),
        pltpu.make_async_copy(yt_ref.at[me], ryt_s.at[me], lsem.at[1]),
    ]
    sib = (me, 1 - g)
    load_part = pltpu.make_async_copy(part_hbm.at[g], own_s, lsem.at[2])
    pair = [remote(part_hbm.at[1 - g], sib_s, ks.at[0], kr.at[0], sib)]
    xpeer = me + 1 - 2 * lax.rem(me, 2)
    ypeer = me + 2 - 4 * (lax.rem(me, 4) // 2)
    dpeer = xpeer + 2 - 4 * (lax.rem(xpeer, 4) // 2)
    plane = [
        remote(own_s.at[:, lax.rem(peer, 4)], r1_s.at[k], ks.at[1 + k], kr.at[1 + k], (peer, g))
        for k, peer in enumerate((dpeer, xpeer, ypeer))
    ]
    column = [
        remote(s2_s.at[lax.rem(z + d, 4)], r2_s.at[d - 1], ks.at[3 + d], kr.at[3 + d],
               (lax.rem(z + d, 4) * 4 + yx, g))
        for d in range(1, 4)
    ]

    def add_pair():
        def one(i, _):
            own_s[i] = (own_s[i].astype(F32) + sib_s[i].astype(F32)).astype(BF16)
            return 0

        lax.fori_loop(0, 4, one, 0)

    def add_plane():
        def one(i, _):
            s2_s[i] = (
                own_s[i, yx].astype(F32) + r1_s[0, i].astype(F32)
                + r1_s[1, i].astype(F32) + r1_s[2, i].astype(F32)
            ).astype(BF16)
            return 0

        lax.fori_loop(0, 4, one, 0)

    early = [
        remote(pwout_ref, swout_ref, xs.at[0], xr.at[0], sib),
        remote(pfin_ref, sfin_ref, xs.at[1], xr.at[1], sib),
        remote(pfout_ref, sfout_ref, xs.at[2], xr.at[2], sib),
        remote(pffb_ref, sffb_ref, xs.at[3], xr.at[3], sib),
    ]
    late = [
        remote(pwin_ref, swin_ref, xs.at[4], xr.at[4], sib),
        remote(psum_ref, ssum_ref, xs.at[5], xr.at[5], sib),
    ]
    load_ga = pltpu.make_async_copy(ga_hbm, ga_s, sem.at[0])
    load_fin = [pltpu.make_async_copy(fin_hbm.at[t], fin_s.at[t], sem.at[1 + t]) for t in range(2)]
    load_fout = [pltpu.make_async_copy(fout_hbm.at[t], fout_s.at[t], sem.at[3 + t]) for t in range(2)]
    load_wout = pltpu.make_async_copy(wout_hbm, wout_s, sem.at[5])
    load_rest = [
        pltpu.make_async_copy(rsw_hbm, rsw_s, sem.at[6]),
    ]
    for c in [load_part, load_ga, load_fin[0], load_fout[0], load_wout, load_fin[1], load_fout[1]] + load_rest + own:
        c.start()
    greeted()
    for c in pair + first + swaps:
        c.start()

    load_ga.wait()
    load_wout.wait()
    ext = ga_s[:, 48:64].astype(F32)[:, 8:16]
    ext_p, ext_q = ext_rows(ext)
    psum_ref[...] = jnp.zeros(psum_ref.shape, F32)
    pffb_ref[...] = jnp.zeros(pffb_ref.shape, F32)

    def chain(t, up, hidden, vec, inv1, inv2, rows, count):
        g0, g1 = gains_ref[t, 0:1, :], gains_ref[t, 1:2, :]
        n2 = (vec.astype(F32) - biases_ref[5, t:t + 1, :]) / g1
        n1 = (hidden.astype(F32) - biases_ref[3, t:t + 1, :]) / g0
        grad_second = norm_back(up, g1, n2, inv2)
        grad_ffn = grad_second.astype(BF16)
        gffn_s[rows, :] = grad_ffn
        grad_hidden = grad_second
        for c in range(4):
            cols = slice(768 * c, 768 * c + 768)
            inner = dot(hidden, fin_s[t, :, cols]) + ffnb_ref[t:t + 1, cols]
            active, slope = gelu_pair(inner)
            act_s[rows, cols] = active.astype(BF16)
            grad_inner = (dot_nt(grad_ffn, fout_s[t, cols, :]) * slope).astype(BF16)
            gin_s[rows, cols] = grad_inner
            pffb_ref[t:t + 1, cols] += jnp.sum(grad_inner.astype(F32), 0, keepdims=True)
            grad_hidden = grad_hidden + dot_nt(grad_inner, fin_s[t, :, cols])
        grad_first = norm_back(grad_hidden, g0, n1, inv1)
        grad_attn = grad_first.astype(BF16)
        gat_s[rows, :] = grad_attn
        gm = dot_nt(grad_attn, wout_s[t]).astype(BF16)
        gm_s[rows, :] = gm
        total = lambda v: jnp.sum(v, 0, keepdims=True)
        psum_ref[t, 0:8, :] += jnp.concatenate([
            total(grad_hidden * n1), total(up * n2), jnp.zeros((1, 768), F32),
            total(gm.astype(F32)), total(grad_attn.astype(F32)), total(grad_hidden),
            total(grad_ffn.astype(F32)), total(up),
        ], 0)

    i1q, i2q = decode_inv(ext_q)
    i1p, i2p = decode_inv(ext_p)
    for blk in range(2):
        if blk == 0:
            load_fin[0].wait()
            load_fout[0].wait()
        lo = blk * 256
        chain(
            0, upq_ref[lo:lo + 256, :],
            ga_s[8 * blk:8 * blk + 8, 64:96].reshape(256, 768),
            ga_s[8 * blk:8 * blk + 8, 0:32].reshape(256, 768),
            i1q[lo:lo + 256], i2q[lo:lo + 256], slice(lo, lo + 256), 256,
        )
        if blk == 0:
            load_part.wait()
            for c in pair:
                c.wait()
            add_pair()
            for c in plane:
                c.start()
            own[0].wait()
            for c in first:
                c.wait()
            for c in second:
                c.start()
    load_fin[1].wait()
    load_fout[1].wait()
    hv = ga_s[:, 32:48].astype(F32)
    chain(
        1, upp_ref[...], hv[:, 0:8].reshape(128, 768).astype(BF16),
        hv[:, 8:16].reshape(128, 768).astype(BF16), i1p, i2p, slice(QR, QR + PR), 128,
    )
    for c in plane:
        c.wait()
    add_plane()
    for c in column:
        c.start()
    for c in second:
        c.wait()
    for c in third:
        c.start()

    for c in load_rest:
        c.wait()
    for t, rows in enumerate((slice(0, QR), slice(QR, QR + PR))):
        count = rows.stop - rows.start
        fo_at = pl.multiple_of((me // 2) * 384, 128)
        tr_s[:, 0:count] = act_s[rows, pl.ds(fo_at, 384)].astype(F32).T.astype(BF16)
        fo_row = pl.multiple_of(lax.rem(me, 2) * 192, 16)
        pfout_ref[t] = dot(tr_s[pl.ds(fo_row, 192), 0:count], gffn_s[rows, :])
        fi_at = pl.multiple_of((me // 8) * 384, 128)
        if t == 0:
            hid = ga_s[:, 64:96, pl.ds(fi_at, 384)].reshape(QR, 384)
        else:
            hid = ga_s[:, 32:48, pl.ds(fi_at, 384)].astype(F32)[:, 0:8].reshape(PR, 384)
        tr_s[:, 0:count] = hid.astype(F32).T.astype(BF16)
        fi_row = pl.multiple_of(lax.rem(me, 8) * 48, 16)
        pfin_ref[t] = dot(tr_s[pl.ds(fi_row, 48), 0:count], gin_s[rows, :])
        if t == 0:
            mx = rsw_s[:, 0:32].reshape(QR, 128)
        else:
            mx = rsw_s[:, 32:48].astype(F32)[:, 0:8].reshape(PR, 128).astype(BF16)
        pwout_ref[t] = dot_tn(mx, gat_s[rows, :])[0:48]
    for c in early:
        c.start()

    def low_rank(read_t, read_p, out_col):
        acc_s[...] = jnp.zeros(acc_s.shape, F32)

        def source(i, _):
            wide = jnp.concatenate([expand_heads(read_p(i)), jnp.zeros((32, 768), F32)], 0)
            acc_s[...] += dot(read_t(i), wide.astype(BF16))
            return 0

        lax.fori_loop(0, 16, source, 0)
        pwin_ref[1, :, out_col:out_col + 768] = acc_s[...]

    def gm_p(i):
        pair = gm_s[pl.ds(pl.multiple_of(QR + (i // 2) * 16, 16), 16), :].astype(F32)
        return jnp.where(lax.rem(i, 2) == 0, pair[0:8], pair[8:16])

    low_rank(lambda i: rsw_s[i, 48:96, :], gm_p, 1536)

    for c in third:
        c.wait()
    for c in swaps:
        c.wait()
    own[1].wait()

    def q_p(i):
        return ga_s[i, 48:64, :].astype(F32)[0:8]

    low_rank(lambda i: ryt_s[i], q_p, 768)
    rg_q = rgq_s[:, :, 0:32].reshape(QR, 768)
    rg_p = rgq_s[:, :, 32:48].astype(F32)[:, :, 0:8].reshape(PR, 768)
    pwin_ref[0, :, 0:768] = dot_tn(rsw_s[:, 0:32].reshape(QR, 128), rg_q)[64:112]
    x_p = rsw_s[:, 32:48].astype(F32)[:, 0:8].reshape(PR, 128).astype(BF16)
    pwin_ref[1, :, 0:768] = dot_tn(x_p, rg_p.astype(BF16))[64:112]
    for c in column:
        c.wait()
    pwin_ref[0, :, pl.ds(pl.multiple_of(768 + 768 * g, 128), 768)] = (
        s2_s[z].astype(F32) + r2_s[0].astype(F32) + r2_s[1].astype(F32) + r2_s[2].astype(F32)
    )
    pwin_ref[0, :, pl.ds(pl.multiple_of(1536 - 768 * g, 128), 768)] = jnp.zeros((48, 768), F32)
    psum_ref[0, 2:3, :] = jnp.sum(rg_q.astype(F32), 0, keepdims=True)
    psum_ref[1, 2:3, :] = jnp.sum(rg_p, 0, keepdims=True)
    for c in late:
        c.start()
    for c in early + late:
        c.wait()


def last(weights, upq, upp, gq, yt, part, ga, rsw):
    attn_in, attn_out, ffn_in, ffn_out, gains, biases, ffn_bias = weights
    vm = pl.BlockSpec(memory_space=pltpu.VMEM)
    hb = pl.BlockSpec(memory_space=pl.ANY)
    sds = jax.ShapeDtypeStruct
    parts = [
        sds((2, 48, 2304), F32), sds((2, 48, 768), F32), sds((2, 48, 3072), F32),
        sds((2, 192, 768), F32), sds((2, 8, 768), F32), sds((2, 3072), F32),
    ]
    return pl.pallas_call(
        last_kernel,
        out_shape=parts + parts,
        in_specs=[vm] * 7 + [hb] * 6,
        out_specs=[vm] * 12,
        scratch_shapes=[
            pltpu.VMEM((4, 4, 48, 768), BF16), pltpu.VMEM((16, 48, 128), BF16),
            pltpu.VMEM((16, 96, 768), BF16), pltpu.VMEM((16, 96, 128), BF16),
            pltpu.VMEM((4, 4, 48, 768), BF16), pltpu.VMEM((4, 4, 48, 768), BF16),
            pltpu.VMEM((3, 4, 48, 768), BF16), pltpu.VMEM((4, 48, 768), BF16),
            pltpu.VMEM((3, 48, 768), BF16), pltpu.VMEM((2, 768, 768), BF16),
            pltpu.VMEM((2, 768, 3072), BF16), pltpu.VMEM((2, 3072, 768), BF16),
            pltpu.VMEM((640, 3072), BF16), pltpu.VMEM((640, 3072), BF16),
            pltpu.VMEM((640, 768), BF16), pltpu.VMEM((640, 768), BF16), pltpu.VMEM((640, 768), BF16),
            pltpu.VMEM((384, 512), BF16),
            pltpu.VMEM((48, 768), F32),
            pltpu.SemaphoreType.DMA((11,)), pltpu.SemaphoreType.DMA((4,)),
            pltpu.SemaphoreType.DMA((7,)), pltpu.SemaphoreType.DMA((7,)),
            pltpu.SemaphoreType.DMA((16,)), pltpu.SemaphoreType.DMA((16,)),
            pltpu.SemaphoreType.DMA((6,)), pltpu.SemaphoreType.DMA((6,)),
            pltpu.SemaphoreType.DMA((7,)), pltpu.SemaphoreType.DMA((7,)),
        ],
        compiler_params=pltpu.CompilerParams(
            collective_id=2, has_side_effects=True, vmem_limit_bytes=62 * 1024 * 1024
        ),
        name="last",
    )(gains, biases, ffn_bias, upq, upp, gq, yt.reshape(16, 48, 128),
      part.reshape(2, 4, 4, 48, 768), ga.reshape(16, 96, 768), rsw, attn_out, ffn_in, ffn_out)


def finish_kernel(
    lens_ref, loss_in, ext_ref, dspq_hbm, dspp_hbm, uw_hbm, raw_hbm, *refs,
):
    ins, outs, (loss_ref, outq_hbm, outp_hbm, dxq_hbm, dxp_hbm), scratch = (
        refs[:12], refs[12:19], refs[19:24], refs[24:]
    )
    part_s, raw_s, sum_s = scratch[:12], scratch[12], scratch[13:17]
    dx_s, dspq_ref, dspp_ref, uw_ref, psem, rsem, ssem, dsem, osem = scratch[17:]
    me, _ = place()
    raw_in = pltpu.make_async_copy(raw_hbm, raw_s, rsem.at[2])
    raw_out = [pltpu.make_async_copy(raw_s.at[t], (outq_hbm, outp_hbm)[t], rsem.at[t]) for t in range(2)]
    gets = [
        pltpu.make_async_copy(uw_hbm, uw_ref, osem.at[0]),
        pltpu.make_async_copy(dspq_hbm, dspq_ref, osem.at[1]),
        pltpu.make_async_copy(dspp_hbm, dspp_ref, osem.at[2]),
    ]
    for c in gets:
        c.start()
    raw_in.start()
    loads = [pltpu.make_async_copy(ins[k], part_s[k], psem.at[k]) for k in range(12)]
    for c in loads:
        c.start()
    loss_ref[...] = loss_in[...]

    for c in gets:
        c.wait()
    extra_p = ext_ref[32:40, :]
    e_hi = extra_p.astype(BF16).astype(F32)
    uw_p = jnp.concatenate([uw_ref[768:960, :].astype(F32), e_hi, extra_p - e_hi], 0).astype(BF16)
    keep = []
    for t in range(2):
        for m in range(4):
            cols = slice(256 * m, 256 * m + 256)
            k = t * 4 + m
            if k >= 2:
                keep[k - 2].wait()
            if t == 0:
                dx_s[k % 2] = dot_tn(dspq_ref[:, cols], uw_ref[0:768, :])
                for c in range(8):
                    dx_s[k % 2, 32 * c:32 * c + 1, :] += ext_ref[8 * m + c:8 * m + c + 1, :]
            else:
                colr = iota((8, 256), 1) + 256 * m
                rowr = iota((8, 256), 0)
                start = jnp.zeros((8, 256), jnp.int32)
                for r in range(2):
                    at = jnp.int32(r * 512)
                    for c in range(4):
                        start = jnp.where(rowr == r * 4 + c, at, start)
                        at = at + lens_ref[r, c]
                sel = jnp.where(colr == start, 1.0, 0.0)
                sel2 = jnp.concatenate([sel, sel], 0).astype(BF16)
                lhs = jnp.concatenate([dspp_ref[:, cols], sel2], 0)
                dx_s[k % 2] = dot_tn(lhs, uw_p)
            c = pltpu.make_async_copy(dx_s.at[k % 2], (dxq_hbm, dxp_hbm)[t].at[cols], dsem.at[k % 2])
            c.start()
            keep.append(c)
            if k == 1:
                raw_in.wait()
                for c in raw_out:
                    c.start()

    stores = []
    for k in range(4):
        loads[k].wait()
        loads[6 + k].wait()
        sum_s[k][...] = part_s[k][...] + part_s[6 + k][...]
        c = pltpu.make_async_copy(sum_s[k], outs[k], ssem.at[k])
        c.start()
        stores.append(c)
    for k in (4, 5, 10, 11):
        loads[k].wait()
    shift = lax.rem(768 - 48 * me, 768)
    for t in range(2):
        sums = pltpu.roll(part_s[4][t] + part_s[10][t], shift, 1)[:, 0:48]
        outs[4][t] = sums[0:2]
        for j in range(6):
            outs[5][j, t:t + 1, :] = sums[2 + j:3 + j]
    ffb = part_s[5][...] + part_s[11][...]
    wide = jnp.concatenate([ffb, jnp.zeros((6, 3072), F32)], 0)
    outs[6][...] = pltpu.roll(wide, lax.rem(3072 - 192 * me, 3072), 1)[0:2, 0:192]
    for c in keep[6:] + stores + raw_out:
        c.wait()


def finish(lengths, loss, dspq, dspp, uw, ext, raw, parts):
    sds = jax.ShapeDtypeStruct
    tokens = dspq.shape[1]
    vm = pl.BlockSpec(memory_space=pltpu.VMEM)
    hb = pl.BlockSpec(memory_space=pl.ANY)
    return pl.pallas_call(
        finish_kernel,
        out_shape=[sds(p.shape, F32) for p in parts[:4]]
        + [sds((2, 2, 48), F32), sds((6, 2, 48), F32), sds((2, 192), F32)]
        + [sds((1, 32), F32), sds((tokens, 768), BF16), sds((tokens, 768), BF16)]
        + [sds((tokens, 768), F32), sds((tokens, 768), F32)],
        in_specs=[pl.BlockSpec(memory_space=pltpu.SMEM)] + [vm] * 2 + [hb] * 16,
        out_specs=[hb] * 4 + [vm] * 4 + [hb] * 4,
        scratch_shapes=[pltpu.VMEM(p.shape, F32) for p in parts]
        + [pltpu.VMEM((2, tokens, 768), BF16)]
        + [pltpu.VMEM(p.shape, F32) for p in parts[:4]]
        + [pltpu.VMEM((2, 256, 768), F32), pltpu.VMEM((768, tokens), BF16)]
        + [pltpu.VMEM((192, tokens), BF16), pltpu.VMEM((960, 768), BF16)]
        + [pltpu.SemaphoreType.DMA((n,)) for n in (12, 3, 4, 2, 3)],
        compiler_params=pltpu.CompilerParams(vmem_limit_bytes=VMEM_LIMIT),
        name="finish",
    )(lengths, loss, ext, dspq, dspp, uw, raw, *parts)


def fast_shards(query_tokens, passage_tokens, lengths, labels, *weights):
    xq = query_tokens.reshape(-1, 768)
    xp = passage_tokens.reshape(-1, 768)
    weights = weights[:5] + (weights[5].transpose(1, 0, 2), weights[6])
    raw, ga, rsw, part, uw, dspq, dspp, loss, upq, upp, gq, yt, ext = run_forward(
        xq, xp, lengths, labels, weights
    )
    parts = last(weights, upq, upp, gq, yt, part, ga, rsw)
    win, wout, fin, fout, gains, biases, ffb, loss, outq, outp, dxq, dxp = finish(
        lengths, loss, dspq, dspp, uw, ext, raw, parts
    )
    return (
        loss.reshape(-1),
        outq.reshape(query_tokens.shape),
        outp.reshape(passage_tokens.shape),
        dxq.reshape(query_tokens.shape),
        dxp.reshape(passage_tokens.shape),
        win, wout, fin, fout, gains, biases.transpose(1, 0, 2), ffb,
    )


def layer_norm(residual, gain_vec, shift_vec):
    centre = residual - jnp.mean(residual, -1, keepdims=True)
    inverse = lax.rsqrt(jnp.mean(centre * centre, -1, keepdims=True) + EPSILON)
    return centre * inverse * gain_vec + shift_vec


def plain_norm_back(residual, gain_vec, upstream):
    centre = residual - jnp.mean(residual, -1, keepdims=True)
    inverse = lax.rsqrt(jnp.mean(centre * centre, -1, keepdims=True) + EPSILON)
    normed = centre * inverse
    scaled = upstream * gain_vec
    grad_res = inverse * (
        scaled
        - jnp.mean(scaled, -1, keepdims=True)
        - normed * jnp.mean(scaled * normed, -1, keepdims=True)
    )
    return (grad_res, jnp.sum(upstream * normed, 0), jnp.sum(upstream, 0))


def cls_index(starts, seq_len):
    return (jnp.arange(starts.shape[0], dtype=jnp.int32)[:, None] * seq_len + starts).reshape(-1)


def forward(tokens, segment, starts, params):
    attn_in, attn_out, ffn_in, ffn_out, gains, biases, ffn_bias = params
    batch_size, seq_len, feature = tokens.shape
    head_count = feature // HEAD_DIM
    flat_tokens = tokens.reshape(batch_size * seq_len, feature)
    zeros_vec = jnp.zeros_like(biases[0])
    joined = jnp.dot(flat_tokens, attn_in, preferred_element_type=jnp.float32) + jnp.concatenate(
        [biases[0], zeros_vec, biases[1]]
    )
    joined = joined.astype(jnp.bfloat16)
    shaped = joined.reshape(batch_size, seq_len, 3, head_count, HEAD_DIM)
    scores = (
        jnp.einsum(
            "bqhd,bkhd->bhqk", shaped[:, :, 0], shaped[:, :, 1], preferred_element_type=jnp.float32
        )
        * KEY_SCALE
    )
    same_seg = segment[:, :, None] == segment[:, None, :]
    scores = jnp.where(same_seg[:, None], scores, -1000000000.0)
    attention = jax.nn.softmax(scores, -1).astype(jnp.bfloat16)
    mixed = jnp.einsum(
        "bhqk,bkhd->bqhd", attention, shaped[:, :, 2], preferred_element_type=jnp.float32
    )
    mixed = mixed.reshape(batch_size * seq_len, feature).astype(jnp.bfloat16)
    first_sum = flat_tokens.astype(jnp.float32) + (
        jnp.dot(mixed, attn_out, preferred_element_type=jnp.float32) + biases[2]
    )
    hidden = layer_norm(first_sum, gains[0], biases[3]).astype(jnp.bfloat16)
    inner = jnp.dot(hidden, ffn_in, preferred_element_type=jnp.float32) + ffn_bias
    active = jax.nn.gelu(inner).astype(jnp.bfloat16)
    second_sum = hidden.astype(jnp.float32) + (
        jnp.dot(active, ffn_out, preferred_element_type=jnp.float32) + biases[4]
    )
    output = layer_norm(second_sum, gains[1], biases[5]).astype(jnp.bfloat16)
    picked = cls_index(starts, seq_len)
    kept = (
        flat_tokens,
        joined,
        mixed[picked],
        first_sum[picked],
        hidden[picked],
        inner[picked],
        active[picked],
        second_sum[picked],
    )
    return (output, picked, kept)


def backward(kept, segment, starts, params, upstream):
    attn_in, attn_out, ffn_in, ffn_out, gains, biases, ffn_bias = params
    flat_tokens, joined, mixed_cls, first_cls, hidden_cls, inner_cls, active_cls, second_cls = kept
    batch_size, seq_len = segment.shape
    per_row = starts.shape[1]
    feature = flat_tokens.shape[1]
    head_count = feature // HEAD_DIM
    grad_second, gain_two, shift_two = plain_norm_back(second_cls, gains[1], upstream)
    grad_ffn = grad_second.astype(jnp.bfloat16)
    grad_down = jnp.dot(active_cls.T, grad_ffn, preferred_element_type=jnp.float32)
    grad_active = jnp.dot(grad_ffn, ffn_out.T, preferred_element_type=jnp.float32)
    grad_inner = jax.vjp(jax.nn.gelu, inner_cls)[1](grad_active)[0].astype(jnp.bfloat16)
    grad_up = jnp.dot(hidden_cls.T, grad_inner, preferred_element_type=jnp.float32)
    grad_hidden = grad_second + jnp.dot(grad_inner, ffn_in.T, preferred_element_type=jnp.float32)
    grad_first, gain_one, shift_one = plain_norm_back(first_cls, gains[0], grad_hidden)
    grad_attn = grad_first.astype(jnp.bfloat16)
    grad_outproj = jnp.dot(mixed_cls.T, grad_attn, preferred_element_type=jnp.float32)
    grad_mixed = jnp.dot(grad_attn, attn_out.T, preferred_element_type=jnp.float32).astype(
        jnp.bfloat16
    )
    grad_mixed = grad_mixed.reshape(batch_size, per_row, head_count, HEAD_DIM)
    shaped = joined.reshape(batch_size, seq_len, 3, head_count, HEAD_DIM)
    key_part = shaped[:, :, 1]
    value_part = shaped[:, :, 2]
    picked = cls_index(starts, seq_len)
    query_cls = joined[picked, :feature].reshape(batch_size, per_row, head_count, HEAD_DIM)
    own_seg = jnp.take_along_axis(segment, starts, 1)
    scores = (
        jnp.einsum("bchd,bkhd->bhck", query_cls, key_part, preferred_element_type=jnp.float32)
        * KEY_SCALE
    )
    scores = jnp.where((own_seg[:, :, None] == segment[:, None, :])[:, None], scores, -1000000000.0)
    attention = jax.nn.softmax(scores, -1)
    grad_attention = jnp.einsum(
        "bchd,bkhd->bhck", grad_mixed, value_part, preferred_element_type=jnp.float32
    )
    grad_scores = attention * (
        grad_attention - jnp.sum(attention * grad_attention, -1, keepdims=True)
    )
    grad_scores = grad_scores.astype(jnp.bfloat16)
    grad_query = (
        jnp.einsum("bhck,bkhd->bchd", grad_scores, key_part, preferred_element_type=jnp.float32)
        * KEY_SCALE
    ).astype(jnp.bfloat16)
    grad_key = (
        jnp.einsum("bhck,bchd->bkhd", grad_scores, query_cls, preferred_element_type=jnp.float32)
        * KEY_SCALE
    ).astype(jnp.bfloat16)
    grad_value = jnp.einsum(
        "bhck,bchd->bkhd",
        attention.astype(jnp.bfloat16),
        grad_mixed,
        preferred_element_type=jnp.float32,
    ).astype(jnp.bfloat16)
    places = jnp.arange(seq_len, dtype=jnp.int32)
    selector = (starts[:, :, None] == places[None, None, :]).astype(jnp.bfloat16)
    grad_query_full = jnp.einsum(
        "bcl,bchd->blhd", selector, grad_query, preferred_element_type=jnp.float32
    ).astype(jnp.bfloat16)
    grad_joined = jnp.stack([grad_query_full, grad_key, grad_value], 2).reshape(
        batch_size * seq_len, 3 * feature
    )
    grad_inproj = jnp.dot(flat_tokens.T, grad_joined, preferred_element_type=jnp.float32)
    grad_tokens = (
        jnp.dot(grad_joined, attn_in.T, preferred_element_type=jnp.float32)
        .at[picked]
        .add(grad_first)
    )
    bias_grads = jnp.stack(
        [
            jnp.sum(grad_query.astype(jnp.float32), (0, 1)).reshape(feature),
            jnp.sum(grad_value.astype(jnp.float32), (0, 1)).reshape(feature),
            jnp.sum(grad_attn.astype(jnp.float32), 0),
            shift_one,
            jnp.sum(grad_ffn.astype(jnp.float32), 0),
            shift_two,
        ]
    )
    gain_grads = jnp.stack([gain_one, gain_two])
    hidden_bias = jnp.sum(grad_inner.astype(jnp.float32), 0)
    grads = (grad_inproj, grad_outproj, grad_up, grad_down, gain_grads, bias_grads, hidden_bias)
    row_data = (hidden_cls, grad_inner, active_cls, grad_ffn)
    return (grads, grad_tokens.reshape(batch_size, seq_len, feature), row_data)


def shards(
    query_tokens,
    passage_tokens,
    lengths,
    labels,
    attn_in,
    attn_out,
    ffn_in,
    ffn_out,
    gains,
    biases,
    ffn_bias,
):
    layers = (attn_in, attn_out, ffn_in, ffn_out, gains, biases, ffn_bias)
    query_params = tuple((matrix[0] for matrix in layers))
    passage_params = tuple((matrix[1] for matrix in layers))
    query_count, query_len, feature = query_tokens.shape
    passage_len = passage_tokens.shape[1]
    query_segment = jnp.zeros((query_count, query_len), jnp.int32)
    query_starts = jnp.zeros((query_count, 1), jnp.int32)
    ends = jnp.cumsum(lengths, -1)
    passage_starts = ends - lengths
    places = jnp.arange(passage_len, dtype=jnp.int32)
    passage_segment = jnp.sum((places[None, :, None] >= ends[:, None, :]).astype(jnp.int32), -1)
    query_out, query_pick, query_kept = forward(
        query_tokens, query_segment, query_starts, query_params
    )
    passage_out, passage_pick, passage_kept = forward(
        passage_tokens, passage_segment, passage_starts, passage_params
    )
    query_vec = query_out[query_pick]
    passage_vec = passage_out[passage_pick]
    passage_count = passage_vec.shape[0]
    float_labels = labels.astype(jnp.float32)
    group_vec = lax.all_gather(passage_vec, "grp", axis=0, tiled=True)
    portion = lax.all_gather(group_vec, "blk", axis=0, tiled=True)
    running_max = jnp.full((query_count,), -1e30, jnp.float32)
    score_block = SCORE_SCALE * jnp.dot(query_vec, portion.T, preferred_element_type=jnp.float32)
    column_ids = jnp.arange(portion.shape[0], dtype=jnp.int32)
    new_max = jnp.maximum(running_max, jnp.max(score_block, -1))
    running_sum = jnp.sum(jnp.exp(score_block - new_max[:, None]), -1)
    hits = column_ids[None, :] == labels[:, None]
    positive = jnp.sum(jnp.where(hits, score_block, 0.0), -1)
    running_max, running_sum, positive = (new_max, running_sum, positive)
    norm_log = running_max + jnp.log(running_sum)
    portion = lax.all_gather(group_vec, "blk", axis=0, tiled=True)
    score_block = SCORE_SCALE * jnp.dot(query_vec, portion.T, preferred_element_type=jnp.float32)
    column_ids = jnp.arange(portion.shape[0], dtype=jnp.int32)
    hits = (column_ids[None, :] == labels[:, None]).astype(jnp.float32)
    grad_block = (jnp.exp(score_block - norm_log[:, None]) - hits).astype(jnp.bfloat16)
    query_up = SCORE_SCALE * jnp.dot(grad_block, portion, preferred_element_type=jnp.float32)
    own_ids = (
        lax.axis_index(("blk", "grp")) * passage_count + jnp.arange(passage_count, dtype=jnp.int32)
    ).astype(jnp.float32)
    remote_vec = lax.all_gather(query_vec.astype(jnp.float32), ("blk", "grp"), axis=0, tiled=True)
    remote_log = lax.all_gather(norm_log, ("blk", "grp"), axis=0, tiled=True)
    remote_label = lax.all_gather(float_labels, ("blk", "grp"), axis=0, tiled=True)
    remote_low = remote_vec.astype(jnp.bfloat16)
    score_block = SCORE_SCALE * jnp.dot(
        remote_low, passage_vec.T, preferred_element_type=jnp.float32
    )
    hits = (remote_label[:, None] == own_ids[None, :]).astype(jnp.float32)
    grad_block = (jnp.exp(score_block - remote_log[:, None]) - hits).astype(jnp.bfloat16)
    passage_up = SCORE_SCALE * jnp.dot(grad_block.T, remote_low, preferred_element_type=jnp.float32)
    query_losses = norm_log - positive
    query_grads, query_back, query_rows = backward(
        query_kept, query_segment, query_starts, query_params, query_up
    )
    passage_grads, passage_back, passage_rows = backward(
        passage_kept, passage_segment, passage_starts, passage_params, passage_up
    )
    stacked = tuple(
        (
            jnp.stack([first_part, second_part])
            for first_part, second_part in zip(query_grads, passage_grads)
        )
    )
    grad_win, grad_wout, grad_up, grad_down, grad_gain, grad_bias, grad_hidden_bias = stacked
    shares = (
        lax.psum_scatter(
            grad_win.astype(jnp.bfloat16), "blk", scatter_dimension=1, tiled=True
        ).astype(jnp.float32),
        lax.psum_scatter(
            grad_wout.astype(jnp.bfloat16), "blk", scatter_dimension=1, tiled=True
        ).astype(jnp.float32),
        lax.psum_scatter(
            grad_up.astype(jnp.bfloat16), "blk", scatter_dimension=1, tiled=True
        ).astype(jnp.float32),
        lax.psum_scatter(
            grad_down.astype(jnp.bfloat16), "blk", scatter_dimension=1, tiled=True
        ).astype(jnp.float32),
        lax.psum_scatter(
            grad_gain.astype(jnp.bfloat16), "blk", scatter_dimension=2, tiled=True
        ).astype(jnp.float32),
        lax.psum_scatter(
            grad_bias.astype(jnp.bfloat16), "blk", scatter_dimension=2, tiled=True
        ).astype(jnp.float32),
        lax.psum_scatter(
            grad_hidden_bias.astype(jnp.bfloat16), "blk", scatter_dimension=1, tiled=True
        ).astype(jnp.float32),
    )
    grad_win, grad_wout, grad_up, grad_down, grad_gain, grad_bias, grad_hidden_bias = (
        lax.psum(shares[0].astype(jnp.bfloat16), "grp").astype(jnp.float32),
        lax.psum(shares[1].astype(jnp.bfloat16), "grp").astype(jnp.float32),
        lax.psum(shares[2].astype(jnp.bfloat16), "grp").astype(jnp.float32),
        lax.psum(shares[3].astype(jnp.bfloat16), "grp").astype(jnp.float32),
        lax.psum(shares[4].astype(jnp.bfloat16), "grp").astype(jnp.float32),
        lax.psum(shares[5].astype(jnp.bfloat16), "grp").astype(jnp.float32),
        lax.psum(shares[6].astype(jnp.bfloat16), "grp").astype(jnp.float32),
    )
    query_shaped = query_out.reshape(query_count, query_len, feature)
    passage_shaped = passage_out.reshape(passage_tokens.shape)
    return (
        query_losses,
        query_shaped,
        passage_shaped,
        query_back,
        passage_back,
        grad_win,
        grad_wout,
        grad_up,
        grad_down,
        grad_gain,
        grad_bias,
        grad_hidden_bias,
    )


def solution(mesh):
    placed = (
        P(("blk", "grp"), None, None),
        P(("blk", "grp"), None, None),
        P(("blk", "grp"), None),
        P(("blk", "grp")),
        P(),
        P(),
        P(),
        P(),
        P(),
        P(),
        P(),
    )
    small = dict(mesh.shape) == {"blk": 16, "grp": 2}
    return jax.shard_map(
        fast_shards if small else shards,
        mesh=mesh,
        in_specs=placed,
        out_specs=(
            P(("blk", "grp")),
            P(("blk", "grp"), None, None),
            P(("blk", "grp"), None, None),
            P(("blk", "grp"), None, None),
            P(("blk", "grp"), None, None),
            P(None, "blk", None),
            P(None, "blk", None),
            P(None, "blk", None),
            P(None, "blk", None),
            P(None, None, "blk"),
            P(None, None, "blk"),
            P(None, "blk"),
        ),
        check_vma=False,
    )
```

```python
import functools
import jax
import jax.numpy as jnp
from jax import lax
from jax.experimental import pallas as pl
from jax.experimental.pallas import tpu as pltpu
from jax.sharding import PartitionSpec as P

MESH = pl.DeviceIdType.MESH
HEAD_DIM = 64
HEADS = 12
EPSILON = 1e-05
SCORE_SCALE = 0.08
KEY_SCALE = 0.125
NEG = -1000000000.0
F32 = jnp.float32
BF16 = jnp.bfloat16
VMEM_LIMIT = 60 * 1024 * 1024


def dot(a, b):
    return lax.dot_general(a, b, (((1,), (0,)), ((), ())), preferred_element_type=F32)


def dot_nt(a, b):
    return lax.dot_general(a, b, (((1,), (1,)), ((), ())), preferred_element_type=F32)


def dot_tn(a, b):
    return lax.dot_general(a, b, (((0,), (0,)), ((), ())), preferred_element_type=F32)


def iota(shape, dim):
    return lax.broadcasted_iota(jnp.int32, shape, dim)


def head_row(h):
    return iota((1, 768), 1) // HEAD_DIM == h


def expand_heads(rows, h0=0, heads=HEADS):
    return jnp.concatenate(
        [jnp.where(head_row(h0 + h), rows, 0.0) for h in range(heads)], 0
    )


def fold_heads(rows, count, h0=0, heads=HEADS):
    out = jnp.where(head_row(h0), rows[:count], 0.0)
    for h in range(1, heads):
        out = out + jnp.where(head_row(h0 + h), rows[h * count:(h + 1) * count], 0.0)
    return out


def norm_stats(residual):
    centre = residual - jnp.mean(residual, -1, keepdims=True)
    inverse = lax.rsqrt(jnp.mean(centre * centre, -1, keepdims=True) + EPSILON)
    return centre * inverse, inverse


def gelu(v):
    return 0.5 * v * (1.0 + jnp.tanh(0.7978845608028654 * (v + 0.044715 * (v * v * v))))


def split3(v):
    hi = v.astype(BF16).astype(F32)
    rest = v - hi
    mid = rest.astype(BF16).astype(F32)
    return hi, mid, rest - mid


def lane_pack(columns, count):
    lane = iota((count, 128), 1)
    out = jnp.zeros((count, 128), F32)
    for j, column in enumerate(columns):
        out = jnp.where(lane == j, column, out)
    return out


def norm_back(up, gain, normed, inverse):
    u = up * gain
    return inverse * (
        u - jnp.mean(u, -1, keepdims=True) - normed * jnp.mean(u * normed, -1, keepdims=True)
    )


def gelu_pair(v):
    sq = v * v
    th = jnp.tanh(0.7978845608028654 * (v + 0.044715 * (v * sq)))
    half = 0.5 * (1.0 + th)
    slope = half + 0.5 * v * (1.0 - th * th) * (0.7978845608028654 * (1.0 + 0.134145 * sq))
    return v * half, slope


def decode_inv(ext):
    return ext[:, 0:1] + ext[:, 1:2] + ext[:, 2:3], ext[:, 3:4] + ext[:, 4:5] + ext[:, 5:6]


def ext_rows(block):
    e_p = block[:, :, 0:128].reshape(128, 128)
    e_q = jnp.concatenate([block[:, :, 128 * a:128 * a + 128] for a in range(1, 5)], 1)
    return e_p, e_q.reshape(512, 128)


def place():
    return lax.axis_index("blk"), lax.axis_index("grp")


def remote(src, dst, send, recv, peer):
    return pltpu.make_async_remote_copy(
        src_ref=src, dst_ref=dst, send_sem=send, recv_sem=recv, device_id=peer, device_id_type=MESH
    )


def greet(me, g):
    barrier = pltpu.get_barrier_semaphore()
    for i in range(1, 16):
        pl.semaphore_signal(barrier, inc=1, device_id=(lax.rem(me + i, 16), g), device_id_type=MESH)
    pl.semaphore_signal(barrier, inc=1, device_id=(me, 1 - g), device_id_type=MESH)


def greeted():
    pl.semaphore_wait(pltpu.get_barrier_semaphore(), 16)


def gather_phases(me, g, pay, ga, ss, rs, base, lo, hi):
    z, yx = me // 4, lax.rem(me, 4)
    xpeer = me + 1 - 2 * lax.rem(me, 2)
    ypeer = me + 2 - 4 * (lax.rem(me, 4) // 2)
    yx_x, yx_y = lax.rem(xpeer, 4), lax.rem(ypeer, 4)
    rows = slice(lo, hi)
    first, second, third = [], [], []

    def add(phase, src, dst, k, peer):
        phase.append(remote(src, dst, ss.at[base + k], rs.at[base + k], (peer, g)))

    for d in range(1, 4):
        peer = lax.rem(z + d, 4) * 4 + yx
        add(first, pay.at[rows], ga.at[z, yx, rows], d - 1, peer)
    add(second, ga.at[:, yx, rows], ga.at[:, yx, rows], 3, xpeer)
    add(second, ga.at[:, yx, rows], ga.at[:, yx, rows], 4, ypeer)
    add(third, ga.at[0:2, yx_x, rows], ga.at[0:2, yx_x, rows], 5, ypeer)
    add(third, ga.at[2:4, yx_y, rows], ga.at[2:4, yx_y, rows], 6, xpeer)
    return first, second, third


QR, PR = 512, 128


def forward_kernel(
    lens_ref, labels_ref, gains_ref, biases_ref, ffnb_ref,
    xq_hbm, xp_hbm, win_hbm, wout_hbm, fin_hbm, fout_hbm,
    out_hbm, uw_hbm, dspq_hbm, dspp_hbm,
    pwin_hbm, pwout_hbm, pfin_hbm, pfout_hbm, psum_hbm, pffb_hbm,
    swin_hbm, swout_hbm, sfin_hbm, sfout_hbm, ssum_hbm, sffb_hbm,
    loss_ref, ext_ref,
    x_s, q_s, kv_s, win_s, wout_s, fin_s, fout_s, pq_s, pp_s, out_s, mix_s, bias_s,
    pay_s, swap_s, ga_ref, gs_ref, rsw_ref, innq_ref, innp_ref, invq_ref, invp_ref, qq_ref, zq_ref,
    grad_s, pv_s, upp_s, gq_s, rgq_s, yt_s, ryt_s, sib_s, r1_s, s2_s, r2_s,
    pwin_s, pwout_s, pfin_s, psum_s, pffb_s, acc_s,
    sem, lsem, osem, ss, rs, as_, ar, xs, xr, ks, kr, psem,
):
    me, g = place()
    z, yx = me // 4, lax.rem(me, 4)
    greet(me, g)
    copies = []
    for t, x_hbm in enumerate((xq_hbm, xp_hbm)):
        copies.append([
            pltpu.make_async_copy(x_hbm, x_s.at[t], sem.at[t, 0]),
            pltpu.make_async_copy(win_hbm.at[t], win_s.at[t], sem.at[t, 1]),
            pltpu.make_async_copy(wout_hbm.at[t], wout_s.at[t], sem.at[t, 2]),
            pltpu.make_async_copy(fin_hbm.at[t], fin_s.at[t], sem.at[t, 3]),
            pltpu.make_async_copy(fout_hbm.at[t], fout_s.at[t], sem.at[t, 4]),
        ])
    for c in copies[0][:2] + copies[1][:2] + copies[0][2:] + copies[1][2:]:
        c.start()
    a1, b1, c1 = gather_phases(me, g, pay_s, ga_ref, ss, rs, 0, 0, 64)
    a2, b2, c2 = gather_phases(me, g, pay_s, ga_ref, ss, rs, 7, 64, 96)
    last_hop = [remote(ga_ref.at[:, :, 0:64], gs_ref, ss.at[14], rs.at[14], (me, 1 - g))]
    swaps = []
    for i in range(1, 16):
        peer = lax.rem(me + i, 16)
        swaps.append(remote(swap_s.at[peer], rsw_ref.at[me], as_.at[i], ar.at[i], (peer, g)))
    own_copy = [
        pltpu.make_async_copy(pay_s, ga_ref.at[z, yx], lsem.at[0]),
        pltpu.make_async_copy(swap_s.at[me], rsw_ref.at[me], lsem.at[1]),
    ]

    tokens = x_s.shape[1]
    col_q = iota((32, tokens), 1)
    row_q = iota((32, tokens), 0)
    sel_q = col_q == row_q * 32
    own_q = col_q // 32 == row_q
    col_p = iota((8, tokens), 1)
    row_p = iota((8, tokens), 0)
    lo = jnp.zeros((8, tokens), jnp.int32)
    hi = jnp.zeros((8, tokens), jnp.int32)
    for r in range(2):
        acc = jnp.int32(r * 512)
        for c in range(4):
            length = lens_ref[r, c]
            lo = jnp.where(row_p == r * 4 + c, acc, lo)
            acc = acc + length
            hi = jnp.where(row_p == r * 4 + c, acc, hi)
    sel_p = col_p == lo
    own_p = (col_p >= lo) & (col_p < hi)

    picks = []
    for t, sel in enumerate((sel_q, sel_p)):
        copies[t][0].wait()
        copies[t][1].wait()
        query_bias = biases_ref[0, t:t + 1, :]
        value_bias = biases_ref[1, t:t + 1, :]

        def kv_step(m, _, t=t, query_bias=query_bias, value_bias=value_bias):
            rows = pl.ds(pl.multiple_of(m * 256, 256), 256)
            x = x_s[t, rows, :]
            kv_s[t, rows, 0:768] = dot(x, win_s[t, :, 768:1536]).astype(BF16)
            kv_s[t, rows, 768:1536] = (dot(x, win_s[t, :, 1536:2304]) + value_bias).astype(BF16)
            q_s[t, rows, :] = (dot(x, win_s[t, :, 0:768]) + query_bias).astype(BF16)
            return 0

        lax.fori_loop(0, tokens // 256, kv_step, 0)
        pick = jnp.where(sel, 1.0, 0.0).astype(BF16)
        picks.append((dot(pick, x_s[t]), dot(pick, q_s[t])))

    done = []
    for t, (own, count, p_s, inn_ref, inv_ref) in enumerate((
        (own_q, 32, pq_s, innq_ref, invq_ref), (own_p, 8, pp_s, innp_ref, invp_ref),
    )):
        xc, qc = picks[t]
        mixed = jnp.zeros((count, 768), F32)
        heads = 4 if t == 0 else HEADS
        mask = jnp.concatenate([jnp.where(own, 0.0, NEG)] * heads, 0)
        for h0 in range(0, HEADS, heads):
            span = slice(h0 * count, (h0 + heads) * count)
            spread = expand_heads(qc, h0, heads).astype(BF16)
            scores = dot_nt(spread, kv_s[t, :, 0:768]) * KEY_SCALE + mask
            weight = jnp.exp(scores - jnp.max(scores, -1, keepdims=True))
            soft = weight * (1.0 / jnp.sum(weight, -1, keepdims=True))
            p_s[span, :] = soft
            soft16 = soft.astype(BF16)
            mixed = mixed + fold_heads(dot(soft16, kv_s[t, :, 768:1536]), count, h0, heads)
            zsum = dot(soft16, x_s[t])
            if t == 0:
                zq_ref[span, :] = zsum.astype(BF16)
            else:
                wide = jnp.concatenate([zsum, jnp.zeros((32, 768), F32)], 0)
                swap_s[:, 48:96, :] = wide.T.astype(BF16).reshape(16, 48, 128)
        mixed = mixed.astype(BF16)
        copies[t][2].wait()
        first = xc + (dot(mixed, wout_s[t]) + biases_ref[2, t:t + 1, :])
        n1, inv1 = norm_stats(first)
        hidden = (n1 * gains_ref[t, 0:1, :] + biases_ref[3, t:t + 1, :]).astype(BF16)
        copies[t][3].wait()
        inner = dot(hidden, fin_s[t]) + ffnb_ref[t:t + 1, :]
        inn_ref[...] = inner
        active = gelu(inner).astype(BF16)
        copies[t][4].wait()
        second = hidden.astype(F32) + (dot(active, fout_s[t]) + biases_ref[4, t:t + 1, :])
        n2, inv2 = norm_stats(second)
        vec = (n2 * gains_ref[t, 1:2, :] + biases_ref[5, t:t + 1, :]).astype(BF16)
        inv_ref[...] = lane_pack([inv1, inv2], count)
        done.append((xc, qc, mixed, hidden, vec, inv1, inv2))

    xq, qq, mq, hq, vq, i1q, i2q = done[0]
    xp, qp, mp, hp, vp, i1p, i2p = done[1]
    lab = labels_ref[...].astype(F32)
    eye = iota((32, 32), 0) == iota((32, 32), 1)
    lab_col = jnp.sum(jnp.where(eye, lab, 0.0), 1, keepdims=True)
    lab_hi = jnp.floor(lab_col * (1.0 / 256.0))
    lab_lo = lab_col - 256.0 * lab_hi
    ext_q = lane_pack([*split3(i1q), *split3(i2q), lab_hi, lab_lo], 32)
    ext_p = lane_pack([*split3(i1p), *split3(i2p)], 8)
    ext = jnp.concatenate(
        [ext_p] + [ext_q[8 * a:8 * a + 8] for a in range(4)] + [jnp.zeros((8, 128), F32)], 1
    )
    pay_s[0:32, :] = vq
    pay_s[32:64, :] = jnp.concatenate([hp.astype(F32), vp.astype(F32), qp, ext], 0).astype(BF16)
    pay_s[64:96, :] = hq
    qq_ref[...] = qq.astype(BF16)
    greeted()
    own_copy[0].start()
    for c in a1 + a2:
        c.start()
    m48 = jnp.concatenate([mq.astype(F32), mp.astype(F32), jnp.zeros((8, 768), F32)], 0)
    x48 = jnp.concatenate([xq, xp, jnp.zeros((8, 768), F32)], 0)
    swap_s[:, 0:48, :] = jnp.zeros((16, 48, 128), BF16)
    for b in range(16):
        swap_s[b, 0:48, 0:48] = m48[:, 48 * b:48 * b + 48].astype(BF16)
        swap_s[b, 0:48, 64:112] = x48[:, 48 * b:48 * b + 48].astype(BF16)
    for c in own_copy[1:]:
        c.start()

    low_half = iota((1, 128), 1) < HEAD_DIM

    def tile(step, _):
        tower = step // 4
        rows = pl.ds(pl.multiple_of(lax.rem(step, 4) * 256, 256), 256)

        def on(k, waits, starts):
            @pl.when(step == k)
            def _():
                for c in waits:
                    c.wait()
                for c in starts:
                    c.start()

        on(2, own_copy[0:1] + a1, b1)
        on(3, a2, b2)
        on(4, b1, c1 + swaps)
        on(5, b2, c2)
        on(6, c1, last_hop)

        @pl.when(step < 4)
        def _():
            same = iota((128, 128), 0) // 32 == iota((128, 128), 1) // 32
            mask = jnp.where(same, 0.0, NEG)
            mask2 = jnp.concatenate([mask, mask], 0)
            for part in range(2):
                at = pl.ds(pl.multiple_of(lax.rem(step, 4) * 256 + part * 128, 128), 128)
                for j in range(HEADS // 2):
                    lanes = slice(128 * j, 128 * j + 128)
                    q = q_s[0, at, lanes]
                    k = kv_s[0, at, lanes]
                    v = kv_s[0, at, 768 + 128 * j:768 + 128 * j + 128]
                    zero = jnp.zeros_like(q)
                    q2 = jnp.concatenate([jnp.where(low_half, q, zero), jnp.where(low_half, zero, q)], 0)
                    s = dot_nt(q2, k) * KEY_SCALE + mask2
                    e = jnp.exp(s - jnp.max(s, -1, keepdims=True))
                    total = jnp.sum(e, -1, keepdims=True)
                    o = dot(e.astype(BF16), v) * (1.0 / total)
                    mix_s[part * 128:part * 128 + 128, lanes] = jnp.where(low_half, o[:128], o[128:]).astype(BF16)

        @pl.when(step >= 4)
        def _():
            row = (step - 4) // 2
            base = lax.rem(step, 2) * 256
            keys = pl.ds(pl.multiple_of(row * 512, 512), 512)
            qpos = iota((256, 512), 0) + base
            kpos = iota((256, 512), 1)
            qseg = jnp.zeros((256, 512), jnp.int32)
            kseg = jnp.zeros((256, 512), jnp.int32)
            end = jnp.int32(0)
            for c in range(3):
                end = end + lens_ref[row, c]
                qseg = qseg + jnp.where(qpos >= end, 1, 0)
                kseg = kseg + jnp.where(kpos >= end, 1, 0)
            mask = jnp.where(qseg == kseg, 0.0, NEG)
            bias_s[...] = mask
            def heads(i, _):
                for j in range(2):
                    lanes = pl.ds(pl.multiple_of(256 * i + 128 * j, 128), 128)
                    q = q_s[1, rows, lanes]
                    k = kv_s[1, keys, lanes]
                    v = kv_s[1, keys, pl.ds(pl.multiple_of(768 + 256 * i + 128 * j, 128), 128)]
                    zero = jnp.zeros_like(q)
                    halves = []
                    for part in (jnp.where(low_half, q, zero), jnp.where(low_half, zero, q)):
                        s = dot_nt(part, k) * KEY_SCALE + bias_s[...]
                        e = jnp.exp(s - jnp.max(s, -1, keepdims=True))
                        total = jnp.sum(e, -1, keepdims=True)
                        halves.append(dot(e.astype(BF16), v) * (1.0 / total))
                    mix_s[:, lanes] = jnp.where(low_half, halves[0], halves[1]).astype(BF16)
                return 0

            lax.fori_loop(0, 3, heads, 0)

        first_sum = x_s[tower, rows, :].astype(F32) + (
            dot(mix_s[...], wout_s[tower]) + biases_ref[2, pl.ds(tower, 1), :]
        )
        n1, _ = norm_stats(first_sum)
        hidden = (n1 * gains_ref[tower, 0:1, :] + biases_ref[3, pl.ds(tower, 1), :]).astype(BF16)
        second_sum = hidden.astype(F32) + biases_ref[4, pl.ds(tower, 1), :]
        for c in range(4):
            cols = slice(768 * c, 768 * c + 768)
            inner = dot(hidden, fin_s[tower, :, cols]) + ffnb_ref[pl.ds(tower, 1), cols]
            second_sum = second_sum + dot(gelu(inner).astype(BF16), fout_s[tower, cols, :])
        n2, _ = norm_stats(second_sum)
        slot = lax.rem(step, 2)

        @pl.when(step >= 2)
        def _():
            pltpu.make_async_copy(out_s.at[slot], out_hbm.at[tower, rows], osem.at[slot]).wait()

        out_s[slot] = (
            n2 * gains_ref[tower, 1:2, :] + biases_ref[5, pl.ds(tower, 1), :]
        ).astype(BF16)
        pltpu.make_async_copy(out_s.at[slot], out_hbm.at[tower, rows], osem.at[slot]).start()
        return 0

    lax.fori_loop(0, 8, tile, 0)
    for c in c2 + last_hop + swaps + own_copy[1:]:
        c.wait()
    for i in range(2):
        pltpu.make_async_copy(out_s.at[i], out_hbm.at[1, 0:256], osem.at[i]).wait()
    ga = ga_ref.reshape(16, 96, 768)
    gs = gs_ref.reshape(16, 64, 768)

    save_dsp = [
        pltpu.make_async_copy(kv_s.at[0, 0:768, 0:tokens], dspq_hbm, osem.at[5]),
        pltpu.make_async_copy(kv_s.at[1, 0:192, 0:tokens], dspp_hbm, osem.at[6]),
    ]
    save_uw = pltpu.make_async_copy(x_s.at[0, 0:960], uw_hbm, osem.at[4])

    pv_own = ga[:, 32:48].astype(F32)[:, 8:16].reshape(128, 768)
    pv_sib = gs[:, 32:48].astype(F32)[:, 8:16].reshape(128, 768)
    pv = jnp.concatenate([pv_own, pv_sib], 0).astype(BF16)
    col = iota((1, 256), 1)
    within = lax.rem(col, 128)
    side = jnp.where(col < 128, g, 1 - g)
    ids = (within // 8) * 16 + side * 8 + lax.rem(within, 8)
    for half, src in enumerate((ga, gs)):
        _, eq = ext_rows(src[:, 48:64].astype(F32)[:, 8:16])
        label = (eq[:, 6:7] * 256.0 + eq[:, 7:8]).astype(jnp.int32)
        logits = SCORE_SCALE * dot_nt(src[:, 0:32].reshape(512, 768), pv)
        top = jnp.max(logits, -1, keepdims=True)
        norm_log = top + jnp.log(jnp.sum(jnp.exp(logits - top), -1, keepdims=True))
        hit = label == ids
        grad = (jnp.exp(logits - norm_log) - jnp.where(hit, 1.0, 0.0)).astype(BF16)
        part = SCORE_SCALE * dot_tn(grad[:, 0:128], src[:, 0:32].reshape(512, 768))
        if half == 0:
            positive = jnp.sum(jnp.where(hit, logits, 0.0), -1, keepdims=True)
            loss = jnp.where(iota((512, 1), 0) // 32 == me, norm_log - positive, 0.0)
            diagonal = lax.rem(iota((512, 32), 0), 32) == iota((512, 32), 1)
            loss_ref[...] = jnp.sum(jnp.where(diagonal, loss, 0.0), 0, keepdims=True)
            grad_s[...] = grad
            upp_s[...] = part
        else:
            upp_s[...] += part
    pv_s[...] = pv

    def query_up(rows):
        return SCORE_SCALE * dot(grad_s[rows, :], pv_s[...])

    mine = ga[me]
    low = mine[32:64].astype(F32)
    gq_rows, keep = [], []
    for t, (count, up, hidden, vec, q, inn_ref, inv_ref, p_s) in enumerate((
        (32, query_up(pl.ds(pl.multiple_of(me * 32, 32), 32)), mine[64:96].astype(F32),
         mine[0:32].astype(F32), qq_ref[...].astype(F32), innq_ref, invq_ref, pq_s),
        (8, upp_s[pl.ds(pl.multiple_of(me * 8, 8), 8), :], low[0:8], low[8:16], low[16:24],
         innp_ref, invp_ref, pp_s),
    )):
        g0, g1 = gains_ref[t, 0:1, :], gains_ref[t, 1:2, :]
        n2 = (vec - biases_ref[5, t:t + 1, :]) / g1
        n1 = (hidden - biases_ref[3, t:t + 1, :]) / g0
        grad_second = norm_back(up, g1, n2, inv_ref[:, 1:2])
        grad_ffn = grad_second.astype(BF16)
        grad_active = dot_nt(grad_ffn, fout_s[t])
        _, slope = gelu_pair(inn_ref[...])
        grad_inner = (grad_active * slope).astype(BF16)
        grad_hidden = grad_second + dot_nt(grad_inner, fin_s[t])
        grad_first = norm_back(grad_hidden, g0, n1, inv_ref[:, 0:1])
        gm = dot_nt(grad_first.astype(BF16), wout_s[t]).astype(BF16)
        n = HEADS * count
        heads = 4 if t == 0 else HEADS
        gq = jnp.zeros((count, 768), F32)
        slopes = []
        rows_y = out_s.reshape(512, 768)
        for h0 in range(0, HEADS, heads):
            span = slice(h0 * count, (h0 + heads) * count)
            wide = expand_heads(gm.astype(F32), h0, heads).astype(BF16)
            dp = dot_nt(wide, kv_s[t, :, 768:1536])
            soft = p_s[span, :]
            ds = (soft * (dp - jnp.sum(soft * dp, -1, keepdims=True))).astype(BF16)
            slopes.append(ds)
            gq = gq + fold_heads(dot(ds, kv_s[t, :, 0:768]), count, h0, heads)
            y = dot(ds, x_s[t]) * KEY_SCALE
            if t == 0:
                rows_y[span, :] = y.astype(BF16)
            else:
                yt_s[...] = jnp.concatenate(
                    [y, jnp.zeros((32, 768), F32)], 0
                ).T.astype(BF16).reshape(16, 48, 128)
        gq = gq * KEY_SCALE
        gq_rows.append(gq)
        wide = expand_heads(gm.astype(F32)).astype(BF16)
        spread = expand_heads(q).astype(BF16)
        if t == 0:
            for lo in range(0, 768, 256):
                q_s[0, lo:lo + 256, :] = dot_tn(rows_y[0:384, lo:lo + 256], spread).astype(BF16)
            for lo in range(0, 768, 256):
                q_s[1, lo:lo + 256, :] = dot_tn(zq_ref[:, lo:lo + 256], wide).astype(BF16)
        for i, ds in enumerate(slopes):
            span = slice(i * heads * count, (i + 1) * heads * count)
            kv_s[t, span, 0:tokens] = ds
        kv_s[t, n:2 * n, 0:tokens] = p_s[...].astype(BF16)
        save_dsp[t].start()
        at = 768 * t
        for lo in range(0, n, 128):
            hi = min(lo + 128, n)
            u = dot_nt(spread[lo:hi], win_s[t, :, 768:1536]) * KEY_SCALE
            x_s[0, at + lo:at + hi, :] = u.astype(BF16)
            x_s[0, at + n + lo:at + n + hi, :] = dot_nt(wide[lo:hi], win_s[t, :, 1536:2304]).astype(BF16)
        extra = dot_nt(gq.astype(BF16), win_s[t, :, 0:768]) + grad_first
        ext_ref[32 * t:32 * t + count, :] = extra
    gq_s[...] = jnp.concatenate(gq_rows + [jnp.zeros((8, 768), F32)], 0).astype(BF16)
    save_uw.start()
    for c in save_dsp:
        c.wait()

    first, second, third = gather_phases(me, g, gq_s, rgq_s, ss, rs, 15, 0, 48)
    rows_swap = []
    for i in range(1, 16):
        peer = lax.rem(me + i, 16)
        rows_swap.append(remote(yt_s.at[peer], ryt_s.at[me], as_.at[16 + i], ar.at[16 + i], (peer, g)))
    own = [
        pltpu.make_async_copy(gq_s, rgq_s.at[z, yx], lsem.at[2]),
        pltpu.make_async_copy(yt_s.at[me], ryt_s.at[me], lsem.at[3]),
    ]
    sib = (me, 1 - g)
    pair = [remote(q_s.at[1 - g, 0:768], sib_s, ks.at[0], kr.at[0], sib)]
    xpeer = me + 1 - 2 * lax.rem(me, 2)
    ypeer = me + 2 - 4 * (lax.rem(me, 4) // 2)
    dpeer = xpeer + 2 - 4 * (lax.rem(xpeer, 4) // 2)
    plane = []
    for k, peer in enumerate((dpeer, xpeer, ypeer)):
        for zz in range(4):
            at = pl.multiple_of(48 * (4 * zz + lax.rem(peer, 4)), 16)
            n = 1 + 4 * k + zz
            plane.append(remote(
                q_s.at[g, pl.ds(at, 48)], r1_s.at[k, zz], ks.at[n], kr.at[n], (peer, g)
            ))
    column = [
        remote(s2_s.at[lax.rem(z + d, 4)], r2_s.at[d - 1], ks.at[12 + d], kr.at[12 + d],
               (lax.rem(z + d, 4) * 4 + yx, g))
        for d in range(1, 4)
    ]

    def add_pair():
        def one(i, _):
            at = pl.ds(pl.multiple_of(48 * i, 16), 48)
            q_s[g, at, :] = (q_s[g, at, :].astype(F32) + sib_s[at, :].astype(F32)).astype(BF16)
            return 0

        lax.fori_loop(0, 16, one, 0)

    def add_plane():
        def one(i, _):
            at = pl.ds(pl.multiple_of(48 * (4 * i + yx), 16), 48)
            s2_s[i] = (
                q_s[g, at, :].astype(F32) + r1_s[0, i].astype(F32)
                + r1_s[1, i].astype(F32) + r1_s[2, i].astype(F32)
            ).astype(BF16)
            return 0

        lax.fori_loop(0, 4, one, 0)

    shares = [(pwout_s, pwout_hbm, swout_hbm), (pfin_s, pfin_hbm, sfin_hbm), (pffb_s, pffb_hbm, sffb_hbm)]
    shares += [
        (pq_s.at[192 * t:192 * t + 192, 0:768], pfout_hbm.at[t], sfout_hbm.at[t]) for t in range(2)
    ]
    shares += [(pwin_s, pwin_hbm, swin_hbm), (psum_s, psum_hbm, ssum_hbm)]
    sends = [remote(a, c, xs.at[n], xr.at[n], sib) for n, (a, b, c) in enumerate(shares)]
    saves = [pltpu.make_async_copy(a, b, psem.at[n]) for n, (a, b, c) in enumerate(shares)]
    early, late = sends[:5] + saves[:5], sends[5:] + saves[5:]
    for c in own + pair + first + rows_swap:
        c.start()

    ext = ga[:, 48:64].astype(F32)[:, 8:16]
    ext_p, ext_q = ext_rows(ext)
    psum_s[...] = jnp.zeros(psum_s.shape, F32)
    pffb_s[...] = jnp.zeros(pffb_s.shape, F32)

    def chain(t, up, hidden, vec, inv1, inv2, rows, count):
        g0, g1 = gains_ref[t, 0:1, :], gains_ref[t, 1:2, :]
        total = lambda v: jnp.sum(v, 0, keepdims=True)
        n2 = (vec.astype(F32) - biases_ref[5, t:t + 1, :]) / g1
        grad_second = norm_back(up, g1, n2, inv2)
        grad_ffn = grad_second.astype(BF16)
        x_s[1, rows, :] = grad_ffn
        psum_s[t, 1:2, :] += total(up * n2)
        psum_s[t, 6:7, :] += total(grad_ffn.astype(F32))
        psum_s[t, 7:8, :] += total(up)
        grad_hidden = grad_second
        for c in range(4):
            cols = slice(768 * c, 768 * c + 768)
            inner = dot(hidden, fin_s[t, :, cols]) + ffnb_ref[t:t + 1, cols]
            active, slope = gelu_pair(inner)
            half = slice(768 * (c % 2), 768 * (c % 2) + 768)

            @pl.when(me // 4 == c)
            def _(active=active):
                win_s[0, rows, 1536:2304] = active.astype(BF16)

            grad_inner = (dot_nt(grad_ffn, fout_s[t, cols, :]) * slope).astype(BF16)
            kv_s[c // 2, rows, half] = grad_inner
            pffb_s[t:t + 1, cols] += jnp.sum(grad_inner.astype(F32), 0, keepdims=True)
            grad_hidden = grad_hidden + dot_nt(grad_inner, fin_s[t, :, cols])
        n1 = (hidden.astype(F32) - biases_ref[3, t:t + 1, :]) / g0
        psum_s[t, 0:1, :] += total(grad_hidden * n1)
        psum_s[t, 5:6, :] += total(grad_hidden)
        grad_attn = norm_back(grad_hidden, g0, n1, inv1).astype(BF16)
        win_s[0, rows, 0:768] = grad_attn
        psum_s[t, 4:5, :] += total(grad_attn.astype(F32))
        gm = dot_nt(grad_attn, wout_s[t]).astype(BF16)
        win_s[0, rows, 768:1536] = gm
        psum_s[t, 3:4, :] += total(gm.astype(F32))

    i1q, i2q = decode_inv(ext_q)
    i1p, i2p = decode_inv(ext_p)
    for blk in range(2):
        lo = blk * 256
        chain(
            0, query_up(slice(lo, lo + 256)),
            ga[8 * blk:8 * blk + 8, 64:96].reshape(256, 768),
            ga[8 * blk:8 * blk + 8, 0:32].reshape(256, 768),
            i1q[lo:lo + 256], i2q[lo:lo + 256], slice(lo, lo + 256), 256,
        )
        if blk == 0:
            for c in pair:
                c.wait()
            add_pair()
            for c in plane:
                c.start()
            own[0].wait()
            for c in first:
                c.wait()
            for c in second:
                c.start()
    hv = ga[:, 32:48].astype(F32)
    chain(
        1, upp_s[...], hv[:, 0:8].reshape(128, 768).astype(BF16),
        hv[:, 8:16].reshape(128, 768).astype(BF16), i1p, i2p, slice(QR, QR + PR), 128,
    )
    for c in plane:
        c.wait()
    add_plane()
    for c in column:
        c.start()
    for c in second:
        c.wait()
    for c in third:
        c.start()

    for t, rows in enumerate((slice(0, QR), slice(QR, QR + PR))):
        count = rows.stop - rows.start
        fo_at = pl.multiple_of(1536 + lax.rem(me // 2, 2) * 384, 128)
        win_s[1, 0:384, 0:count] = win_s[0, rows, pl.ds(fo_at, 384)].astype(F32).T.astype(BF16)
        fo_row = pl.multiple_of(lax.rem(me, 2) * 192, 16)
        pq_s[192 * t:192 * t + 192, 0:768] = dot(
            win_s[1, pl.ds(fo_row, 192), 0:count], x_s[1, rows, :]
        )
        fi_at = pl.multiple_of((me // 8) * 384, 128)
        if t == 0:
            hid = ga[:, 64:96, pl.ds(fi_at, 384)].reshape(QR, 384)
        else:
            hid = ga[:, 32:48, pl.ds(fi_at, 384)].astype(F32)[:, 0:8].reshape(PR, 384)
        win_s[1, 0:384, 768:768 + count] = hid.astype(F32).T.astype(BF16)
        fi_row = pl.multiple_of(lax.rem(me, 8) * 48, 16)
        lhs = win_s[1, pl.ds(fi_row, 48), 768:768 + count]
        for h in range(2):
            pfin_s[t, :, 1536 * h:1536 * h + 1536] = dot(lhs, kv_s[h, rows, :])
        if t == 0:
            mx = rsw_ref[:, 0:32].reshape(QR, 128)
        else:
            mx = rsw_ref[:, 32:48].astype(F32)[:, 0:8].reshape(PR, 128).astype(BF16)
        pwout_s[t] = dot_tn(mx, win_s[0, rows, 0:768])[0:48]
    for c in early:
        c.start()

    def low_rank(read_t, read_p, out_col):
        acc_s[...] = jnp.zeros(acc_s.shape, F32)

        def source(i, _):
            wide = jnp.concatenate([expand_heads(read_p(i)), jnp.zeros((32, 768), F32)], 0)
            acc_s[...] += dot(read_t(i), wide.astype(BF16))
            return 0

        lax.fori_loop(0, 16, source, 0)
        pwin_s[1, :, out_col:out_col + 768] = acc_s[...]

    def gm_p(i):
        pair = win_s[0, pl.ds(pl.multiple_of(QR + (i // 2) * 16, 16), 16), 768:1536].astype(F32)
        return jnp.where(lax.rem(i, 2) == 0, pair[0:8], pair[8:16])

    low_rank(lambda i: rsw_ref[i, 48:96, :], gm_p, 1536)

    for c in third:
        c.wait()
    for c in rows_swap:
        c.wait()
    own[1].wait()

    def q_p(i):
        return ga[i, 48:64, :].astype(F32)[0:8]

    low_rank(lambda i: ryt_s[i], q_p, 768)
    rg_q = rgq_s[:, :, 0:32].reshape(QR, 768)
    rg_p = rgq_s[:, :, 32:48].astype(F32)[:, :, 0:8].reshape(PR, 768)
    pwin_s[0, :, 0:768] = dot_tn(rsw_ref[:, 0:32].reshape(QR, 128), rg_q)[64:112]
    x_p = rsw_ref[:, 32:48].astype(F32)[:, 0:8].reshape(PR, 128).astype(BF16)
    pwin_s[1, :, 0:768] = dot_tn(x_p, rg_p.astype(BF16))[64:112]
    for c in column:
        c.wait()
    pwin_s[0, :, pl.ds(pl.multiple_of(768 + 768 * g, 128), 768)] = (
        s2_s[z].astype(F32) + r2_s[0].astype(F32) + r2_s[1].astype(F32) + r2_s[2].astype(F32)
    )
    pwin_s[0, :, pl.ds(pl.multiple_of(1536 - 768 * g, 128), 768)] = jnp.zeros((48, 768), F32)
    psum_s[0, 2:3, :] = jnp.sum(rg_q.astype(F32), 0, keepdims=True)
    psum_s[1, 2:3, :] = jnp.sum(rg_p, 0, keepdims=True)
    for c in late:
        c.start()
    for c in early + late:
        c.wait()
    save_uw.wait()


def run_forward(xq, xp, lengths, labels, weights):
    attn_in, attn_out, ffn_in, ffn_out, gains, biases, ffn_bias = weights
    tokens = xq.shape[0]
    vm = pl.BlockSpec(memory_space=pltpu.VMEM)
    hb = pl.BlockSpec(memory_space=pl.ANY)
    sds = jax.ShapeDtypeStruct
    parts = [
        sds((2, 48, 2304), F32), sds((2, 48, 768), F32), sds((2, 48, 3072), F32),
        sds((2, 192, 768), F32), sds((2, 8, 768), F32), sds((2, 3072), F32),
    ]
    return pl.pallas_call(
        forward_kernel,
        out_shape=[
            sds((2, tokens, 768), BF16), sds((960, 768), BF16),
            sds((768, tokens), BF16), sds((192, tokens), BF16),
        ] + parts + parts + [sds((1, 32), F32), sds((40, 768), F32)],
        in_specs=[pl.BlockSpec(memory_space=pltpu.SMEM), vm, vm, vm, vm] + [hb] * 6,
        out_specs=[hb] * 16 + [vm] * 2,
        scratch_shapes=[
            pltpu.VMEM((2, tokens, 768), BF16), pltpu.VMEM((2, tokens, 768), BF16),
            pltpu.VMEM((2, tokens, 1536), BF16),
            pltpu.VMEM((2, 768, 2304), BF16), pltpu.VMEM((2, 768, 768), BF16),
            pltpu.VMEM((2, 768, 3072), BF16), pltpu.VMEM((2, 3072, 768), BF16),
            pltpu.VMEM((384, tokens), F32), pltpu.VMEM((96, tokens), F32),
            pltpu.VMEM((2, 256, 768), BF16), pltpu.VMEM((256, 768), BF16),
            pltpu.VMEM((256, 512), F32),
            pltpu.VMEM((96, 768), BF16), pltpu.VMEM((16, 96, 128), BF16),
            pltpu.VMEM((4, 4, 96, 768), BF16), pltpu.VMEM((4, 4, 64, 768), BF16), pltpu.VMEM((16, 96, 128), BF16),
            pltpu.VMEM((32, 3072), F32), pltpu.VMEM((8, 3072), F32),
            pltpu.VMEM((32, 128), F32), pltpu.VMEM((8, 128), F32),
            pltpu.VMEM((32, 768), BF16), pltpu.VMEM((384, 768), BF16),
            pltpu.VMEM((512, 256), BF16), pltpu.VMEM((256, 768), BF16), pltpu.VMEM((128, 768), F32),
            pltpu.VMEM((48, 768), BF16), pltpu.VMEM((4, 4, 48, 768), BF16),
            pltpu.VMEM((16, 48, 128), BF16), pltpu.VMEM((16, 48, 128), BF16),
            pltpu.VMEM((768, 768), BF16), pltpu.VMEM((3, 4, 48, 768), BF16),
            pltpu.VMEM((4, 48, 768), BF16), pltpu.VMEM((3, 48, 768), BF16),
            pltpu.VMEM((2, 48, 2304), F32), pltpu.VMEM((2, 48, 768), F32), pltpu.VMEM((2, 48, 3072), F32),
            pltpu.VMEM((2, 8, 768), F32), pltpu.VMEM((2, 3072), F32), pltpu.VMEM((48, 768), F32),
            pltpu.SemaphoreType.DMA((2, 5)), pltpu.SemaphoreType.DMA((4,)), pltpu.SemaphoreType.DMA((7,)),
            pltpu.SemaphoreType.DMA((22,)), pltpu.SemaphoreType.DMA((22,)),
            pltpu.SemaphoreType.DMA((32,)), pltpu.SemaphoreType.DMA((32,)),
            pltpu.SemaphoreType.DMA((7,)), pltpu.SemaphoreType.DMA((7,)),
            pltpu.SemaphoreType.DMA((16,)), pltpu.SemaphoreType.DMA((16,)), pltpu.SemaphoreType.DMA((7,)),
        ],
        compiler_params=pltpu.CompilerParams(
            collective_id=1, has_side_effects=True, vmem_limit_bytes=63 * 1024 * 1024
        ),
        name="forward",
    )(lengths, labels.reshape(1, -1), gains, biases, ffn_bias, xq, xp, attn_in, attn_out, ffn_in, ffn_out)


def finish_kernel(
    lens_ref, loss_in, ext_ref, dspq_hbm, dspp_hbm, uw_hbm, raw_hbm, *refs,
):
    ins, outs, (loss_ref, outq_hbm, outp_hbm, dxq_hbm, dxp_hbm), scratch = (
        refs[:12], refs[12:19], refs[19:24], refs[24:]
    )
    part_s, raw_s, sum_s = scratch[:12], scratch[12], scratch[13:17]
    dx_s, dspq_ref, dspp_ref, uw_ref, psem, rsem, ssem, dsem, osem = scratch[17:]
    me, _ = place()
    raw_in = pltpu.make_async_copy(raw_hbm, raw_s, rsem.at[2])
    raw_out = [pltpu.make_async_copy(raw_s.at[t], (outq_hbm, outp_hbm)[t], rsem.at[t]) for t in range(2)]
    gets = [
        pltpu.make_async_copy(uw_hbm, uw_ref, osem.at[0]),
        pltpu.make_async_copy(dspq_hbm, dspq_ref, osem.at[1]),
        pltpu.make_async_copy(dspp_hbm, dspp_ref, osem.at[2]),
    ]
    for c in gets:
        c.start()
    raw_in.start()
    loads = [pltpu.make_async_copy(ins[k], part_s[k], psem.at[k]) for k in range(12)]
    for c in loads:
        c.start()
    loss_ref[...] = loss_in[...]

    for c in gets:
        c.wait()
    extra_p = ext_ref[32:40, :]
    e_hi = extra_p.astype(BF16).astype(F32)
    uw_p = jnp.concatenate([uw_ref[768:960, :].astype(F32), e_hi, extra_p - e_hi], 0).astype(BF16)
    keep = []
    for t in range(2):
        for m in range(4):
            cols = slice(256 * m, 256 * m + 256)
            k = t * 4 + m
            if k >= 2:
                keep[k - 2].wait()
            if t == 0:
                dx_s[k % 2] = dot_tn(dspq_ref[:, cols], uw_ref[0:768, :])
                for c in range(8):
                    dx_s[k % 2, 32 * c:32 * c + 1, :] += ext_ref[8 * m + c:8 * m + c + 1, :]
            else:
                colr = iota((8, 256), 1) + 256 * m
                rowr = iota((8, 256), 0)
                start = jnp.zeros((8, 256), jnp.int32)
                for r in range(2):
                    at = jnp.int32(r * 512)
                    for c in range(4):
                        start = jnp.where(rowr == r * 4 + c, at, start)
                        at = at + lens_ref[r, c]
                sel = jnp.where(colr == start, 1.0, 0.0)
                sel2 = jnp.concatenate([sel, sel], 0).astype(BF16)
                lhs = jnp.concatenate([dspp_ref[:, cols], sel2], 0)
                dx_s[k % 2] = dot_tn(lhs, uw_p)
            c = pltpu.make_async_copy(dx_s.at[k % 2], (dxq_hbm, dxp_hbm)[t].at[cols], dsem.at[k % 2])
            c.start()
            keep.append(c)
            if k == 1:
                raw_in.wait()
                for c in raw_out:
                    c.start()

    stores = []
    for k in range(4):
        loads[k].wait()
        loads[6 + k].wait()
        sum_s[k][...] = part_s[k][...] + part_s[6 + k][...]
        c = pltpu.make_async_copy(sum_s[k], outs[k], ssem.at[k])
        c.start()
        stores.append(c)
    for k in (4, 5, 10, 11):
        loads[k].wait()
    shift = lax.rem(768 - 48 * me, 768)
    for t in range(2):
        sums = pltpu.roll(part_s[4][t] + part_s[10][t], shift, 1)[:, 0:48]
        outs[4][t] = sums[0:2]
        for j in range(6):
            outs[5][j, t:t + 1, :] = sums[2 + j:3 + j]
    ffb = part_s[5][...] + part_s[11][...]
    wide = jnp.concatenate([ffb, jnp.zeros((6, 3072), F32)], 0)
    outs[6][...] = pltpu.roll(wide, lax.rem(3072 - 192 * me, 3072), 1)[0:2, 0:192]
    for c in keep[6:] + stores + raw_out:
        c.wait()


def finish(lengths, loss, dspq, dspp, uw, ext, raw, parts):
    sds = jax.ShapeDtypeStruct
    tokens = dspq.shape[1]
    vm = pl.BlockSpec(memory_space=pltpu.VMEM)
    hb = pl.BlockSpec(memory_space=pl.ANY)
    return pl.pallas_call(
        finish_kernel,
        out_shape=[sds(p.shape, F32) for p in parts[:4]]
        + [sds((2, 2, 48), F32), sds((6, 2, 48), F32), sds((2, 192), F32)]
        + [sds((1, 32), F32), sds((tokens, 768), BF16), sds((tokens, 768), BF16)]
        + [sds((tokens, 768), F32), sds((tokens, 768), F32)],
        in_specs=[pl.BlockSpec(memory_space=pltpu.SMEM)] + [vm] * 2 + [hb] * 16,
        out_specs=[hb] * 4 + [vm] * 4 + [hb] * 4,
        scratch_shapes=[pltpu.VMEM(p.shape, F32) for p in parts]
        + [pltpu.VMEM((2, tokens, 768), BF16)]
        + [pltpu.VMEM(p.shape, F32) for p in parts[:4]]
        + [pltpu.VMEM((2, 256, 768), F32), pltpu.VMEM((768, tokens), BF16)]
        + [pltpu.VMEM((192, tokens), BF16), pltpu.VMEM((960, 768), BF16)]
        + [pltpu.SemaphoreType.DMA((n,)) for n in (12, 3, 4, 2, 3)],
        compiler_params=pltpu.CompilerParams(vmem_limit_bytes=VMEM_LIMIT),
        name="finish",
    )(lengths, loss, ext, dspq, dspp, uw, raw, *parts)


def fast_shards(query_tokens, passage_tokens, lengths, labels, *weights):
    xq = query_tokens.reshape(-1, 768)
    xp = passage_tokens.reshape(-1, 768)
    weights = weights[:5] + (weights[5].transpose(1, 0, 2), weights[6])
    raw, uw, dspq, dspp, *parts, loss, ext = run_forward(xq, xp, lengths, labels, weights)
    win, wout, fin, fout, gains, biases, ffb, loss, outq, outp, dxq, dxp = finish(
        lengths, loss, dspq, dspp, uw, ext, raw, parts
    )
    return (
        loss.reshape(-1),
        outq.reshape(query_tokens.shape),
        outp.reshape(passage_tokens.shape),
        dxq.reshape(query_tokens.shape),
        dxp.reshape(passage_tokens.shape),
        win, wout, fin, fout, gains, biases.transpose(1, 0, 2), ffb,
    )


def layer_norm(residual, gain_vec, shift_vec):
    centre = residual - jnp.mean(residual, -1, keepdims=True)
    inverse = lax.rsqrt(jnp.mean(centre * centre, -1, keepdims=True) + EPSILON)
    return centre * inverse * gain_vec + shift_vec


def plain_norm_back(residual, gain_vec, upstream):
    centre = residual - jnp.mean(residual, -1, keepdims=True)
    inverse = lax.rsqrt(jnp.mean(centre * centre, -1, keepdims=True) + EPSILON)
    normed = centre * inverse
    scaled = upstream * gain_vec
    grad_res = inverse * (
        scaled
        - jnp.mean(scaled, -1, keepdims=True)
        - normed * jnp.mean(scaled * normed, -1, keepdims=True)
    )
    return (grad_res, jnp.sum(upstream * normed, 0), jnp.sum(upstream, 0))


def cls_index(starts, seq_len):
    return (jnp.arange(starts.shape[0], dtype=jnp.int32)[:, None] * seq_len + starts).reshape(-1)


def forward(tokens, segment, starts, params):
    attn_in, attn_out, ffn_in, ffn_out, gains, biases, ffn_bias = params
    batch_size, seq_len, feature = tokens.shape
    head_count = feature // HEAD_DIM
    flat_tokens = tokens.reshape(batch_size * seq_len, feature)
    zeros_vec = jnp.zeros_like(biases[0])
    joined = jnp.dot(flat_tokens, attn_in, preferred_element_type=jnp.float32) + jnp.concatenate(
        [biases[0], zeros_vec, biases[1]]
    )
    joined = joined.astype(jnp.bfloat16)
    shaped = joined.reshape(batch_size, seq_len, 3, head_count, HEAD_DIM)
    scores = (
        jnp.einsum(
            "bqhd,bkhd->bhqk", shaped[:, :, 0], shaped[:, :, 1], preferred_element_type=jnp.float32
        )
        * KEY_SCALE
    )
    same_seg = segment[:, :, None] == segment[:, None, :]
    scores = jnp.where(same_seg[:, None], scores, -1000000000.0)
    attention = jax.nn.softmax(scores, -1).astype(jnp.bfloat16)
    mixed = jnp.einsum(
        "bhqk,bkhd->bqhd", attention, shaped[:, :, 2], preferred_element_type=jnp.float32
    )
    mixed = mixed.reshape(batch_size * seq_len, feature).astype(jnp.bfloat16)
    first_sum = flat_tokens.astype(jnp.float32) + (
        jnp.dot(mixed, attn_out, preferred_element_type=jnp.float32) + biases[2]
    )
    hidden = layer_norm(first_sum, gains[0], biases[3]).astype(jnp.bfloat16)
    inner = jnp.dot(hidden, ffn_in, preferred_element_type=jnp.float32) + ffn_bias
    active = jax.nn.gelu(inner).astype(jnp.bfloat16)
    second_sum = hidden.astype(jnp.float32) + (
        jnp.dot(active, ffn_out, preferred_element_type=jnp.float32) + biases[4]
    )
    output = layer_norm(second_sum, gains[1], biases[5]).astype(jnp.bfloat16)
    picked = cls_index(starts, seq_len)
    kept = (
        flat_tokens,
        joined,
        mixed[picked],
        first_sum[picked],
        hidden[picked],
        inner[picked],
        active[picked],
        second_sum[picked],
    )
    return (output, picked, kept)


def backward(kept, segment, starts, params, upstream):
    attn_in, attn_out, ffn_in, ffn_out, gains, biases, ffn_bias = params
    flat_tokens, joined, mixed_cls, first_cls, hidden_cls, inner_cls, active_cls, second_cls = kept
    batch_size, seq_len = segment.shape
    per_row = starts.shape[1]
    feature = flat_tokens.shape[1]
    head_count = feature // HEAD_DIM
    grad_second, gain_two, shift_two = plain_norm_back(second_cls, gains[1], upstream)
    grad_ffn = grad_second.astype(jnp.bfloat16)
    grad_down = jnp.dot(active_cls.T, grad_ffn, preferred_element_type=jnp.float32)
    grad_active = jnp.dot(grad_ffn, ffn_out.T, preferred_element_type=jnp.float32)
    grad_inner = jax.vjp(jax.nn.gelu, inner_cls)[1](grad_active)[0].astype(jnp.bfloat16)
    grad_up = jnp.dot(hidden_cls.T, grad_inner, preferred_element_type=jnp.float32)
    grad_hidden = grad_second + jnp.dot(grad_inner, ffn_in.T, preferred_element_type=jnp.float32)
    grad_first, gain_one, shift_one = plain_norm_back(first_cls, gains[0], grad_hidden)
    grad_attn = grad_first.astype(jnp.bfloat16)
    grad_outproj = jnp.dot(mixed_cls.T, grad_attn, preferred_element_type=jnp.float32)
    grad_mixed = jnp.dot(grad_attn, attn_out.T, preferred_element_type=jnp.float32).astype(
        jnp.bfloat16
    )
    grad_mixed = grad_mixed.reshape(batch_size, per_row, head_count, HEAD_DIM)
    shaped = joined.reshape(batch_size, seq_len, 3, head_count, HEAD_DIM)
    key_part = shaped[:, :, 1]
    value_part = shaped[:, :, 2]
    picked = cls_index(starts, seq_len)
    query_cls = joined[picked, :feature].reshape(batch_size, per_row, head_count, HEAD_DIM)
    own_seg = jnp.take_along_axis(segment, starts, 1)
    scores = (
        jnp.einsum("bchd,bkhd->bhck", query_cls, key_part, preferred_element_type=jnp.float32)
        * KEY_SCALE
    )
    scores = jnp.where((own_seg[:, :, None] == segment[:, None, :])[:, None], scores, -1000000000.0)
    attention = jax.nn.softmax(scores, -1)
    grad_attention = jnp.einsum(
        "bchd,bkhd->bhck", grad_mixed, value_part, preferred_element_type=jnp.float32
    )
    grad_scores = attention * (
        grad_attention - jnp.sum(attention * grad_attention, -1, keepdims=True)
    )
    grad_scores = grad_scores.astype(jnp.bfloat16)
    grad_query = (
        jnp.einsum("bhck,bkhd->bchd", grad_scores, key_part, preferred_element_type=jnp.float32)
        * KEY_SCALE
    ).astype(jnp.bfloat16)
    grad_key = (
        jnp.einsum("bhck,bchd->bkhd", grad_scores, query_cls, preferred_element_type=jnp.float32)
        * KEY_SCALE
    ).astype(jnp.bfloat16)
    grad_value = jnp.einsum(
        "bhck,bchd->bkhd",
        attention.astype(jnp.bfloat16),
        grad_mixed,
        preferred_element_type=jnp.float32,
    ).astype(jnp.bfloat16)
    places = jnp.arange(seq_len, dtype=jnp.int32)
    selector = (starts[:, :, None] == places[None, None, :]).astype(jnp.bfloat16)
    grad_query_full = jnp.einsum(
        "bcl,bchd->blhd", selector, grad_query, preferred_element_type=jnp.float32
    ).astype(jnp.bfloat16)
    grad_joined = jnp.stack([grad_query_full, grad_key, grad_value], 2).reshape(
        batch_size * seq_len, 3 * feature
    )
    grad_inproj = jnp.dot(flat_tokens.T, grad_joined, preferred_element_type=jnp.float32)
    grad_tokens = (
        jnp.dot(grad_joined, attn_in.T, preferred_element_type=jnp.float32)
        .at[picked]
        .add(grad_first)
    )
    bias_grads = jnp.stack(
        [
            jnp.sum(grad_query.astype(jnp.float32), (0, 1)).reshape(feature),
            jnp.sum(grad_value.astype(jnp.float32), (0, 1)).reshape(feature),
            jnp.sum(grad_attn.astype(jnp.float32), 0),
            shift_one,
            jnp.sum(grad_ffn.astype(jnp.float32), 0),
            shift_two,
        ]
    )
    gain_grads = jnp.stack([gain_one, gain_two])
    hidden_bias = jnp.sum(grad_inner.astype(jnp.float32), 0)
    grads = (grad_inproj, grad_outproj, grad_up, grad_down, gain_grads, bias_grads, hidden_bias)
    row_data = (hidden_cls, grad_inner, active_cls, grad_ffn)
    return (grads, grad_tokens.reshape(batch_size, seq_len, feature), row_data)


def shards(
    query_tokens,
    passage_tokens,
    lengths,
    labels,
    attn_in,
    attn_out,
    ffn_in,
    ffn_out,
    gains,
    biases,
    ffn_bias,
):
    layers = (attn_in, attn_out, ffn_in, ffn_out, gains, biases, ffn_bias)
    query_params = tuple((matrix[0] for matrix in layers))
    passage_params = tuple((matrix[1] for matrix in layers))
    query_count, query_len, feature = query_tokens.shape
    passage_len = passage_tokens.shape[1]
    query_segment = jnp.zeros((query_count, query_len), jnp.int32)
    query_starts = jnp.zeros((query_count, 1), jnp.int32)
    ends = jnp.cumsum(lengths, -1)
    passage_starts = ends - lengths
    places = jnp.arange(passage_len, dtype=jnp.int32)
    passage_segment = jnp.sum((places[None, :, None] >= ends[:, None, :]).astype(jnp.int32), -1)
    query_out, query_pick, query_kept = forward(
        query_tokens, query_segment, query_starts, query_params
    )
    passage_out, passage_pick, passage_kept = forward(
        passage_tokens, passage_segment, passage_starts, passage_params
    )
    query_vec = query_out[query_pick]
    passage_vec = passage_out[passage_pick]
    passage_count = passage_vec.shape[0]
    float_labels = labels.astype(jnp.float32)
    group_vec = lax.all_gather(passage_vec, "grp", axis=0, tiled=True)
    portion = lax.all_gather(group_vec, "blk", axis=0, tiled=True)
    running_max = jnp.full((query_count,), -1e30, jnp.float32)
    score_block = SCORE_SCALE * jnp.dot(query_vec, portion.T, preferred_element_type=jnp.float32)
    column_ids = jnp.arange(portion.shape[0], dtype=jnp.int32)
    new_max = jnp.maximum(running_max, jnp.max(score_block, -1))
    running_sum = jnp.sum(jnp.exp(score_block - new_max[:, None]), -1)
    hits = column_ids[None, :] == labels[:, None]
    positive = jnp.sum(jnp.where(hits, score_block, 0.0), -1)
    running_max, running_sum, positive = (new_max, running_sum, positive)
    norm_log = running_max + jnp.log(running_sum)
    portion = lax.all_gather(group_vec, "blk", axis=0, tiled=True)
    score_block = SCORE_SCALE * jnp.dot(query_vec, portion.T, preferred_element_type=jnp.float32)
    column_ids = jnp.arange(portion.shape[0], dtype=jnp.int32)
    hits = (column_ids[None, :] == labels[:, None]).astype(jnp.float32)
    grad_block = (jnp.exp(score_block - norm_log[:, None]) - hits).astype(jnp.bfloat16)
    query_up = SCORE_SCALE * jnp.dot(grad_block, portion, preferred_element_type=jnp.float32)
    own_ids = (
        lax.axis_index(("blk", "grp")) * passage_count + jnp.arange(passage_count, dtype=jnp.int32)
    ).astype(jnp.float32)
    remote_vec = lax.all_gather(query_vec.astype(jnp.float32), ("blk", "grp"), axis=0, tiled=True)
    remote_log = lax.all_gather(norm_log, ("blk", "grp"), axis=0, tiled=True)
    remote_label = lax.all_gather(float_labels, ("blk", "grp"), axis=0, tiled=True)
    remote_low = remote_vec.astype(jnp.bfloat16)
    score_block = SCORE_SCALE * jnp.dot(
        remote_low, passage_vec.T, preferred_element_type=jnp.float32
    )
    hits = (remote_label[:, None] == own_ids[None, :]).astype(jnp.float32)
    grad_block = (jnp.exp(score_block - remote_log[:, None]) - hits).astype(jnp.bfloat16)
    passage_up = SCORE_SCALE * jnp.dot(grad_block.T, remote_low, preferred_element_type=jnp.float32)
    query_losses = norm_log - positive
    query_grads, query_back, query_rows = backward(
        query_kept, query_segment, query_starts, query_params, query_up
    )
    passage_grads, passage_back, passage_rows = backward(
        passage_kept, passage_segment, passage_starts, passage_params, passage_up
    )
    stacked = tuple(
        (
            jnp.stack([first_part, second_part])
            for first_part, second_part in zip(query_grads, passage_grads)
        )
    )
    grad_win, grad_wout, grad_up, grad_down, grad_gain, grad_bias, grad_hidden_bias = stacked
    shares = (
        lax.psum_scatter(
            grad_win.astype(jnp.bfloat16), "blk", scatter_dimension=1, tiled=True
        ).astype(jnp.float32),
        lax.psum_scatter(
            grad_wout.astype(jnp.bfloat16), "blk", scatter_dimension=1, tiled=True
        ).astype(jnp.float32),
        lax.psum_scatter(
            grad_up.astype(jnp.bfloat16), "blk", scatter_dimension=1, tiled=True
        ).astype(jnp.float32),
        lax.psum_scatter(
            grad_down.astype(jnp.bfloat16), "blk", scatter_dimension=1, tiled=True
        ).astype(jnp.float32),
        lax.psum_scatter(
            grad_gain.astype(jnp.bfloat16), "blk", scatter_dimension=2, tiled=True
        ).astype(jnp.float32),
        lax.psum_scatter(
            grad_bias.astype(jnp.bfloat16), "blk", scatter_dimension=2, tiled=True
        ).astype(jnp.float32),
        lax.psum_scatter(
            grad_hidden_bias.astype(jnp.bfloat16), "blk", scatter_dimension=1, tiled=True
        ).astype(jnp.float32),
    )
    grad_win, grad_wout, grad_up, grad_down, grad_gain, grad_bias, grad_hidden_bias = (
        lax.psum(shares[0].astype(jnp.bfloat16), "grp").astype(jnp.float32),
        lax.psum(shares[1].astype(jnp.bfloat16), "grp").astype(jnp.float32),
        lax.psum(shares[2].astype(jnp.bfloat16), "grp").astype(jnp.float32),
        lax.psum(shares[3].astype(jnp.bfloat16), "grp").astype(jnp.float32),
        lax.psum(shares[4].astype(jnp.bfloat16), "grp").astype(jnp.float32),
        lax.psum(shares[5].astype(jnp.bfloat16), "grp").astype(jnp.float32),
        lax.psum(shares[6].astype(jnp.bfloat16), "grp").astype(jnp.float32),
    )
    query_shaped = query_out.reshape(query_count, query_len, feature)
    passage_shaped = passage_out.reshape(passage_tokens.shape)
    return (
        query_losses,
        query_shaped,
        passage_shaped,
        query_back,
        passage_back,
        grad_win,
        grad_wout,
        grad_up,
        grad_down,
        grad_gain,
        grad_bias,
        grad_hidden_bias,
    )


def solution(mesh):
    placed = (
        P(("blk", "grp"), None, None),
        P(("blk", "grp"), None, None),
        P(("blk", "grp"), None),
        P(("blk", "grp")),
        P(),
        P(),
        P(),
        P(),
        P(),
        P(),
        P(),
    )
    small = dict(mesh.shape) == {"blk": 16, "grp": 2}
    return jax.shard_map(
        fast_shards if small else shards,
        mesh=mesh,
        in_specs=placed,
        out_specs=(
            P(("blk", "grp")),
            P(("blk", "grp"), None, None),
            P(("blk", "grp"), None, None),
            P(("blk", "grp"), None, None),
            P(("blk", "grp"), None, None),
            P(None, "blk", None),
            P(None, "blk", None),
            P(None, "blk", None),
            P(None, "blk", None),
            P(None, None, "blk"),
            P(None, None, "blk"),
            P(None, "blk"),
        ),
        check_vma=False,
    )
```

```python
import functools
import jax
import jax.numpy as jnp
from jax import lax
from jax.experimental import pallas as pl
from jax.experimental.pallas import tpu as pltpu
from jax.sharding import PartitionSpec as P

MESH = pl.DeviceIdType.MESH
HEAD_DIM = 64
HEADS = 12
EPSILON = 1e-05
SCORE_SCALE = 0.08
KEY_SCALE = 0.125
NEG = -1000000000.0
GELU_A = 0.7978845608028654
GELU_B = 0.044715 * GELU_A
F32 = jnp.float32
BF16 = jnp.bfloat16
VMEM_LIMIT = 60 * 1024 * 1024


def dot(a, b):
    return lax.dot_general(a, b, (((1,), (0,)), ((), ())), preferred_element_type=F32)


def dot_nt(a, b):
    return lax.dot_general(a, b, (((1,), (1,)), ((), ())), preferred_element_type=F32)


def dot_tn(a, b):
    return lax.dot_general(a, b, (((0,), (0,)), ((), ())), preferred_element_type=F32)


def iota(shape, dim):
    return lax.broadcasted_iota(jnp.int32, shape, dim)


def head_row(h):
    return iota((1, 768), 1) // HEAD_DIM == h


def expand_heads(rows, h0=0, heads=HEADS):
    return jnp.concatenate(
        [jnp.where(head_row(h0 + h), rows, 0.0) for h in range(heads)], 0
    )


def fold_heads(rows, count, h0=0, heads=HEADS):
    out = jnp.where(head_row(h0), rows[:count], 0.0)
    for h in range(1, heads):
        out = out + jnp.where(head_row(h0 + h), rows[h * count:(h + 1) * count], 0.0)
    return out


def norm_stats(residual):
    centre = residual - jnp.mean(residual, -1, keepdims=True)
    inverse = lax.rsqrt(jnp.mean(centre * centre, -1, keepdims=True) + EPSILON)
    return centre * inverse, inverse


def gelu(v):
    half = 0.5 + 0.5 * jnp.tanh(v * (GELU_A + GELU_B * (v * v)))
    return v * half


def split3(v):
    hi = v.astype(BF16).astype(F32)
    rest = v - hi
    mid = rest.astype(BF16).astype(F32)
    return hi, mid, rest - mid


def lane_pack(columns, count):
    lane = iota((count, 128), 1)
    out = jnp.zeros((count, 128), F32)
    for j, column in enumerate(columns):
        out = jnp.where(lane == j, column, out)
    return out


def norm_back(up, gain, normed, inverse):
    u = up * gain
    return inverse * (
        u - jnp.mean(u, -1, keepdims=True) - normed * jnp.mean(u * normed, -1, keepdims=True)
    )


def gelu_pair(v):
    sq = v * v
    half = 0.5 + 0.5 * jnp.tanh(v * (GELU_A + GELU_B * sq))
    value = v * half
    return value, half + (value - value * half) * (2.0 * GELU_A + 6.0 * GELU_B * sq)


def decode_inv(ext):
    return ext[:, 0:1] + ext[:, 1:2] + ext[:, 2:3], ext[:, 3:4] + ext[:, 4:5] + ext[:, 5:6]


def ext_rows(block):
    e_p = block[:, :, 0:128].reshape(128, 128)
    e_q = jnp.concatenate([block[:, :, 128 * a:128 * a + 128] for a in range(1, 5)], 1)
    return e_p, e_q.reshape(512, 128)


def place():
    return lax.axis_index("blk"), lax.axis_index("grp")


def remote(src, dst, send, recv, peer):
    return pltpu.make_async_remote_copy(
        src_ref=src, dst_ref=dst, send_sem=send, recv_sem=recv, device_id=peer, device_id_type=MESH
    )


def greet(me, g):
    barrier = pltpu.get_barrier_semaphore()
    for i in range(1, 16):
        pl.semaphore_signal(barrier, inc=1, device_id=(lax.rem(me + i, 16), g), device_id_type=MESH)
    pl.semaphore_signal(barrier, inc=1, device_id=(me, 1 - g), device_id_type=MESH)


def greeted():
    pl.semaphore_wait(pltpu.get_barrier_semaphore(), 16)


def gather_phases(me, g, pay, ga, ss, rs, base, lo, hi):
    z, yx = me // 4, lax.rem(me, 4)
    xpeer = me + 1 - 2 * lax.rem(me, 2)
    ypeer = me + 2 - 4 * (lax.rem(me, 4) // 2)
    yx_x, yx_y = lax.rem(xpeer, 4), lax.rem(ypeer, 4)
    rows = slice(lo, hi)
    first, second, third = [], [], []

    def add(phase, src, dst, k, peer):
        phase.append(remote(src, dst, ss.at[base + k], rs.at[base + k], (peer, g)))

    for d in range(1, 4):
        peer = lax.rem(z + d, 4) * 4 + yx
        add(first, pay.at[rows], ga.at[z, yx, rows], d - 1, peer)
    add(second, ga.at[:, yx, rows], ga.at[:, yx, rows], 3, xpeer)
    add(second, ga.at[:, yx, rows], ga.at[:, yx, rows], 4, ypeer)
    add(third, ga.at[0:2, yx_x, rows], ga.at[0:2, yx_x, rows], 5, ypeer)
    add(third, ga.at[2:4, yx_y, rows], ga.at[2:4, yx_y, rows], 6, xpeer)
    return first, second, third


QR, PR = 512, 128


def forward_kernel(
    lens_ref, labels_ref, gains_ref, biases_ref, ffnb_ref,
    xq_hbm, xp_hbm, win_hbm, wout_hbm, fin_hbm, fout_hbm,
    out_hbm, uw_hbm, dspq_hbm, dspp_hbm,
    pwin_hbm, pwout_hbm, pfin_hbm, pfout_hbm, psum_hbm, pffb_hbm,
    swin_hbm, swout_hbm, sfin_hbm, sfout_hbm, ssum_hbm, sffb_hbm,
    loss_ref, ext_ref,
    x_s, q_s, kv_s, win_s, wout_s, fin_s, fout_s, pq_s, pp_s, out_s, mix_s, bias_s,
    pay_s, swap_s, ga_ref, gs_ref, rsw_ref, innq_ref, innp_ref, invq_ref, invp_ref, qq_ref, zq_ref,
    grad_s, pv_s, upp_s, gq_s, rgq_s, yt_s, ryt_s, sib_s, r1_s, s2_s, r2_s,
    pwin_s, pwout_s, pfin_s, pfout_s, psum_s, pffb_s, acc_s,
    sem, lsem, osem, ss, rs, as_, ar, xs, xr, ks, kr, psem,
):
    me, g = place()
    z, yx = me // 4, lax.rem(me, 4)
    greet(me, g)
    copies = []
    for t, x_hbm in enumerate((xq_hbm, xp_hbm)):
        copies.append([
            pltpu.make_async_copy(x_hbm, x_s.at[t], sem.at[t, 0]),
            pltpu.make_async_copy(win_hbm.at[t], win_s.at[t], sem.at[t, 1]),
            pltpu.make_async_copy(wout_hbm.at[t], wout_s.at[t], sem.at[t, 2]),
            pltpu.make_async_copy(fin_hbm.at[t], fin_s.at[t], sem.at[t, 3]),
            pltpu.make_async_copy(fout_hbm.at[t], fout_s.at[t], sem.at[t, 4]),
        ])
    for c in copies[0][:2] + copies[1][:2] + copies[0][2:] + copies[1][2:]:
        c.start()
    a1, b1, c1 = gather_phases(me, g, pay_s, ga_ref, ss, rs, 0, 0, 64)
    a2, b2, c2 = gather_phases(me, g, pay_s, ga_ref, ss, rs, 7, 64, 96)
    last_hop = [remote(ga_ref.at[:, :, 0:64], gs_ref, ss.at[14], rs.at[14], (me, 1 - g))]
    swaps = []
    for i in range(1, 16):
        peer = lax.rem(me + i, 16)
        swaps.append(remote(swap_s.at[peer], rsw_ref.at[me], as_.at[i], ar.at[i], (peer, g)))
    own_copy = [
        pltpu.make_async_copy(pay_s, ga_ref.at[z, yx], lsem.at[0]),
        pltpu.make_async_copy(swap_s.at[me], rsw_ref.at[me], lsem.at[1]),
    ]

    tokens = x_s.shape[1]
    col_q = iota((32, tokens), 1)
    row_q = iota((32, tokens), 0)
    sel_q = col_q == row_q * 32
    own_q = col_q // 32 == row_q
    col_p = iota((8, tokens), 1)
    row_p = iota((8, tokens), 0)
    lo = jnp.zeros((8, tokens), jnp.int32)
    hi = jnp.zeros((8, tokens), jnp.int32)
    for r in range(2):
        acc = jnp.int32(r * 512)
        for c in range(4):
            length = lens_ref[r, c]
            lo = jnp.where(row_p == r * 4 + c, acc, lo)
            acc = acc + length
            hi = jnp.where(row_p == r * 4 + c, acc, hi)
    sel_p = col_p == lo
    own_p = (col_p >= lo) & (col_p < hi)

    picks = []
    for t, sel in enumerate((sel_q, sel_p)):
        copies[t][0].wait()
        copies[t][1].wait()
        query_bias = biases_ref[0, t:t + 1, :]
        value_bias = biases_ref[1, t:t + 1, :]

        def kv_step(m, _, t=t, query_bias=query_bias, value_bias=value_bias):
            rows = pl.ds(pl.multiple_of(m * 256, 256), 256)
            x = x_s[t, rows, :]
            kv_s[t, rows, 0:768] = dot(x, win_s[t, :, 768:1536]).astype(BF16)
            kv_s[t, rows, 768:1536] = (dot(x, win_s[t, :, 1536:2304]) + value_bias).astype(BF16)
            q_s[t, rows, :] = (dot(x, win_s[t, :, 0:768]) + query_bias).astype(BF16)
            return 0

        lax.fori_loop(0, tokens // 256, kv_step, 0)
        pick = jnp.where(sel, 1.0, 0.0).astype(BF16)
        picks.append((dot(pick, x_s[t]), dot(pick, q_s[t])))

    done = []
    for t, (own, count, p_s, inn_ref, inv_ref) in enumerate((
        (own_q, 32, pq_s, innq_ref, invq_ref), (own_p, 8, pp_s, innp_ref, invp_ref),
    )):
        xc, qc = picks[t]
        mixed = jnp.zeros((count, 768), F32)
        heads = 4 if t == 0 else HEADS
        mask = jnp.concatenate([jnp.where(own, 0.0, NEG)] * heads, 0)
        for h0 in range(0, HEADS, heads):
            span = slice(h0 * count, (h0 + heads) * count)
            spread = expand_heads(qc, h0, heads).astype(BF16)
            scores = dot_nt(spread, kv_s[t, :, 0:768]) * KEY_SCALE + mask
            weight = jnp.exp(scores - jnp.max(scores, -1, keepdims=True))
            soft = weight * (1.0 / jnp.sum(weight, -1, keepdims=True))
            p_s[span, :] = soft
            soft16 = soft.astype(BF16)
            mixed = mixed + fold_heads(dot(soft16, kv_s[t, :, 768:1536]), count, h0, heads)
            zsum = dot(soft16, x_s[t])
            if t == 0:
                zq_ref[span, :] = zsum.astype(BF16)
            else:
                wide = jnp.concatenate([zsum, jnp.zeros((32, 768), F32)], 0)
                swap_s[:, 48:96, :] = wide.T.astype(BF16).reshape(16, 48, 128)
        mixed = mixed.astype(BF16)
        copies[t][2].wait()
        first = xc + (dot(mixed, wout_s[t]) + biases_ref[2, t:t + 1, :])
        n1, inv1 = norm_stats(first)
        hidden = (n1 * gains_ref[t, 0:1, :] + biases_ref[3, t:t + 1, :]).astype(BF16)
        copies[t][3].wait()
        inner = dot(hidden, fin_s[t]) + ffnb_ref[t:t + 1, :]
        inn_ref[...] = inner
        active = gelu(inner).astype(BF16)
        copies[t][4].wait()
        second = hidden.astype(F32) + (dot(active, fout_s[t]) + biases_ref[4, t:t + 1, :])
        n2, inv2 = norm_stats(second)
        vec = (n2 * gains_ref[t, 1:2, :] + biases_ref[5, t:t + 1, :]).astype(BF16)
        inv_ref[...] = lane_pack([inv1, inv2], count)
        done.append((xc, qc, mixed, hidden, vec, inv1, inv2))

    xq, qq, mq, hq, vq, i1q, i2q = done[0]
    xp, qp, mp, hp, vp, i1p, i2p = done[1]
    lab = labels_ref[...].astype(F32)
    eye = iota((32, 32), 0) == iota((32, 32), 1)
    lab_col = jnp.sum(jnp.where(eye, lab, 0.0), 1, keepdims=True)
    lab_hi = jnp.floor(lab_col * (1.0 / 256.0))
    lab_lo = lab_col - 256.0 * lab_hi
    ext_q = lane_pack([*split3(i1q), *split3(i2q), lab_hi, lab_lo], 32)
    ext_p = lane_pack([*split3(i1p), *split3(i2p)], 8)
    ext = jnp.concatenate(
        [ext_p] + [ext_q[8 * a:8 * a + 8] for a in range(4)] + [jnp.zeros((8, 128), F32)], 1
    )
    pay_s[0:32, :] = vq
    pay_s[32:64, :] = jnp.concatenate([hp.astype(F32), vp.astype(F32), qp, ext], 0).astype(BF16)
    pay_s[64:96, :] = hq
    qq_ref[...] = qq.astype(BF16)
    greeted()
    own_copy[0].start()
    for c in a1 + a2:
        c.start()
    m48 = jnp.concatenate([mq.astype(F32), mp.astype(F32), jnp.zeros((8, 768), F32)], 0)
    x48 = jnp.concatenate([xq, xp, jnp.zeros((8, 768), F32)], 0)
    swap_s[:, 0:48, :] = jnp.zeros((16, 48, 128), BF16)
    for b in range(16):
        swap_s[b, 0:48, 0:48] = m48[:, 48 * b:48 * b + 48].astype(BF16)
        swap_s[b, 0:48, 64:112] = x48[:, 48 * b:48 * b + 48].astype(BF16)
    for c in own_copy[1:]:
        c.start()

    low_half = iota((1, 128), 1) < HEAD_DIM

    def tile(step, _):
        tower = step // 4
        rows = pl.ds(pl.multiple_of(lax.rem(step, 4) * 256, 256), 256)

        def on(k, waits, starts):
            @pl.when(step == k)
            def _():
                for c in waits:
                    c.wait()
                for c in starts:
                    c.start()

        on(2, own_copy[0:1] + a1, b1)
        on(3, a2, b2)
        on(4, b1, c1 + swaps)
        on(5, b2, c2)
        on(6, c1, last_hop)

        @pl.when(step < 4)
        def _():
            same = iota((128, 128), 0) // 32 == iota((128, 128), 1) // 32
            mask = jnp.where(same, 0.0, NEG)
            mask2 = jnp.concatenate([mask, mask], 0)
            for part in range(2):
                at = pl.ds(pl.multiple_of(lax.rem(step, 4) * 256 + part * 128, 128), 128)
                for j in range(HEADS // 2):
                    lanes = slice(128 * j, 128 * j + 128)
                    q = q_s[0, at, lanes]
                    k = kv_s[0, at, lanes]
                    v = kv_s[0, at, 768 + 128 * j:768 + 128 * j + 128]
                    zero = jnp.zeros_like(q)
                    q2 = jnp.concatenate([jnp.where(low_half, q, zero), jnp.where(low_half, zero, q)], 0)
                    s = dot_nt(q2, k) * KEY_SCALE + mask2
                    e = jnp.exp(s - jnp.max(s, -1, keepdims=True))
                    total = jnp.sum(e, -1, keepdims=True)
                    o = dot(e.astype(BF16), v) * (1.0 / total)
                    mix_s[part * 128:part * 128 + 128, lanes] = jnp.where(low_half, o[:128], o[128:]).astype(BF16)

        @pl.when(step >= 4)
        def _():
            row = (step - 4) // 2
            base = lax.rem(step, 2) * 256
            keys = pl.ds(pl.multiple_of(row * 512, 512), 512)
            qpos = iota((256, 512), 0) + base
            kpos = iota((256, 512), 1)
            qseg = jnp.zeros((256, 512), jnp.int32)
            kseg = jnp.zeros((256, 512), jnp.int32)
            end = jnp.int32(0)
            for c in range(3):
                end = end + lens_ref[row, c]
                qseg = qseg + jnp.where(qpos >= end, 1, 0)
                kseg = kseg + jnp.where(kpos >= end, 1, 0)
            mask = jnp.where(qseg == kseg, 0.0, NEG)
            bias_s[...] = mask
            def heads(i, _):
                for j in range(2):
                    lanes = pl.ds(pl.multiple_of(256 * i + 128 * j, 128), 128)
                    q = q_s[1, rows, lanes]
                    k = kv_s[1, keys, lanes]
                    v = kv_s[1, keys, pl.ds(pl.multiple_of(768 + 256 * i + 128 * j, 128), 128)]
                    zero = jnp.zeros_like(q)
                    halves = []
                    for part in (jnp.where(low_half, q, zero), jnp.where(low_half, zero, q)):
                        s = dot_nt(part, k) * KEY_SCALE + bias_s[...]
                        e = jnp.exp(s - jnp.max(s, -1, keepdims=True))
                        total = jnp.sum(e, -1, keepdims=True)
                        halves.append(dot(e.astype(BF16), v) * (1.0 / total))
                    mix_s[:, lanes] = jnp.where(low_half, halves[0], halves[1]).astype(BF16)
                return 0

            lax.fori_loop(0, 3, heads, 0)

        first_sum = x_s[tower, rows, :].astype(F32) + (
            dot(mix_s[...], wout_s[tower]) + biases_ref[2, pl.ds(tower, 1), :]
        )
        n1, _ = norm_stats(first_sum)
        hidden = (n1 * gains_ref[tower, 0:1, :] + biases_ref[3, pl.ds(tower, 1), :]).astype(BF16)
        second_sum = hidden.astype(F32) + biases_ref[4, pl.ds(tower, 1), :]
        for c in range(4):
            cols = slice(768 * c, 768 * c + 768)
            inner = dot(hidden, fin_s[tower, :, cols]) + ffnb_ref[pl.ds(tower, 1), cols]
            second_sum = second_sum + dot(gelu(inner).astype(BF16), fout_s[tower, cols, :])
        n2, _ = norm_stats(second_sum)
        slot = lax.rem(step, 2)

        @pl.when(step >= 2)
        def _():
            pltpu.make_async_copy(out_s.at[slot], out_hbm.at[tower, rows], osem.at[slot]).wait()

        out_s[slot] = (
            n2 * gains_ref[tower, 1:2, :] + biases_ref[5, pl.ds(tower, 1), :]
        ).astype(BF16)
        pltpu.make_async_copy(out_s.at[slot], out_hbm.at[tower, rows], osem.at[slot]).start()
        return 0

    lax.fori_loop(0, 8, tile, 0)
    for c in c2 + last_hop + swaps + own_copy[1:]:
        c.wait()
    for i in range(2):
        pltpu.make_async_copy(out_s.at[i], out_hbm.at[1, 0:256], osem.at[i]).wait()
    ga = ga_ref.reshape(16, 96, 768)
    gs = gs_ref.reshape(16, 64, 768)

    sib = (me, 1 - g)
    pair = [remote(q_s.at[1 - g, 0:768], sib_s, ks.at[0], kr.at[0], sib)]
    save_dsp = [
        pltpu.make_async_copy(kv_s.at[0, 0:768, 0:tokens], dspq_hbm, osem.at[5]),
        pltpu.make_async_copy(kv_s.at[1, 0:192, 0:tokens], dspp_hbm, osem.at[6]),
    ]
    save_uw = pltpu.make_async_copy(x_s.at[0, 0:960], uw_hbm, osem.at[4])

    pv_own = ga[:, 32:48].astype(F32)[:, 8:16].reshape(128, 768)
    pv_sib = gs[:, 32:48].astype(F32)[:, 8:16].reshape(128, 768)
    pv = jnp.concatenate([pv_own, pv_sib], 0).astype(BF16)
    col = iota((1, 256), 1)
    within = lax.rem(col, 128)
    side = jnp.where(col < 128, g, 1 - g)
    ids = (within // 8) * 16 + side * 8 + lax.rem(within, 8)
    for half, src in enumerate((ga, gs)):
        _, eq = ext_rows(src[:, 48:64].astype(F32)[:, 8:16])
        label = (eq[:, 6:7] * 256.0 + eq[:, 7:8]).astype(jnp.int32)
        logits = SCORE_SCALE * dot_nt(src[:, 0:32].reshape(512, 768), pv)
        top = jnp.max(logits, -1, keepdims=True)
        norm_log = top + jnp.log(jnp.sum(jnp.exp(logits - top), -1, keepdims=True))
        hit = label == ids
        grad = (jnp.exp(logits - norm_log) - jnp.where(hit, 1.0, 0.0)).astype(BF16)
        part = SCORE_SCALE * dot_tn(grad[:, 0:128], src[:, 0:32].reshape(512, 768))
        if half == 0:
            positive = jnp.sum(jnp.where(hit, logits, 0.0), -1, keepdims=True)
            loss = jnp.where(iota((512, 1), 0) // 32 == me, norm_log - positive, 0.0)
            diagonal = lax.rem(iota((512, 32), 0), 32) == iota((512, 32), 1)
            loss_ref[...] = jnp.sum(jnp.where(diagonal, loss, 0.0), 0, keepdims=True)
            grad_s[...] = grad
            upp_s[...] = part
        else:
            upp_s[...] += part
    pv_s[...] = pv

    def query_up(rows):
        return SCORE_SCALE * dot(grad_s[rows, :], pv_s[...])

    mine = ga[me]
    low = mine[32:64].astype(F32)
    gq_rows, keep = [], []
    for t, (count, up, hidden, vec, q, inn_ref, inv_ref, p_s) in enumerate((
        (32, query_up(pl.ds(pl.multiple_of(me * 32, 32), 32)), mine[64:96].astype(F32),
         mine[0:32].astype(F32), qq_ref[...].astype(F32), innq_ref, invq_ref, pq_s),
        (8, upp_s[pl.ds(pl.multiple_of(me * 8, 8), 8), :], low[0:8], low[8:16], low[16:24],
         innp_ref, invp_ref, pp_s),
    )):
        g0, g1 = gains_ref[t, 0:1, :], gains_ref[t, 1:2, :]
        n2 = (vec - biases_ref[5, t:t + 1, :]) / g1
        n1 = (hidden - biases_ref[3, t:t + 1, :]) / g0
        grad_second = norm_back(up, g1, n2, inv_ref[:, 1:2])
        grad_ffn = grad_second.astype(BF16)
        grad_active = dot_nt(grad_ffn, fout_s[t])
        _, slope = gelu_pair(inn_ref[...])
        grad_inner = (grad_active * slope).astype(BF16)
        grad_hidden = grad_second + dot_nt(grad_inner, fin_s[t])
        grad_first = norm_back(grad_hidden, g0, n1, inv_ref[:, 0:1])
        gm = dot_nt(grad_first.astype(BF16), wout_s[t]).astype(BF16)
        n = HEADS * count
        heads = 4 if t == 0 else HEADS
        gq = jnp.zeros((count, 768), F32)
        slopes = []
        rows_y = out_s.reshape(512, 768)
        for h0 in range(0, HEADS, heads):
            span = slice(h0 * count, (h0 + heads) * count)
            wide = expand_heads(gm.astype(F32), h0, heads).astype(BF16)
            dp = dot_nt(wide, kv_s[t, :, 768:1536])
            soft = p_s[span, :]
            ds = (soft * (dp - jnp.sum(soft * dp, -1, keepdims=True))).astype(BF16)
            slopes.append(ds)
            gq = gq + fold_heads(dot(ds, kv_s[t, :, 0:768]), count, h0, heads)
            y = dot(ds, x_s[t]) * KEY_SCALE
            if t == 0:
                rows_y[span, :] = y.astype(BF16)
            else:
                yt_s[...] = jnp.concatenate(
                    [y, jnp.zeros((32, 768), F32)], 0
                ).T.astype(BF16).reshape(16, 48, 128)
        gq = gq * KEY_SCALE
        gq_rows.append(gq)
        wide = expand_heads(gm.astype(F32)).astype(BF16)
        spread = expand_heads(q).astype(BF16)
        if t == 0:
            for lo in range(0, 768, 256):
                q_s[0, lo:lo + 256, :] = dot_tn(rows_y[0:384, lo:lo + 256], spread).astype(BF16)
            for lo in range(0, 768, 256):
                q_s[1, lo:lo + 256, :] = dot_tn(zq_ref[:, lo:lo + 256], wide).astype(BF16)
            for c in pair:
                c.start()
        for i, ds in enumerate(slopes):
            span = slice(i * heads * count, (i + 1) * heads * count)
            kv_s[t, span, 0:tokens] = ds
        kv_s[t, n:2 * n, 0:tokens] = p_s[...].astype(BF16)
        save_dsp[t].start()
        at = 768 * t
        for lo in range(0, n, 128):
            hi = min(lo + 128, n)
            u = dot_nt(spread[lo:hi], win_s[t, :, 768:1536]) * KEY_SCALE
            x_s[0, at + lo:at + hi, :] = u.astype(BF16)
            x_s[0, at + n + lo:at + n + hi, :] = dot_nt(wide[lo:hi], win_s[t, :, 1536:2304]).astype(BF16)
        extra = dot_nt(gq.astype(BF16), win_s[t, :, 0:768]) + grad_first
        ext_ref[32 * t:32 * t + count, :] = extra
    gq_s[...] = jnp.concatenate(gq_rows + [jnp.zeros((8, 768), F32)], 0).astype(BF16)
    save_uw.start()
    for c in save_dsp:
        c.wait()

    first, second, third = gather_phases(me, g, gq_s, rgq_s, ss, rs, 15, 0, 48)
    rows_swap = []
    for i in range(1, 16):
        peer = lax.rem(me + i, 16)
        rows_swap.append(remote(yt_s.at[peer], ryt_s.at[me], as_.at[16 + i], ar.at[16 + i], (peer, g)))
    own = [
        pltpu.make_async_copy(gq_s, rgq_s.at[z, yx], lsem.at[2]),
        pltpu.make_async_copy(yt_s.at[me], ryt_s.at[me], lsem.at[3]),
    ]
    xpeer = me + 1 - 2 * lax.rem(me, 2)
    ypeer = me + 2 - 4 * (lax.rem(me, 4) // 2)
    dpeer = xpeer + 2 - 4 * (lax.rem(xpeer, 4) // 2)
    plane = []
    for k, peer in enumerate((dpeer, xpeer, ypeer)):
        for zz in range(4):
            at = pl.multiple_of(48 * (4 * zz + lax.rem(peer, 4)), 16)
            n = 1 + 4 * k + zz
            plane.append(remote(
                q_s.at[g, pl.ds(at, 48)], r1_s.at[k, zz], ks.at[n], kr.at[n], (peer, g)
            ))
    column = [
        remote(s2_s.at[lax.rem(z + d, 4)], r2_s.at[d - 1], ks.at[12 + d], kr.at[12 + d],
               (lax.rem(z + d, 4) * 4 + yx, g))
        for d in range(1, 4)
    ]

    def add_pair():
        def one(i, _):
            at = pl.ds(pl.multiple_of(48 * i, 16), 48)
            q_s[g, at, :] = (q_s[g, at, :].astype(F32) + sib_s[at, :].astype(F32)).astype(BF16)
            return 0

        lax.fori_loop(0, 16, one, 0)

    def add_plane():
        def one(i, _):
            at = pl.ds(pl.multiple_of(48 * (4 * i + yx), 16), 48)
            s2_s[i] = (
                q_s[g, at, :].astype(F32) + r1_s[0, i].astype(F32)
                + r1_s[1, i].astype(F32) + r1_s[2, i].astype(F32)
            ).astype(BF16)
            return 0

        lax.fori_loop(0, 4, one, 0)

    shares = [(pwout_s, pwout_hbm, swout_hbm), (pfin_s, pfin_hbm, sfin_hbm), (pffb_s, pffb_hbm, sffb_hbm)]
    shares += [
        (pfout_s.at[t], pfout_hbm.at[t], sfout_hbm.at[t]) for t in range(2)
    ]
    shares += [(pwin_s, pwin_hbm, swin_hbm), (psum_s, psum_hbm, ssum_hbm)]
    sends = [remote(a, c, xs.at[n], xr.at[n], sib) for n, (a, b, c) in enumerate(shares)]
    saves = [pltpu.make_async_copy(a, b, psem.at[n]) for n, (a, b, c) in enumerate(shares)]
    early, late = sends[:5] + saves[:5], sends[5:] + saves[5:]
    for c in own + first + rows_swap:
        c.start()
    for c in pair:
        c.wait()
    add_pair()
    for c in plane:
        c.start()

    ext = ga[:, 48:64].astype(F32)[:, 8:16]
    ext_p, ext_q = ext_rows(ext)
    psum_s[...] = jnp.zeros(psum_s.shape, F32)
    pffb_s[...] = jnp.zeros(pffb_s.shape, F32)

    def chain(t, up, hidden, vec, inv1, inv2, rows, count):
        g0, g1 = gains_ref[t, 0:1, :], gains_ref[t, 1:2, :]
        total = lambda v: jnp.sum(v, 0, keepdims=True)
        n2 = (vec.astype(F32) - biases_ref[5, t:t + 1, :]) / g1
        grad_second = norm_back(up, g1, n2, inv2)
        grad_ffn = grad_second.astype(BF16)
        x_s[1, rows, :] = grad_ffn
        psum_s[t, 1:2, :] += total(up * n2)
        psum_s[t, 6:7, :] += total(grad_ffn.astype(F32))
        psum_s[t, 7:8, :] += total(up)
        grad_hidden = grad_second
        for c in range(4):
            cols = slice(768 * c, 768 * c + 768)
            inner = dot(hidden, fin_s[t, :, cols]) + ffnb_ref[t:t + 1, cols]
            active, slope = gelu_pair(inner)
            half = slice(768 * (c % 2), 768 * (c % 2) + 768)
            kept = active if c == 0 else jnp.where(me // 4 == c, active, kept)
            grad_inner = (dot_nt(grad_ffn, fout_s[t, cols, :]) * slope).astype(BF16)
            kv_s[c // 2, rows, half] = grad_inner
            pffb_s[t:t + 1, cols] += jnp.sum(grad_inner.astype(F32), 0, keepdims=True)
            grad_hidden = grad_hidden + dot_nt(grad_inner, fin_s[t, :, cols])
        win_s[0, rows, 1536:2304] = kept.astype(BF16)
        n1 = (hidden.astype(F32) - biases_ref[3, t:t + 1, :]) / g0
        psum_s[t, 0:1, :] += total(grad_hidden * n1)
        psum_s[t, 5:6, :] += total(grad_hidden)
        grad_attn = norm_back(grad_hidden, g0, n1, inv1).astype(BF16)
        win_s[0, rows, 0:768] = grad_attn
        psum_s[t, 4:5, :] += total(grad_attn.astype(F32))
        gm = dot_nt(grad_attn, wout_s[t]).astype(BF16)
        win_s[0, rows, 768:1536] = gm
        psum_s[t, 3:4, :] += total(gm.astype(F32))

    i1q, i2q = decode_inv(ext_q)
    i1p, i2p = decode_inv(ext_p)
    for blk in range(2):
        lo = blk * 256
        chain(
            0, query_up(slice(lo, lo + 256)),
            ga[8 * blk:8 * blk + 8, 64:96].reshape(256, 768),
            ga[8 * blk:8 * blk + 8, 0:32].reshape(256, 768),
            i1q[lo:lo + 256], i2q[lo:lo + 256], slice(lo, lo + 256), 256,
        )
        if blk == 0:
            own[0].wait()
            for c in first:
                c.wait()
            for c in second:
                c.start()
    hv = ga[:, 32:48].astype(F32)
    chain(
        1, upp_s[...], hv[:, 0:8].reshape(128, 768).astype(BF16),
        hv[:, 8:16].reshape(128, 768).astype(BF16), i1p, i2p, slice(QR, QR + PR), 128,
    )
    for c in plane:
        c.wait()
    add_plane()
    for c in column:
        c.start()
    for c in second:
        c.wait()
    for c in third:
        c.start()

    for t, rows in enumerate((slice(0, QR), slice(QR, QR + PR))):
        count = rows.stop - rows.start
        fo_at = pl.multiple_of(1536 + lax.rem(me // 2, 2) * 384, 128)
        win_s[1, 0:384, 0:count] = win_s[0, rows, pl.ds(fo_at, 384)].astype(F32).T.astype(BF16)
        fo_row = pl.multiple_of(lax.rem(me, 2) * 192, 16)
        pfout_s[t] = dot(win_s[1, pl.ds(fo_row, 192), 0:count], x_s[1, rows, :]).astype(BF16)
        fi_at = pl.multiple_of((me // 8) * 384, 128)
        if t == 0:
            hid = ga[:, 64:96, pl.ds(fi_at, 384)].reshape(QR, 384)
        else:
            hid = ga[:, 32:48, pl.ds(fi_at, 384)].astype(F32)[:, 0:8].reshape(PR, 384)
        win_s[1, 0:384, 768:768 + count] = hid.astype(F32).T.astype(BF16)
        fi_row = pl.multiple_of(lax.rem(me, 8) * 48, 16)
        lhs = win_s[1, pl.ds(fi_row, 48), 768:768 + count]
        for h in range(2):
            pfin_s[t, :, 1536 * h:1536 * h + 1536] = dot(lhs, kv_s[h, rows, :]).astype(BF16)
        if t == 0:
            mx = rsw_ref[:, 0:32].reshape(QR, 128)
        else:
            mx = rsw_ref[:, 32:48].astype(F32)[:, 0:8].reshape(PR, 128).astype(BF16)
        pwout_s[t] = dot_tn(mx, win_s[0, rows, 0:768])[0:48].astype(BF16)
    for c in early:
        c.start()

    def low_rank(read_t, read_p, out_col):
        acc_s[...] = jnp.zeros(acc_s.shape, F32)
        pad = jnp.zeros((32, 768), F32)

        def source(i, _):
            total = acc_s[...]
            for j in (2 * i, 2 * i + 1):
                even, odd = read_p(j)
                wide = jnp.concatenate([expand_heads(even), pad, expand_heads(odd), pad], 0)
                left = jnp.concatenate([read_t(2 * j), read_t(2 * j + 1)], 1)
                total = total + dot(left, wide.astype(BF16))
            acc_s[...] = total
            return 0

        lax.fori_loop(0, 4, source, 0)
        pwin_s[1, :, out_col:out_col + 768] = acc_s[...].astype(BF16)

    def gm_p(j):
        both = win_s[0, pl.ds(pl.multiple_of(QR + j * 16, 16), 16), 768:1536].astype(F32)
        return both[0:8], both[8:16]

    low_rank(lambda i: rsw_ref[i, 48:96, :], gm_p, 1536)

    for c in third:
        c.wait()
    for c in rows_swap:
        c.wait()
    own[1].wait()

    def q_p(j):
        return tuple(ga[2 * j + u, 48:64, :].astype(F32)[0:8] for u in range(2))

    low_rank(lambda i: ryt_s[i], q_p, 768)
    rg_q = rgq_s[:, :, 0:32].reshape(QR, 768)
    rg_p = rgq_s[:, :, 32:48].astype(F32)[:, :, 0:8].reshape(PR, 768)
    pwin_s[0, :, 0:768] = dot_tn(rsw_ref[:, 0:32].reshape(QR, 128), rg_q)[64:112].astype(BF16)
    x_p = rsw_ref[:, 32:48].astype(F32)[:, 0:8].reshape(PR, 128).astype(BF16)
    pwin_s[1, :, 0:768] = dot_tn(x_p, rg_p.astype(BF16))[64:112].astype(BF16)
    for c in column:
        c.wait()
    pwin_s[0, :, pl.ds(pl.multiple_of(768 + 768 * g, 128), 768)] = (
        s2_s[z].astype(F32) + r2_s[0].astype(F32) + r2_s[1].astype(F32) + r2_s[2].astype(F32)
    ).astype(BF16)
    pwin_s[0, :, pl.ds(pl.multiple_of(1536 - 768 * g, 128), 768)] = jnp.zeros((48, 768), BF16)
    psum_s[0, 2:3, :] = jnp.sum(rg_q.astype(F32), 0, keepdims=True)
    psum_s[1, 2:3, :] = jnp.sum(rg_p, 0, keepdims=True)
    for c in late:
        c.start()
    for c in early + late:
        c.wait()
    save_uw.wait()


def run_forward(xq, xp, lengths, labels, weights):
    attn_in, attn_out, ffn_in, ffn_out, gains, biases, ffn_bias = weights
    tokens = xq.shape[0]
    vm = pl.BlockSpec(memory_space=pltpu.VMEM)
    hb = pl.BlockSpec(memory_space=pl.ANY)
    sds = jax.ShapeDtypeStruct
    parts = [
        sds((2, 48, 2304), BF16), sds((2, 48, 768), BF16), sds((2, 48, 3072), BF16),
        sds((2, 192, 768), BF16), sds((2, 8, 768), F32), sds((2, 3072), F32),
    ]
    return pl.pallas_call(
        forward_kernel,
        out_shape=[
            sds((2, tokens, 768), BF16), sds((960, 768), BF16),
            sds((768, tokens), BF16), sds((192, tokens), BF16),
        ] + parts + parts + [sds((1, 32), F32), sds((40, 768), F32)],
        in_specs=[pl.BlockSpec(memory_space=pltpu.SMEM), vm, vm, vm, vm] + [hb] * 6,
        out_specs=[hb] * 16 + [vm] * 2,
        scratch_shapes=[
            pltpu.VMEM((2, tokens, 768), BF16), pltpu.VMEM((2, tokens, 768), BF16),
            pltpu.VMEM((2, tokens, 1536), BF16),
            pltpu.VMEM((2, 768, 2304), BF16), pltpu.VMEM((2, 768, 768), BF16),
            pltpu.VMEM((2, 768, 3072), BF16), pltpu.VMEM((2, 3072, 768), BF16),
            pltpu.VMEM((384, tokens), F32), pltpu.VMEM((96, tokens), F32),
            pltpu.VMEM((2, 256, 768), BF16), pltpu.VMEM((256, 768), BF16),
            pltpu.VMEM((256, 512), F32),
            pltpu.VMEM((96, 768), BF16), pltpu.VMEM((16, 96, 128), BF16),
            pltpu.VMEM((4, 4, 96, 768), BF16), pltpu.VMEM((4, 4, 64, 768), BF16), pltpu.VMEM((16, 96, 128), BF16),
            pltpu.VMEM((32, 3072), F32), pltpu.VMEM((8, 3072), F32),
            pltpu.VMEM((32, 128), F32), pltpu.VMEM((8, 128), F32),
            pltpu.VMEM((32, 768), BF16), pltpu.VMEM((384, 768), BF16),
            pltpu.VMEM((512, 256), BF16), pltpu.VMEM((256, 768), BF16), pltpu.VMEM((128, 768), F32),
            pltpu.VMEM((48, 768), BF16), pltpu.VMEM((4, 4, 48, 768), BF16),
            pltpu.VMEM((16, 48, 128), BF16), pltpu.VMEM((16, 48, 128), BF16),
            pltpu.VMEM((768, 768), BF16), pltpu.VMEM((3, 4, 48, 768), BF16),
            pltpu.VMEM((4, 48, 768), BF16), pltpu.VMEM((3, 48, 768), BF16),
            pltpu.VMEM((2, 48, 2304), BF16), pltpu.VMEM((2, 48, 768), BF16), pltpu.VMEM((2, 48, 3072), BF16),
            pltpu.VMEM((2, 192, 768), BF16),
            pltpu.VMEM((2, 8, 768), F32), pltpu.VMEM((2, 3072), F32), pltpu.VMEM((48, 768), F32),
            pltpu.SemaphoreType.DMA((2, 5)), pltpu.SemaphoreType.DMA((4,)), pltpu.SemaphoreType.DMA((7,)),
            pltpu.SemaphoreType.DMA((22,)), pltpu.SemaphoreType.DMA((22,)),
            pltpu.SemaphoreType.DMA((32,)), pltpu.SemaphoreType.DMA((32,)),
            pltpu.SemaphoreType.DMA((7,)), pltpu.SemaphoreType.DMA((7,)),
            pltpu.SemaphoreType.DMA((16,)), pltpu.SemaphoreType.DMA((16,)), pltpu.SemaphoreType.DMA((7,)),
        ],
        compiler_params=pltpu.CompilerParams(
            collective_id=1, has_side_effects=True, vmem_limit_bytes=63 * 1024 * 1024
        ),
        name="forward",
    )(lengths, labels.reshape(1, -1), gains, biases, ffn_bias, xq, xp, attn_in, attn_out, ffn_in, ffn_out)


def finish_kernel(
    lens_ref, loss_in, ext_ref, dspq_hbm, dspp_hbm, uw_hbm, raw_hbm, *refs,
):
    ins, outs, (loss_ref, outq_hbm, outp_hbm, dxq_hbm, dxp_hbm), scratch = (
        refs[:12], refs[12:19], refs[19:24], refs[24:]
    )
    part_s, raw_s, sum_s = scratch[:12], scratch[12], scratch[13:17]
    dx_s, dspq_ref, dspp_ref, uw_ref, psem, rsem, ssem, dsem, osem = scratch[17:]
    me, _ = place()
    raw_in = pltpu.make_async_copy(raw_hbm, raw_s, rsem.at[2])
    raw_out = [pltpu.make_async_copy(raw_s.at[t], (outq_hbm, outp_hbm)[t], rsem.at[t]) for t in range(2)]
    gets = [
        pltpu.make_async_copy(uw_hbm, uw_ref, osem.at[0]),
        pltpu.make_async_copy(dspq_hbm, dspq_ref, osem.at[1]),
        pltpu.make_async_copy(dspp_hbm, dspp_ref, osem.at[2]),
    ]
    for c in gets:
        c.start()
    raw_in.start()
    loads = [pltpu.make_async_copy(ins[k], part_s[k], psem.at[k]) for k in range(12)]
    for c in loads:
        c.start()
    loss_ref[...] = loss_in[...]

    for c in gets:
        c.wait()
    extra_p = ext_ref[32:40, :]
    e_hi = extra_p.astype(BF16).astype(F32)
    uw_p = jnp.concatenate([uw_ref[768:960, :].astype(F32), e_hi, extra_p - e_hi], 0).astype(BF16)
    keep = []
    for t in range(2):
        for m in range(4):
            cols = slice(256 * m, 256 * m + 256)
            k = t * 4 + m
            if k >= 2:
                keep[k - 2].wait()
            if t == 0:
                dx_s[k % 2] = dot_tn(dspq_ref[:, cols], uw_ref[0:768, :])
                for c in range(8):
                    dx_s[k % 2, 32 * c:32 * c + 1, :] += ext_ref[8 * m + c:8 * m + c + 1, :]
            else:
                colr = iota((8, 256), 1) + 256 * m
                rowr = iota((8, 256), 0)
                start = jnp.zeros((8, 256), jnp.int32)
                for r in range(2):
                    at = jnp.int32(r * 512)
                    for c in range(4):
                        start = jnp.where(rowr == r * 4 + c, at, start)
                        at = at + lens_ref[r, c]
                sel = jnp.where(colr == start, 1.0, 0.0)
                sel2 = jnp.concatenate([sel, sel], 0).astype(BF16)
                lhs = jnp.concatenate([dspp_ref[:, cols], sel2], 0)
                dx_s[k % 2] = dot_tn(lhs, uw_p)
            c = pltpu.make_async_copy(dx_s.at[k % 2], (dxq_hbm, dxp_hbm)[t].at[cols], dsem.at[k % 2])
            c.start()
            keep.append(c)
            if k == 1:
                raw_in.wait()
                for c in raw_out:
                    c.start()

    stores = []
    for k in range(4):
        loads[k].wait()
        loads[6 + k].wait()
        sum_s[k][...] = part_s[k][...].astype(F32) + part_s[6 + k][...].astype(F32)
        c = pltpu.make_async_copy(sum_s[k], outs[k], ssem.at[k])
        c.start()
        stores.append(c)
    for k in (4, 5, 10, 11):
        loads[k].wait()
    shift = lax.rem(768 - 48 * me, 768)
    for t in range(2):
        sums = pltpu.roll(part_s[4][t] + part_s[10][t], shift, 1)[:, 0:48]
        outs[4][t] = sums[0:2]
        for j in range(6):
            outs[5][j, t:t + 1, :] = sums[2 + j:3 + j]
    ffb = part_s[5][...] + part_s[11][...]
    wide = jnp.concatenate([ffb, jnp.zeros((6, 3072), F32)], 0)
    outs[6][...] = pltpu.roll(wide, lax.rem(3072 - 192 * me, 3072), 1)[0:2, 0:192]
    for c in keep[6:] + stores + raw_out:
        c.wait()


def finish(lengths, loss, dspq, dspp, uw, ext, raw, parts):
    sds = jax.ShapeDtypeStruct
    tokens = dspq.shape[1]
    vm = pl.BlockSpec(memory_space=pltpu.VMEM)
    hb = pl.BlockSpec(memory_space=pl.ANY)
    return pl.pallas_call(
        finish_kernel,
        out_shape=[sds(p.shape, F32) for p in parts[:4]]
        + [sds((2, 2, 48), F32), sds((6, 2, 48), F32), sds((2, 192), F32)]
        + [sds((1, 32), F32), sds((tokens, 768), BF16), sds((tokens, 768), BF16)]
        + [sds((tokens, 768), F32), sds((tokens, 768), F32)],
        in_specs=[pl.BlockSpec(memory_space=pltpu.SMEM)] + [vm] * 2 + [hb] * 16,
        out_specs=[hb] * 4 + [vm] * 4 + [hb] * 4,
        scratch_shapes=[pltpu.VMEM(p.shape, p.dtype) for p in parts]
        + [pltpu.VMEM((2, tokens, 768), BF16)]
        + [pltpu.VMEM(p.shape, F32) for p in parts[:4]]
        + [pltpu.VMEM((2, 256, 768), F32), pltpu.VMEM((768, tokens), BF16)]
        + [pltpu.VMEM((192, tokens), BF16), pltpu.VMEM((960, 768), BF16)]
        + [pltpu.SemaphoreType.DMA((n,)) for n in (12, 3, 4, 2, 3)],
        compiler_params=pltpu.CompilerParams(vmem_limit_bytes=VMEM_LIMIT),
        name="finish",
    )(lengths, loss, ext, dspq, dspp, uw, raw, *parts)


def fast_shards(query_tokens, passage_tokens, lengths, labels, *weights):
    xq = query_tokens.reshape(-1, 768)
    xp = passage_tokens.reshape(-1, 768)
    weights = weights[:5] + (weights[5].transpose(1, 0, 2), weights[6])
    raw, uw, dspq, dspp, *parts, loss, ext = run_forward(xq, xp, lengths, labels, weights)
    win, wout, fin, fout, gains, biases, ffb, loss, outq, outp, dxq, dxp = finish(
        lengths, loss, dspq, dspp, uw, ext, raw, parts
    )
    return (
        loss.reshape(-1),
        outq.reshape(query_tokens.shape),
        outp.reshape(passage_tokens.shape),
        dxq.reshape(query_tokens.shape),
        dxp.reshape(passage_tokens.shape),
        win, wout, fin, fout, gains, biases.transpose(1, 0, 2), ffb,
    )


def layer_norm(residual, gain_vec, shift_vec):
    centre = residual - jnp.mean(residual, -1, keepdims=True)
    inverse = lax.rsqrt(jnp.mean(centre * centre, -1, keepdims=True) + EPSILON)
    return centre * inverse * gain_vec + shift_vec


def plain_norm_back(residual, gain_vec, upstream):
    centre = residual - jnp.mean(residual, -1, keepdims=True)
    inverse = lax.rsqrt(jnp.mean(centre * centre, -1, keepdims=True) + EPSILON)
    normed = centre * inverse
    scaled = upstream * gain_vec
    grad_res = inverse * (
        scaled
        - jnp.mean(scaled, -1, keepdims=True)
        - normed * jnp.mean(scaled * normed, -1, keepdims=True)
    )
    return (grad_res, jnp.sum(upstream * normed, 0), jnp.sum(upstream, 0))


def cls_index(starts, seq_len):
    return (jnp.arange(starts.shape[0], dtype=jnp.int32)[:, None] * seq_len + starts).reshape(-1)


def forward(tokens, segment, starts, params):
    attn_in, attn_out, ffn_in, ffn_out, gains, biases, ffn_bias = params
    batch_size, seq_len, feature = tokens.shape
    head_count = feature // HEAD_DIM
    flat_tokens = tokens.reshape(batch_size * seq_len, feature)
    zeros_vec = jnp.zeros_like(biases[0])
    joined = jnp.dot(flat_tokens, attn_in, preferred_element_type=jnp.float32) + jnp.concatenate(
        [biases[0], zeros_vec, biases[1]]
    )
    joined = joined.astype(jnp.bfloat16)
    shaped = joined.reshape(batch_size, seq_len, 3, head_count, HEAD_DIM)
    scores = (
        jnp.einsum(
            "bqhd,bkhd->bhqk", shaped[:, :, 0], shaped[:, :, 1], preferred_element_type=jnp.float32
        )
        * KEY_SCALE
    )
    same_seg = segment[:, :, None] == segment[:, None, :]
    scores = jnp.where(same_seg[:, None], scores, -1000000000.0)
    attention = jax.nn.softmax(scores, -1).astype(jnp.bfloat16)
    mixed = jnp.einsum(
        "bhqk,bkhd->bqhd", attention, shaped[:, :, 2], preferred_element_type=jnp.float32
    )
    mixed = mixed.reshape(batch_size * seq_len, feature).astype(jnp.bfloat16)
    first_sum = flat_tokens.astype(jnp.float32) + (
        jnp.dot(mixed, attn_out, preferred_element_type=jnp.float32) + biases[2]
    )
    hidden = layer_norm(first_sum, gains[0], biases[3]).astype(jnp.bfloat16)
    inner = jnp.dot(hidden, ffn_in, preferred_element_type=jnp.float32) + ffn_bias
    active = jax.nn.gelu(inner).astype(jnp.bfloat16)
    second_sum = hidden.astype(jnp.float32) + (
        jnp.dot(active, ffn_out, preferred_element_type=jnp.float32) + biases[4]
    )
    output = layer_norm(second_sum, gains[1], biases[5]).astype(jnp.bfloat16)
    picked = cls_index(starts, seq_len)
    kept = (
        flat_tokens,
        joined,
        mixed[picked],
        first_sum[picked],
        hidden[picked],
        inner[picked],
        active[picked],
        second_sum[picked],
    )
    return (output, picked, kept)


def backward(kept, segment, starts, params, upstream):
    attn_in, attn_out, ffn_in, ffn_out, gains, biases, ffn_bias = params
    flat_tokens, joined, mixed_cls, first_cls, hidden_cls, inner_cls, active_cls, second_cls = kept
    batch_size, seq_len = segment.shape
    per_row = starts.shape[1]
    feature = flat_tokens.shape[1]
    head_count = feature // HEAD_DIM
    grad_second, gain_two, shift_two = plain_norm_back(second_cls, gains[1], upstream)
    grad_ffn = grad_second.astype(jnp.bfloat16)
    grad_down = jnp.dot(active_cls.T, grad_ffn, preferred_element_type=jnp.float32)
    grad_active = jnp.dot(grad_ffn, ffn_out.T, preferred_element_type=jnp.float32)
    grad_inner = jax.vjp(jax.nn.gelu, inner_cls)[1](grad_active)[0].astype(jnp.bfloat16)
    grad_up = jnp.dot(hidden_cls.T, grad_inner, preferred_element_type=jnp.float32)
    grad_hidden = grad_second + jnp.dot(grad_inner, ffn_in.T, preferred_element_type=jnp.float32)
    grad_first, gain_one, shift_one = plain_norm_back(first_cls, gains[0], grad_hidden)
    grad_attn = grad_first.astype(jnp.bfloat16)
    grad_outproj = jnp.dot(mixed_cls.T, grad_attn, preferred_element_type=jnp.float32)
    grad_mixed = jnp.dot(grad_attn, attn_out.T, preferred_element_type=jnp.float32).astype(
        jnp.bfloat16
    )
    grad_mixed = grad_mixed.reshape(batch_size, per_row, head_count, HEAD_DIM)
    shaped = joined.reshape(batch_size, seq_len, 3, head_count, HEAD_DIM)
    key_part = shaped[:, :, 1]
    value_part = shaped[:, :, 2]
    picked = cls_index(starts, seq_len)
    query_cls = joined[picked, :feature].reshape(batch_size, per_row, head_count, HEAD_DIM)
    own_seg = jnp.take_along_axis(segment, starts, 1)
    scores = (
        jnp.einsum("bchd,bkhd->bhck", query_cls, key_part, preferred_element_type=jnp.float32)
        * KEY_SCALE
    )
    scores = jnp.where((own_seg[:, :, None] == segment[:, None, :])[:, None], scores, -1000000000.0)
    attention = jax.nn.softmax(scores, -1)
    grad_attention = jnp.einsum(
        "bchd,bkhd->bhck", grad_mixed, value_part, preferred_element_type=jnp.float32
    )
    grad_scores = attention * (
        grad_attention - jnp.sum(attention * grad_attention, -1, keepdims=True)
    )
    grad_scores = grad_scores.astype(jnp.bfloat16)
    grad_query = (
        jnp.einsum("bhck,bkhd->bchd", grad_scores, key_part, preferred_element_type=jnp.float32)
        * KEY_SCALE
    ).astype(jnp.bfloat16)
    grad_key = (
        jnp.einsum("bhck,bchd->bkhd", grad_scores, query_cls, preferred_element_type=jnp.float32)
        * KEY_SCALE
    ).astype(jnp.bfloat16)
    grad_value = jnp.einsum(
        "bhck,bchd->bkhd",
        attention.astype(jnp.bfloat16),
        grad_mixed,
        preferred_element_type=jnp.float32,
    ).astype(jnp.bfloat16)
    places = jnp.arange(seq_len, dtype=jnp.int32)
    selector = (starts[:, :, None] == places[None, None, :]).astype(jnp.bfloat16)
    grad_query_full = jnp.einsum(
        "bcl,bchd->blhd", selector, grad_query, preferred_element_type=jnp.float32
    ).astype(jnp.bfloat16)
    grad_joined = jnp.stack([grad_query_full, grad_key, grad_value], 2).reshape(
        batch_size * seq_len, 3 * feature
    )
    grad_inproj = jnp.dot(flat_tokens.T, grad_joined, preferred_element_type=jnp.float32)
    grad_tokens = (
        jnp.dot(grad_joined, attn_in.T, preferred_element_type=jnp.float32)
        .at[picked]
        .add(grad_first)
    )
    bias_grads = jnp.stack(
        [
            jnp.sum(grad_query.astype(jnp.float32), (0, 1)).reshape(feature),
            jnp.sum(grad_value.astype(jnp.float32), (0, 1)).reshape(feature),
            jnp.sum(grad_attn.astype(jnp.float32), 0),
            shift_one,
            jnp.sum(grad_ffn.astype(jnp.float32), 0),
            shift_two,
        ]
    )
    gain_grads = jnp.stack([gain_one, gain_two])
    hidden_bias = jnp.sum(grad_inner.astype(jnp.float32), 0)
    grads = (grad_inproj, grad_outproj, grad_up, grad_down, gain_grads, bias_grads, hidden_bias)
    row_data = (hidden_cls, grad_inner, active_cls, grad_ffn)
    return (grads, grad_tokens.reshape(batch_size, seq_len, feature), row_data)


def shards(
    query_tokens,
    passage_tokens,
    lengths,
    labels,
    attn_in,
    attn_out,
    ffn_in,
    ffn_out,
    gains,
    biases,
    ffn_bias,
):
    layers = (attn_in, attn_out, ffn_in, ffn_out, gains, biases, ffn_bias)
    query_params = tuple((matrix[0] for matrix in layers))
    passage_params = tuple((matrix[1] for matrix in layers))
    query_count, query_len, feature = query_tokens.shape
    passage_len = passage_tokens.shape[1]
    query_segment = jnp.zeros((query_count, query_len), jnp.int32)
    query_starts = jnp.zeros((query_count, 1), jnp.int32)
    ends = jnp.cumsum(lengths, -1)
    passage_starts = ends - lengths
    places = jnp.arange(passage_len, dtype=jnp.int32)
    passage_segment = jnp.sum((places[None, :, None] >= ends[:, None, :]).astype(jnp.int32), -1)
    query_out, query_pick, query_kept = forward(
        query_tokens, query_segment, query_starts, query_params
    )
    passage_out, passage_pick, passage_kept = forward(
        passage_tokens, passage_segment, passage_starts, passage_params
    )
    query_vec = query_out[query_pick]
    passage_vec = passage_out[passage_pick]
    passage_count = passage_vec.shape[0]
    float_labels = labels.astype(jnp.float32)
    group_vec = lax.all_gather(passage_vec, "grp", axis=0, tiled=True)
    portion = lax.all_gather(group_vec, "blk", axis=0, tiled=True)
    running_max = jnp.full((query_count,), -1e30, jnp.float32)
    score_block = SCORE_SCALE * jnp.dot(query_vec, portion.T, preferred_element_type=jnp.float32)
    column_ids = jnp.arange(portion.shape[0], dtype=jnp.int32)
    new_max = jnp.maximum(running_max, jnp.max(score_block, -1))
    running_sum = jnp.sum(jnp.exp(score_block - new_max[:, None]), -1)
    hits = column_ids[None, :] == labels[:, None]
    positive = jnp.sum(jnp.where(hits, score_block, 0.0), -1)
    running_max, running_sum, positive = (new_max, running_sum, positive)
    norm_log = running_max + jnp.log(running_sum)
    portion = lax.all_gather(group_vec, "blk", axis=0, tiled=True)
    score_block = SCORE_SCALE * jnp.dot(query_vec, portion.T, preferred_element_type=jnp.float32)
    column_ids = jnp.arange(portion.shape[0], dtype=jnp.int32)
    hits = (column_ids[None, :] == labels[:, None]).astype(jnp.float32)
    grad_block = (jnp.exp(score_block - norm_log[:, None]) - hits).astype(jnp.bfloat16)
    query_up = SCORE_SCALE * jnp.dot(grad_block, portion, preferred_element_type=jnp.float32)
    own_ids = (
        lax.axis_index(("blk", "grp")) * passage_count + jnp.arange(passage_count, dtype=jnp.int32)
    ).astype(jnp.float32)
    remote_vec = lax.all_gather(query_vec.astype(jnp.float32), ("blk", "grp"), axis=0, tiled=True)
    remote_log = lax.all_gather(norm_log, ("blk", "grp"), axis=0, tiled=True)
    remote_label = lax.all_gather(float_labels, ("blk", "grp"), axis=0, tiled=True)
    remote_low = remote_vec.astype(jnp.bfloat16)
    score_block = SCORE_SCALE * jnp.dot(
        remote_low, passage_vec.T, preferred_element_type=jnp.float32
    )
    hits = (remote_label[:, None] == own_ids[None, :]).astype(jnp.float32)
    grad_block = (jnp.exp(score_block - remote_log[:, None]) - hits).astype(jnp.bfloat16)
    passage_up = SCORE_SCALE * jnp.dot(grad_block.T, remote_low, preferred_element_type=jnp.float32)
    query_losses = norm_log - positive
    query_grads, query_back, query_rows = backward(
        query_kept, query_segment, query_starts, query_params, query_up
    )
    passage_grads, passage_back, passage_rows = backward(
        passage_kept, passage_segment, passage_starts, passage_params, passage_up
    )
    stacked = tuple(
        (
            jnp.stack([first_part, second_part])
            for first_part, second_part in zip(query_grads, passage_grads)
        )
    )
    grad_win, grad_wout, grad_up, grad_down, grad_gain, grad_bias, grad_hidden_bias = stacked
    shares = (
        lax.psum_scatter(
            grad_win.astype(jnp.bfloat16), "blk", scatter_dimension=1, tiled=True
        ).astype(jnp.float32),
        lax.psum_scatter(
            grad_wout.astype(jnp.bfloat16), "blk", scatter_dimension=1, tiled=True
        ).astype(jnp.float32),
        lax.psum_scatter(
            grad_up.astype(jnp.bfloat16), "blk", scatter_dimension=1, tiled=True
        ).astype(jnp.float32),
        lax.psum_scatter(
            grad_down.astype(jnp.bfloat16), "blk", scatter_dimension=1, tiled=True
        ).astype(jnp.float32),
        lax.psum_scatter(
            grad_gain.astype(jnp.bfloat16), "blk", scatter_dimension=2, tiled=True
        ).astype(jnp.float32),
        lax.psum_scatter(
            grad_bias.astype(jnp.bfloat16), "blk", scatter_dimension=2, tiled=True
        ).astype(jnp.float32),
        lax.psum_scatter(
            grad_hidden_bias.astype(jnp.bfloat16), "blk", scatter_dimension=1, tiled=True
        ).astype(jnp.float32),
    )
    grad_win, grad_wout, grad_up, grad_down, grad_gain, grad_bias, grad_hidden_bias = (
        lax.psum(shares[0].astype(jnp.bfloat16), "grp").astype(jnp.float32),
        lax.psum(shares[1].astype(jnp.bfloat16), "grp").astype(jnp.float32),
        lax.psum(shares[2].astype(jnp.bfloat16), "grp").astype(jnp.float32),
        lax.psum(shares[3].astype(jnp.bfloat16), "grp").astype(jnp.float32),
        lax.psum(shares[4].astype(jnp.bfloat16), "grp").astype(jnp.float32),
        lax.psum(shares[5].astype(jnp.bfloat16), "grp").astype(jnp.float32),
        lax.psum(shares[6].astype(jnp.bfloat16), "grp").astype(jnp.float32),
    )
    query_shaped = query_out.reshape(query_count, query_len, feature)
    passage_shaped = passage_out.reshape(passage_tokens.shape)
    return (
        query_losses,
        query_shaped,
        passage_shaped,
        query_back,
        passage_back,
        grad_win,
        grad_wout,
        grad_up,
        grad_down,
        grad_gain,
        grad_bias,
        grad_hidden_bias,
    )


def solution(mesh):
    placed = (
        P(("blk", "grp"), None, None),
        P(("blk", "grp"), None, None),
        P(("blk", "grp"), None),
        P(("blk", "grp")),
        P(),
        P(),
        P(),
        P(),
        P(),
        P(),
        P(),
    )
    small = dict(mesh.shape) == {"blk": 16, "grp": 2}
    return jax.shard_map(
        fast_shards if small else shards,
        mesh=mesh,
        in_specs=placed,
        out_specs=(
            P(("blk", "grp")),
            P(("blk", "grp"), None, None),
            P(("blk", "grp"), None, None),
            P(("blk", "grp"), None, None),
            P(("blk", "grp"), None, None),
            P(None, "blk", None),
            P(None, "blk", None),
            P(None, "blk", None),
            P(None, "blk", None),
            P(None, None, "blk"),
            P(None, None, "blk"),
            P(None, "blk"),
        ),
        check_vma=False,
    )
```

```python
import functools
import jax
import jax.numpy as jnp
from jax import lax
from jax.experimental import pallas as pl
from jax.experimental.pallas import tpu as pltpu
from jax.sharding import PartitionSpec as P

MESH = pl.DeviceIdType.MESH
HEAD_DIM = 64
HEADS = 12
EPSILON = 1e-05
SCORE_SCALE = 0.08
KEY_SCALE = 0.125
NEG = -1000000000.0
GELU_A = 0.7978845608028654
GELU_B = 0.044715 * GELU_A
F32 = jnp.float32
BF16 = jnp.bfloat16
VMEM_LIMIT = 60 * 1024 * 1024


def dot(a, b):
    return lax.dot_general(a, b, (((1,), (0,)), ((), ())), preferred_element_type=F32)


def dot_nt(a, b):
    return lax.dot_general(a, b, (((1,), (1,)), ((), ())), preferred_element_type=F32)


def dot_tn(a, b):
    return lax.dot_general(a, b, (((0,), (0,)), ((), ())), preferred_element_type=F32)


def iota(shape, dim):
    return lax.broadcasted_iota(jnp.int32, shape, dim)


def head_row(h):
    return iota((1, 768), 1) // HEAD_DIM == h


def expand_heads(rows, h0=0, heads=HEADS):
    return jnp.concatenate(
        [jnp.where(head_row(h0 + h), rows, 0.0) for h in range(heads)], 0
    )


def fold_heads(rows, count, h0=0, heads=HEADS):
    out = jnp.where(head_row(h0), rows[:count], 0.0)
    for h in range(1, heads):
        out = out + jnp.where(head_row(h0 + h), rows[h * count:(h + 1) * count], 0.0)
    return out


def norm_stats(residual):
    centre = residual - jnp.mean(residual, -1, keepdims=True)
    inverse = lax.rsqrt(jnp.mean(centre * centre, -1, keepdims=True) + EPSILON)
    return centre * inverse, inverse


def gelu(v):
    half = 0.5 + 0.5 * jnp.tanh(v * (GELU_A + GELU_B * (v * v)))
    return v * half


def split3(v):
    hi = v.astype(BF16).astype(F32)
    rest = v - hi
    mid = rest.astype(BF16).astype(F32)
    return hi, mid, rest - mid


def lane_pack(columns, count):
    lane = iota((count, 128), 1)
    out = jnp.zeros((count, 128), F32)
    for j, column in enumerate(columns):
        out = jnp.where(lane == j, column, out)
    return out


def norm_back(up, gain, normed, inverse):
    u = up * gain
    return inverse * (
        u - jnp.mean(u, -1, keepdims=True) - normed * jnp.mean(u * normed, -1, keepdims=True)
    )


def gelu_pair(v):
    sq = v * v
    half = 0.5 + 0.5 * jnp.tanh(v * (GELU_A + GELU_B * sq))
    value = v * half
    return value, half + (value - value * half) * (2.0 * GELU_A + 6.0 * GELU_B * sq)


def decode_inv(ext):
    return ext[:, 0:1] + ext[:, 1:2] + ext[:, 2:3], ext[:, 3:4] + ext[:, 4:5] + ext[:, 5:6]


def ext_rows(block):
    e_p = block[:, :, 0:128].reshape(128, 128)
    e_q = jnp.concatenate([block[:, :, 128 * a:128 * a + 128] for a in range(1, 5)], 1)
    return e_p, e_q.reshape(512, 128)


def place():
    return lax.axis_index("blk"), lax.axis_index("grp")


def remote(src, dst, send, recv, peer):
    return pltpu.make_async_remote_copy(
        src_ref=src, dst_ref=dst, send_sem=send, recv_sem=recv, device_id=peer, device_id_type=MESH
    )


def greet(me, g):
    barrier = pltpu.get_barrier_semaphore()
    for i in range(1, 16):
        pl.semaphore_signal(barrier, inc=1, device_id=(lax.rem(me + i, 16), g), device_id_type=MESH)
    pl.semaphore_signal(barrier, inc=1, device_id=(me, 1 - g), device_id_type=MESH)


def greeted():
    pl.semaphore_wait(pltpu.get_barrier_semaphore(), 16)


def gather_phases(me, g, pay, ga, ss, rs, base, lo, hi):
    z, yx = me // 4, lax.rem(me, 4)
    xpeer = me + 1 - 2 * lax.rem(me, 2)
    ypeer = me + 2 - 4 * (lax.rem(me, 4) // 2)
    yx_x, yx_y = lax.rem(xpeer, 4), lax.rem(ypeer, 4)
    rows = slice(lo, hi)
    first, second, third = [], [], []

    def add(phase, src, dst, k, peer):
        phase.append(remote(src, dst, ss.at[base + k], rs.at[base + k], (peer, g)))

    for d in range(1, 4):
        peer = lax.rem(z + d, 4) * 4 + yx
        add(first, pay.at[rows], ga.at[z, yx, rows], d - 1, peer)
    add(second, ga.at[:, yx, rows], ga.at[:, yx, rows], 3, xpeer)
    add(second, ga.at[:, yx, rows], ga.at[:, yx, rows], 4, ypeer)
    add(third, ga.at[0:2, yx_x, rows], ga.at[0:2, yx_x, rows], 5, ypeer)
    add(third, ga.at[2:4, yx_y, rows], ga.at[2:4, yx_y, rows], 6, xpeer)
    return first, second, third


QR, PR = 512, 128


def forward_kernel(
    lens_ref, labels_ref, gains_ref, biases_ref, ffnb_ref,
    xq_hbm, xp_hbm, win_hbm, wout_hbm, fin_hbm, fout_hbm,
    out_hbm, uw_hbm, dspq_hbm, dspp_hbm,
    pwin_hbm, pwout_hbm, pfin_hbm, pfout_hbm, psum_hbm, pffb_hbm,
    swin_hbm, swout_hbm, sfin_hbm, sfout_hbm, ssum_hbm, sffb_hbm,
    loss_ref, ext_ref,
    x_s, q_s, kv_s, win_s, wout_s, fin_s, fout_s, pq_s, pp_s, out_s, mix_s, bias_s,
    pay_s, swap_s, ga_ref, gs_ref, rsw_ref, innq_ref, innp_ref, invq_ref, invp_ref, qq_ref, zq_ref,
    grad_s, upp_s, gq_s, rgq_s, yt_s, ryt_s, sib_s, r1_s, s2_s, r2_s,
    pwin_s, pwout_s, pfin_s, pfout_s, psum_s, pffb_s, acc_s,
    sem, lsem, osem, ss, rs, as_, ar, xs, xr, ks, kr, psem,
):
    me, g = place()
    z, yx = me // 4, lax.rem(me, 4)
    greet(me, g)
    copies = []
    for t, x_hbm in enumerate((xq_hbm, xp_hbm)):
        copies.append([
            pltpu.make_async_copy(x_hbm, x_s.at[t], sem.at[t, 0]),
            pltpu.make_async_copy(win_hbm.at[t], win_s.at[t], sem.at[t, 1]),
            pltpu.make_async_copy(wout_hbm.at[t], wout_s.at[t], sem.at[t, 2]),
            pltpu.make_async_copy(fin_hbm.at[t], fin_s.at[t], sem.at[t, 3]),
            pltpu.make_async_copy(fout_hbm.at[t], fout_s.at[t], sem.at[t, 4]),
        ])
    for c in copies[0][:2] + copies[1][:2] + copies[0][2:] + copies[1][2:]:
        c.start()
    a1, b1, c1 = gather_phases(me, g, pay_s, ga_ref, ss, rs, 0, 0, 64)
    a2, b2, c2 = gather_phases(me, g, pay_s, ga_ref, ss, rs, 7, 64, 96)
    last_hop = [remote(ga_ref.at[:, :, 0:64], gs_ref, ss.at[14], rs.at[14], (me, 1 - g))]
    swaps = []
    for i in range(1, 16):
        peer = lax.rem(me + i, 16)
        swaps.append(remote(swap_s.at[peer], rsw_ref.at[me], as_.at[i], ar.at[i], (peer, g)))
    own_copy = [
        pltpu.make_async_copy(pay_s, ga_ref.at[z, yx], lsem.at[0]),
        pltpu.make_async_copy(swap_s.at[me], rsw_ref.at[me], lsem.at[1]),
    ]

    tokens = x_s.shape[1]
    col_q = iota((32, tokens), 1)
    row_q = iota((32, tokens), 0)
    sel_q = col_q == row_q * 32
    own_q = col_q // 32 == row_q
    col_p = iota((8, tokens), 1)
    row_p = iota((8, tokens), 0)
    lo = jnp.zeros((8, tokens), jnp.int32)
    hi = jnp.zeros((8, tokens), jnp.int32)
    for r in range(2):
        acc = jnp.int32(r * 512)
        for c in range(4):
            length = lens_ref[r, c]
            lo = jnp.where(row_p == r * 4 + c, acc, lo)
            acc = acc + length
            hi = jnp.where(row_p == r * 4 + c, acc, hi)
    sel_p = col_p == lo
    own_p = (col_p >= lo) & (col_p < hi)

    picks = []
    for t, sel in enumerate((sel_q, sel_p)):
        copies[t][0].wait()
        copies[t][1].wait()
        query_bias = biases_ref[0, t:t + 1, :]
        value_bias = biases_ref[1, t:t + 1, :]

        def kv_step(m, _, t=t, query_bias=query_bias, value_bias=value_bias):
            rows = pl.ds(pl.multiple_of(m * 256, 256), 256)
            x = x_s[t, rows, :]
            kv_s[t, rows, 0:768] = dot(x, win_s[t, :, 768:1536]).astype(BF16)
            kv_s[t, rows, 768:1536] = (dot(x, win_s[t, :, 1536:2304]) + value_bias).astype(BF16)
            q_s[t, rows, :] = (dot(x, win_s[t, :, 0:768]) + query_bias).astype(BF16)
            return 0

        lax.fori_loop(0, tokens // 256, kv_step, 0)
        pick = jnp.where(sel, 1.0, 0.0).astype(BF16)
        picks.append((dot(pick, x_s[t]), dot(pick, q_s[t])))

    done = []
    for t, (own, count, p_s, inn_ref, inv_ref) in enumerate((
        (own_q, 32, pq_s, innq_ref, invq_ref), (own_p, 8, pp_s, innp_ref, invp_ref),
    )):
        xc, qc = picks[t]
        mixed = jnp.zeros((count, 768), F32)
        heads = 4 if t == 0 else HEADS
        mask = jnp.concatenate([jnp.where(own, 0.0, NEG)] * heads, 0)
        for h0 in range(0, HEADS, heads):
            span = slice(h0 * count, (h0 + heads) * count)
            spread = expand_heads(qc, h0, heads).astype(BF16)
            scores = dot_nt(spread, kv_s[t, :, 0:768]) * KEY_SCALE + mask
            weight = jnp.exp(scores - jnp.max(scores, -1, keepdims=True))
            soft = weight * (1.0 / jnp.sum(weight, -1, keepdims=True))
            p_s[span, :] = soft
            soft16 = soft.astype(BF16)
            mixed = mixed + fold_heads(dot(soft16, kv_s[t, :, 768:1536]), count, h0, heads)
            zsum = dot(soft16, x_s[t])
            if t == 0:
                zq_ref[span, :] = zsum.astype(BF16)
            else:
                wide = jnp.concatenate([zsum, jnp.zeros((32, 768), F32)], 0)
                swap_s[:, 48:96, :] = wide.T.astype(BF16).reshape(16, 48, 128)
        mixed = mixed.astype(BF16)
        copies[t][2].wait()
        first = xc + (dot(mixed, wout_s[t]) + biases_ref[2, t:t + 1, :])
        n1, inv1 = norm_stats(first)
        hidden = (n1 * gains_ref[t, 0:1, :] + biases_ref[3, t:t + 1, :]).astype(BF16)
        copies[t][3].wait()
        inner = dot(hidden, fin_s[t]) + ffnb_ref[t:t + 1, :]
        inn_ref[...] = inner
        active = gelu(inner).astype(BF16)
        copies[t][4].wait()
        second = hidden.astype(F32) + (dot(active, fout_s[t]) + biases_ref[4, t:t + 1, :])
        n2, inv2 = norm_stats(second)
        vec = (n2 * gains_ref[t, 1:2, :] + biases_ref[5, t:t + 1, :]).astype(BF16)
        inv_ref[...] = lane_pack([inv1, inv2], count)
        done.append((xc, qc, mixed, hidden, vec, inv1, inv2))

    xq, qq, mq, hq, vq, i1q, i2q = done[0]
    xp, qp, mp, hp, vp, i1p, i2p = done[1]
    lab = labels_ref[...].astype(F32)
    eye = iota((32, 32), 0) == iota((32, 32), 1)
    lab_col = jnp.sum(jnp.where(eye, lab, 0.0), 1, keepdims=True)
    lab_hi = jnp.floor(lab_col * (1.0 / 256.0))
    lab_lo = lab_col - 256.0 * lab_hi
    ext_q = lane_pack([*split3(i1q), *split3(i2q), lab_hi, lab_lo], 32)
    ext_p = lane_pack([*split3(i1p), *split3(i2p)], 8)
    ext = jnp.concatenate(
        [ext_p] + [ext_q[8 * a:8 * a + 8] for a in range(4)] + [jnp.zeros((8, 128), F32)], 1
    )
    pay_s[0:32, :] = vq
    pay_s[32:64, :] = jnp.concatenate([hp.astype(F32), vp.astype(F32), qp, ext], 0).astype(BF16)
    pay_s[64:96, :] = hq
    qq_ref[...] = qq.astype(BF16)
    greeted()
    own_copy[0].start()
    for c in a1 + a2:
        c.start()
    m48 = jnp.concatenate([mq.astype(F32), mp.astype(F32), jnp.zeros((8, 768), F32)], 0)
    x48 = jnp.concatenate([xq, xp, jnp.zeros((8, 768), F32)], 0)
    swap_s[:, 0:48, :] = jnp.zeros((16, 48, 128), BF16)
    for b in range(16):
        swap_s[b, 0:48, 0:48] = m48[:, 48 * b:48 * b + 48].astype(BF16)
        swap_s[b, 0:48, 64:112] = x48[:, 48 * b:48 * b + 48].astype(BF16)
    for c in own_copy[1:]:
        c.start()

    low_half = iota((1, 128), 1) < HEAD_DIM

    def tile(step, _):
        tower = step // 4
        rows = pl.ds(pl.multiple_of(lax.rem(step, 4) * 256, 256), 256)

        def on(k, waits, starts):
            @pl.when(step == k)
            def _():
                for c in waits:
                    c.wait()
                for c in starts:
                    c.start()

        on(2, own_copy[0:1] + a1, b1)
        on(3, a2, b2)
        on(4, b1, c1 + swaps)
        on(5, b2, c2)
        on(6, c1, last_hop)

        @pl.when(step < 4)
        def _():
            same = iota((128, 128), 0) // 32 == iota((128, 128), 1) // 32
            mask = jnp.where(same, 0.0, NEG)
            mask2 = jnp.concatenate([mask, mask], 0)
            for part in range(2):
                at = pl.ds(pl.multiple_of(lax.rem(step, 4) * 256 + part * 128, 128), 128)
                for j in range(HEADS // 2):
                    lanes = slice(128 * j, 128 * j + 128)
                    q = q_s[0, at, lanes] * KEY_SCALE
                    k = kv_s[0, at, lanes]
                    v = kv_s[0, at, 768 + 128 * j:768 + 128 * j + 128]
                    zero = jnp.zeros_like(q)
                    q2 = jnp.concatenate([jnp.where(low_half, q, zero), jnp.where(low_half, zero, q)], 0)
                    s = dot_nt(q2, k) + mask2
                    e = jnp.exp(s - jnp.max(s, -1, keepdims=True))
                    total = jnp.sum(e, -1, keepdims=True)
                    o = dot(e.astype(BF16), v) * (1.0 / total)
                    mix_s[part * 128:part * 128 + 128, lanes] = jnp.where(low_half, o[:128], o[128:]).astype(BF16)

        @pl.when(step >= 4)
        def _():
            row = (step - 4) // 2
            base = lax.rem(step, 2) * 256
            keys = pl.ds(pl.multiple_of(row * 512, 512), 512)
            qpos = iota((256, 512), 0) + base
            kpos = iota((256, 512), 1)
            qseg = jnp.zeros((256, 512), jnp.int32)
            kseg = jnp.zeros((256, 512), jnp.int32)
            end = jnp.int32(0)
            for c in range(3):
                end = end + lens_ref[row, c]
                qseg = qseg + jnp.where(qpos >= end, 1, 0)
                kseg = kseg + jnp.where(kpos >= end, 1, 0)
            mask = jnp.where(qseg == kseg, 0.0, NEG)
            bias_s[...] = mask
            for j in range(HEADS // 2):
                lanes = slice(128 * j, 128 * j + 128)
                q = q_s[1, rows, lanes] * KEY_SCALE
                k = kv_s[1, keys, lanes]
                v = kv_s[1, keys, 768 + 128 * j:768 + 128 * j + 128]
                zero = jnp.zeros_like(q)
                halves = []
                for part in (jnp.where(low_half, q, zero), jnp.where(low_half, zero, q)):
                    s = dot_nt(part, k) + bias_s[...]
                    e = jnp.exp(s - jnp.max(s, -1, keepdims=True))
                    total = jnp.sum(e, -1, keepdims=True)
                    halves.append(dot(e.astype(BF16), v) * (1.0 / total))
                mix_s[:, lanes] = jnp.where(low_half, halves[0], halves[1]).astype(BF16)

        first_sum = x_s[tower, rows, :].astype(F32) + (
            dot(mix_s[...], wout_s[tower]) + biases_ref[2, pl.ds(tower, 1), :]
        )
        n1, _ = norm_stats(first_sum)
        hidden = (n1 * gains_ref[tower, 0:1, :] + biases_ref[3, pl.ds(tower, 1), :]).astype(BF16)
        second_sum = hidden.astype(F32) + biases_ref[4, pl.ds(tower, 1), :]
        for c in range(4):
            cols = slice(768 * c, 768 * c + 768)
            inner = dot(hidden, fin_s[tower, :, cols]) + ffnb_ref[pl.ds(tower, 1), cols]
            second_sum = second_sum + dot(gelu(inner).astype(BF16), fout_s[tower, cols, :])
        n2, _ = norm_stats(second_sum)
        slot = lax.rem(step, 2)

        @pl.when(step >= 2)
        def _():
            pltpu.make_async_copy(out_s.at[slot], out_hbm.at[tower, rows], osem.at[slot]).wait()

        out_s[slot] = (
            n2 * gains_ref[tower, 1:2, :] + biases_ref[5, pl.ds(tower, 1), :]
        ).astype(BF16)
        pltpu.make_async_copy(out_s.at[slot], out_hbm.at[tower, rows], osem.at[slot]).start()
        return 0

    lax.fori_loop(0, 8, tile, 0)
    for c in c2 + last_hop + swaps + own_copy[1:]:
        c.wait()
    for i in range(2):
        pltpu.make_async_copy(out_s.at[i], out_hbm.at[1, 0:256], osem.at[i]).wait()
    ga = ga_ref.reshape(16, 96, 768)
    gs = gs_ref.reshape(16, 64, 768)

    sib = (me, 1 - g)
    pair = [remote(q_s.at[1 - g, 0:768], sib_s, ks.at[0], kr.at[0], sib)]
    save_dsp = [
        pltpu.make_async_copy(kv_s.at[0, 0:768, 0:tokens], dspq_hbm, osem.at[5]),
        pltpu.make_async_copy(kv_s.at[1, 0:192, 0:tokens], dspp_hbm, osem.at[6]),
    ]
    save_uw = pltpu.make_async_copy(x_s.at[0, 0:960], uw_hbm, osem.at[4])

    pv_own = ga[:, 32:48].astype(F32)[:, 8:16].reshape(128, 768)
    pv_sib = gs[:, 32:48].astype(F32)[:, 8:16].reshape(128, 768)
    pv = jnp.concatenate([pv_own, pv_sib], 0).astype(BF16)
    col = iota((1, 256), 1)
    within = lax.rem(col, 128)
    side = jnp.where(col < 128, g, 1 - g)
    ids = (within // 8) * 16 + side * 8 + lax.rem(within, 8)
    for half, src in enumerate((ga, gs)):
        _, eq = ext_rows(src[:, 48:64].astype(F32)[:, 8:16])
        label = (eq[:, 6:7] * 256.0 + eq[:, 7:8]).astype(jnp.int32)
        logits = SCORE_SCALE * dot_nt(src[:, 0:32].reshape(512, 768), pv)
        top = jnp.max(logits, -1, keepdims=True)
        norm_log = top + jnp.log(jnp.sum(jnp.exp(logits - top), -1, keepdims=True))
        hit = label == ids
        grad = (jnp.exp(logits - norm_log) - jnp.where(hit, 1.0, 0.0)).astype(BF16)
        part = SCORE_SCALE * dot_tn(grad[:, 0:128], src[:, 0:32].reshape(512, 768))
        if half == 0:
            positive = jnp.sum(jnp.where(hit, logits, 0.0), -1, keepdims=True)
            loss = jnp.where(iota((512, 1), 0) // 32 == me, norm_log - positive, 0.0)
            diagonal = lax.rem(iota((512, 32), 0), 32) == iota((512, 32), 1)
            loss_ref[...] = jnp.sum(jnp.where(diagonal, loss, 0.0), 0, keepdims=True)
            grad_s[...] = grad
            upp_s[...] = part
        else:
            upp_s[...] += part
    mix_s[...] = pv

    def query_up(rows):
        return SCORE_SCALE * dot(grad_s[rows, :], mix_s[...])

    mine = ga[me]
    low = mine[32:64].astype(F32)
    gq_rows, keep = [], []
    for t, (count, up, hidden, vec, q, inn_ref, inv_ref, p_s) in enumerate((
        (32, query_up(pl.ds(pl.multiple_of(me * 32, 32), 32)), mine[64:96].astype(F32),
         mine[0:32].astype(F32), qq_ref[...].astype(F32), innq_ref, invq_ref, pq_s),
        (8, upp_s[pl.ds(pl.multiple_of(me * 8, 8), 8), :], low[0:8], low[8:16], low[16:24],
         innp_ref, invp_ref, pp_s),
    )):
        g0, g1 = gains_ref[t, 0:1, :], gains_ref[t, 1:2, :]
        n2 = (vec - biases_ref[5, t:t + 1, :]) / g1
        n1 = (hidden - biases_ref[3, t:t + 1, :]) / g0
        grad_second = norm_back(up, g1, n2, inv_ref[:, 1:2])
        grad_ffn = grad_second.astype(BF16)
        grad_active = dot_nt(grad_ffn, fout_s[t])
        _, slope = gelu_pair(inn_ref[...])
        grad_inner = (grad_active * slope).astype(BF16)
        grad_hidden = grad_second + dot_nt(grad_inner, fin_s[t])
        grad_first = norm_back(grad_hidden, g0, n1, inv_ref[:, 0:1])
        gm = dot_nt(grad_first.astype(BF16), wout_s[t]).astype(BF16)
        n = HEADS * count
        heads = 4 if t == 0 else HEADS
        gq = jnp.zeros((count, 768), F32)
        slopes = []
        rows_y = out_s.reshape(512, 768)
        for h0 in range(0, HEADS, heads):
            span = slice(h0 * count, (h0 + heads) * count)
            wide = expand_heads(gm.astype(F32), h0, heads).astype(BF16)
            dp = dot_nt(wide, kv_s[t, :, 768:1536])
            soft = p_s[span, :]
            ds = (soft * (dp - jnp.sum(soft * dp, -1, keepdims=True))).astype(BF16)
            slopes.append(ds)
            gq = gq + fold_heads(dot(ds, kv_s[t, :, 0:768]), count, h0, heads)
            y = dot(ds, x_s[t]) * KEY_SCALE
            if t == 0:
                rows_y[span, :] = y.astype(BF16)
            else:
                yt_s[...] = jnp.concatenate(
                    [y, jnp.zeros((32, 768), F32)], 0
                ).T.astype(BF16).reshape(16, 48, 128)
        gq = gq * KEY_SCALE
        gq_rows.append(gq)
        wide = expand_heads(gm.astype(F32)).astype(BF16)
        spread = expand_heads(q).astype(BF16)
        if t == 0:
            for lo in range(0, 768, 256):
                q_s[0, lo:lo + 256, :] = dot_tn(rows_y[0:384, lo:lo + 256], spread).astype(BF16)
            for lo in range(0, 768, 256):
                q_s[1, lo:lo + 256, :] = dot_tn(zq_ref[:, lo:lo + 256], wide).astype(BF16)
            for c in pair:
                c.start()
        for i, ds in enumerate(slopes):
            span = slice(i * heads * count, (i + 1) * heads * count)
            kv_s[t, span, 0:tokens] = ds
        kv_s[t, n:2 * n, 0:tokens] = p_s[...].astype(BF16)
        save_dsp[t].start()
        at = 768 * t
        for lo in range(0, n, 128):
            hi = min(lo + 128, n)
            u = dot_nt(spread[lo:hi], win_s[t, :, 768:1536]) * KEY_SCALE
            x_s[0, at + lo:at + hi, :] = u.astype(BF16)
            x_s[0, at + n + lo:at + n + hi, :] = dot_nt(wide[lo:hi], win_s[t, :, 1536:2304]).astype(BF16)
        extra = dot_nt(gq.astype(BF16), win_s[t, :, 0:768]) + grad_first
        ext_ref[32 * t:32 * t + count, :] = extra
    gq_s[...] = jnp.concatenate(gq_rows + [jnp.zeros((8, 768), F32)], 0).astype(BF16)
    save_uw.start()
    for c in save_dsp:
        c.wait()

    first, second, third = gather_phases(me, g, gq_s, rgq_s, ss, rs, 15, 0, 48)
    rows_swap = []
    for i in range(1, 16):
        peer = lax.rem(me + i, 16)
        rows_swap.append(remote(yt_s.at[peer], ryt_s.at[me], as_.at[16 + i], ar.at[16 + i], (peer, g)))
    own = [
        pltpu.make_async_copy(gq_s, rgq_s.at[z, yx], lsem.at[2]),
        pltpu.make_async_copy(yt_s.at[me], ryt_s.at[me], lsem.at[3]),
    ]
    xpeer = me + 1 - 2 * lax.rem(me, 2)
    ypeer = me + 2 - 4 * (lax.rem(me, 4) // 2)
    dpeer = xpeer + 2 - 4 * (lax.rem(xpeer, 4) // 2)
    plane = []
    for k, peer in enumerate((dpeer, xpeer, ypeer)):
        for zz in range(4):
            at = pl.multiple_of(48 * (4 * zz + lax.rem(peer, 4)), 16)
            n = 1 + 4 * k + zz
            plane.append(remote(
                q_s.at[g, pl.ds(at, 48)], r1_s.at[k, zz], ks.at[n], kr.at[n], (peer, g)
            ))
    column = [
        remote(s2_s.at[lax.rem(z + d, 4)], r2_s.at[d - 1], ks.at[12 + d], kr.at[12 + d],
               (lax.rem(z + d, 4) * 4 + yx, g))
        for d in range(1, 4)
    ]

    def add_pair():
        def one(i, _):
            at = pl.ds(pl.multiple_of(48 * i, 16), 48)
            q_s[g, at, :] = (q_s[g, at, :].astype(F32) + sib_s[at, :].astype(F32)).astype(BF16)
            return 0

        lax.fori_loop(0, 16, one, 0)

    def add_plane():
        def one(i, _):
            at = pl.ds(pl.multiple_of(48 * (4 * i + yx), 16), 48)
            s2_s[i] = (
                q_s[g, at, :].astype(F32) + r1_s[0, i].astype(F32)
                + r1_s[1, i].astype(F32) + r1_s[2, i].astype(F32)
            ).astype(BF16)
            return 0

        lax.fori_loop(0, 4, one, 0)

    shares = [(pwout_s, pwout_hbm, swout_hbm), (pfin_s, pfin_hbm, sfin_hbm), (pffb_s, pffb_hbm, sffb_hbm)]
    shares += [
        (pfout_s.at[t], pfout_hbm.at[t], sfout_hbm.at[t]) for t in range(2)
    ]
    shares += [(pwin_s, pwin_hbm, swin_hbm), (psum_s, psum_hbm, ssum_hbm)]
    sends = [remote(a, c, xs.at[n], xr.at[n], sib) for n, (a, b, c) in enumerate(shares)]
    saves = [pltpu.make_async_copy(a, b, psem.at[n]) for n, (a, b, c) in enumerate(shares)]
    early, late = sends[:5] + saves[:5], sends[5:] + saves[5:]
    for c in own + first + rows_swap:
        c.start()
    for c in pair:
        c.wait()
    add_pair()
    for c in plane:
        c.start()

    psum_s[...] = jnp.zeros(psum_s.shape, F32)
    pffb_s[...] = jnp.zeros(pffb_s.shape, F32)

    def chain(t, up, hidden, vec, inv1, inv2, rows, count):
        g0, g1 = gains_ref[t, 0:1, :], gains_ref[t, 1:2, :]
        total = lambda v: jnp.sum(v, 0, keepdims=True)
        n2 = (vec.astype(F32) - biases_ref[5, t:t + 1, :]) / g1
        grad_second = norm_back(up, g1, n2, inv2)
        grad_ffn = grad_second.astype(BF16)
        x_s[1, rows, :] = grad_ffn
        psum_s[t, 1:2, :] += total(up * n2)
        psum_s[t, 6:7, :] += total(grad_ffn.astype(F32))
        psum_s[t, 7:8, :] += total(up)
        grad_hidden = grad_second
        for c in range(4):
            cols = slice(768 * c, 768 * c + 768)
            inner = dot(hidden, fin_s[t, :, cols]) + ffnb_ref[t:t + 1, cols]
            active, slope = gelu_pair(inner)
            half = slice(768 * (c % 2), 768 * (c % 2) + 768)
            kept = active if c == 0 else jnp.where(me // 4 == c, active, kept)
            grad_inner = (dot_nt(grad_ffn, fout_s[t, cols, :]) * slope).astype(BF16)
            kv_s[c // 2, rows, half] = grad_inner
            pffb_s[t:t + 1, cols] += jnp.sum(grad_inner.astype(F32), 0, keepdims=True)
            grad_hidden = grad_hidden + dot_nt(grad_inner, fin_s[t, :, cols])
        win_s[0, rows, 1536:2304] = kept.astype(BF16)
        n1 = (hidden.astype(F32) - biases_ref[3, t:t + 1, :]) / g0
        psum_s[t, 0:1, :] += total(grad_hidden * n1)
        psum_s[t, 5:6, :] += total(grad_hidden)
        grad_attn = norm_back(grad_hidden, g0, n1, inv1).astype(BF16)
        win_s[0, rows, 0:768] = grad_attn
        psum_s[t, 4:5, :] += total(grad_attn.astype(F32))
        gm = dot_nt(grad_attn, wout_s[t]).astype(BF16)
        win_s[0, rows, 768:1536] = gm
        psum_s[t, 3:4, :] += total(gm.astype(F32))

    def query_block(blk, _):
        src = pl.ds(pl.multiple_of(8 * blk, 8), 8)
        rows = pl.ds(pl.multiple_of(256 * blk, 256), 256)
        block = ga[src, 48:64].astype(F32)[:, 8:16]
        ext_q = jnp.concatenate([block[:, :, 128 * a:128 * a + 128] for a in range(1, 5)], 1)
        i1q, i2q = decode_inv(ext_q.reshape(256, 128))
        chain(
            0, query_up(rows), ga[src, 64:96].reshape(256, 768), ga[src, 0:32].reshape(256, 768),
            i1q, i2q, rows, 256,
        )

        @pl.when(blk == 0)
        def _():
            own[0].wait()
            for c in first:
                c.wait()
            for c in second:
                c.start()

        return 0

    lax.fori_loop(0, 2, query_block, 0)
    i1p, i2p = decode_inv(ga[:, 48:64].astype(F32)[:, 8:16, 0:128].reshape(128, 128))
    hv = ga[:, 32:48].astype(F32)
    chain(
        1, upp_s[...], hv[:, 0:8].reshape(128, 768).astype(BF16),
        hv[:, 8:16].reshape(128, 768).astype(BF16), i1p, i2p, slice(QR, QR + PR), 128,
    )
    for c in plane:
        c.wait()
    add_plane()
    for c in column:
        c.start()
    for c in second:
        c.wait()
    for c in third:
        c.start()

    for t, rows in enumerate((slice(0, QR), slice(QR, QR + PR))):
        count = rows.stop - rows.start
        fo_at = pl.multiple_of(1536 + lax.rem(me // 2, 2) * 384, 128)
        win_s[1, 0:384, 0:count] = win_s[0, rows, pl.ds(fo_at, 384)].astype(F32).T.astype(BF16)
        fo_row = pl.multiple_of(lax.rem(me, 2) * 192, 16)
        pfout_s[t] = dot(win_s[1, pl.ds(fo_row, 192), 0:count], x_s[1, rows, :]).astype(BF16)
        fi_at = pl.multiple_of((me // 8) * 384, 128)
        if t == 0:
            hid = ga[:, 64:96, pl.ds(fi_at, 384)].reshape(QR, 384)
        else:
            hid = ga[:, 32:48, pl.ds(fi_at, 384)].astype(F32)[:, 0:8].reshape(PR, 384)
        win_s[1, 0:384, 768:768 + count] = hid.astype(F32).T.astype(BF16)
        fi_row = pl.multiple_of(lax.rem(me, 8) * 48, 16)
        lhs = win_s[1, pl.ds(fi_row, 48), 768:768 + count]
        for h in range(2):
            pfin_s[t, :, 1536 * h:1536 * h + 1536] = dot(lhs, kv_s[h, rows, :]).astype(BF16)
        if t == 0:
            mx = rsw_ref[:, 0:32].reshape(QR, 128)
        else:
            mx = rsw_ref[:, 32:48].astype(F32)[:, 0:8].reshape(PR, 128).astype(BF16)
        pwout_s[t] = dot_tn(mx, win_s[0, rows, 0:768])[0:48].astype(BF16)
    for c in early:
        c.start()

    def low_rank(read_t, read_p, out_col):
        acc_s[...] = jnp.zeros(acc_s.shape, F32)
        pad = jnp.zeros((32, 768), F32)

        def source(i, _):
            total = acc_s[...]
            for j in (2 * i, 2 * i + 1):
                even, odd = read_p(j)
                wide = jnp.concatenate([expand_heads(even), pad, expand_heads(odd), pad], 0)
                left = jnp.concatenate([read_t(2 * j), read_t(2 * j + 1)], 1)
                total = total + dot(left, wide.astype(BF16))
            acc_s[...] = total
            return 0

        lax.fori_loop(0, 4, source, 0)
        pwin_s[1, :, out_col:out_col + 768] = acc_s[...].astype(BF16)

    def gm_p(j):
        both = win_s[0, pl.ds(pl.multiple_of(QR + j * 16, 16), 16), 768:1536].astype(F32)
        return both[0:8], both[8:16]

    low_rank(lambda i: rsw_ref[i, 48:96, :], gm_p, 1536)

    for c in third:
        c.wait()
    for c in rows_swap:
        c.wait()
    own[1].wait()

    def q_p(j):
        return tuple(ga[2 * j + u, 48:64, :].astype(F32)[0:8] for u in range(2))

    low_rank(lambda i: ryt_s[i], q_p, 768)
    rg_q = rgq_s[:, :, 0:32].reshape(QR, 768)
    rg_p = rgq_s[:, :, 32:48].astype(F32)[:, :, 0:8].reshape(PR, 768)
    pwin_s[0, :, 0:768] = dot_tn(rsw_ref[:, 0:32].reshape(QR, 128), rg_q)[64:112].astype(BF16)
    x_p = rsw_ref[:, 32:48].astype(F32)[:, 0:8].reshape(PR, 128).astype(BF16)
    pwin_s[1, :, 0:768] = dot_tn(x_p, rg_p.astype(BF16))[64:112].astype(BF16)
    for c in column:
        c.wait()
    pwin_s[0, :, pl.ds(pl.multiple_of(768 + 768 * g, 128), 768)] = (
        s2_s[z].astype(F32) + r2_s[0].astype(F32) + r2_s[1].astype(F32) + r2_s[2].astype(F32)
    ).astype(BF16)
    pwin_s[0, :, pl.ds(pl.multiple_of(1536 - 768 * g, 128), 768)] = jnp.zeros((48, 768), BF16)
    psum_s[0, 2:3, :] = jnp.sum(rg_q.astype(F32), 0, keepdims=True)
    psum_s[1, 2:3, :] = jnp.sum(rg_p, 0, keepdims=True)
    for c in late:
        c.start()
    for c in early + late:
        c.wait()
    save_uw.wait()


def run_forward(xq, xp, lengths, labels, weights):
    attn_in, attn_out, ffn_in, ffn_out, gains, biases, ffn_bias = weights
    tokens = xq.shape[0]
    vm = pl.BlockSpec(memory_space=pltpu.VMEM)
    hb = pl.BlockSpec(memory_space=pl.ANY)
    sds = jax.ShapeDtypeStruct
    parts = [
        sds((2, 48, 2304), BF16), sds((2, 48, 768), BF16), sds((2, 48, 3072), BF16),
        sds((2, 192, 768), BF16), sds((2, 8, 768), F32), sds((2, 3072), F32),
    ]
    return pl.pallas_call(
        forward_kernel,
        out_shape=[
            sds((2, tokens, 768), BF16), sds((960, 768), BF16),
            sds((768, tokens), BF16), sds((192, tokens), BF16),
        ] + parts + parts + [sds((1, 32), F32), sds((40, 768), F32)],
        in_specs=[pl.BlockSpec(memory_space=pltpu.SMEM), vm, vm, vm, vm] + [hb] * 6,
        out_specs=[hb] * 16 + [vm] * 2,
        scratch_shapes=[
            pltpu.VMEM((2, tokens, 768), BF16), pltpu.VMEM((2, tokens, 768), BF16),
            pltpu.VMEM((2, tokens, 1536), BF16),
            pltpu.VMEM((2, 768, 2304), BF16), pltpu.VMEM((2, 768, 768), BF16),
            pltpu.VMEM((2, 768, 3072), BF16), pltpu.VMEM((2, 3072, 768), BF16),
            pltpu.VMEM((384, tokens), F32), pltpu.VMEM((96, tokens), F32),
            pltpu.VMEM((2, 256, 768), BF16), pltpu.VMEM((256, 768), BF16),
            pltpu.VMEM((256, 512), F32),
            pltpu.VMEM((96, 768), BF16), pltpu.VMEM((16, 96, 128), BF16),
            pltpu.VMEM((4, 4, 96, 768), BF16), pltpu.VMEM((4, 4, 64, 768), BF16), pltpu.VMEM((16, 96, 128), BF16),
            pltpu.VMEM((32, 3072), F32), pltpu.VMEM((8, 3072), F32),
            pltpu.VMEM((32, 128), F32), pltpu.VMEM((8, 128), F32),
            pltpu.VMEM((32, 768), BF16), pltpu.VMEM((384, 768), BF16),
            pltpu.VMEM((512, 256), BF16), pltpu.VMEM((128, 768), F32),
            pltpu.VMEM((48, 768), BF16), pltpu.VMEM((4, 4, 48, 768), BF16),
            pltpu.VMEM((16, 48, 128), BF16), pltpu.VMEM((16, 48, 128), BF16),
            pltpu.VMEM((768, 768), BF16), pltpu.VMEM((3, 4, 48, 768), BF16),
            pltpu.VMEM((4, 48, 768), BF16), pltpu.VMEM((3, 48, 768), BF16),
            pltpu.VMEM((2, 48, 2304), BF16), pltpu.VMEM((2, 48, 768), BF16), pltpu.VMEM((2, 48, 3072), BF16),
            pltpu.VMEM((2, 192, 768), BF16),
            pltpu.VMEM((2, 8, 768), F32), pltpu.VMEM((2, 3072), F32), pltpu.VMEM((48, 768), F32),
            pltpu.SemaphoreType.DMA((2, 5)), pltpu.SemaphoreType.DMA((4,)), pltpu.SemaphoreType.DMA((7,)),
            pltpu.SemaphoreType.DMA((22,)), pltpu.SemaphoreType.DMA((22,)),
            pltpu.SemaphoreType.DMA((32,)), pltpu.SemaphoreType.DMA((32,)),
            pltpu.SemaphoreType.DMA((7,)), pltpu.SemaphoreType.DMA((7,)),
            pltpu.SemaphoreType.DMA((16,)), pltpu.SemaphoreType.DMA((16,)), pltpu.SemaphoreType.DMA((7,)),
        ],
        compiler_params=pltpu.CompilerParams(
            collective_id=1, has_side_effects=True, vmem_limit_bytes=65400 * 1024
        ),
        name="forward",
    )(lengths, labels.reshape(1, -1), gains, biases, ffn_bias, xq, xp, attn_in, attn_out, ffn_in, ffn_out)


def finish_kernel(
    lens_ref, loss_in, ext_ref, dspq_hbm, dspp_hbm, uw_hbm, raw_hbm, *refs,
):
    ins, outs, (loss_ref, outq_hbm, outp_hbm, dxq_hbm, dxp_hbm), scratch = (
        refs[:12], refs[12:19], refs[19:24], refs[24:]
    )
    part_s, raw_s, sum_s = scratch[:12], scratch[12], scratch[13:17]
    dx_s, dspq_ref, dspp_ref, uw_ref, psem, rsem, ssem, dsem, osem = scratch[17:]
    me, _ = place()
    raw_in = pltpu.make_async_copy(raw_hbm, raw_s, rsem.at[2])
    raw_out = [pltpu.make_async_copy(raw_s.at[t], (outq_hbm, outp_hbm)[t], rsem.at[t]) for t in range(2)]
    gets = [
        pltpu.make_async_copy(uw_hbm, uw_ref, osem.at[0]),
        pltpu.make_async_copy(dspq_hbm, dspq_ref, osem.at[1]),
        pltpu.make_async_copy(dspp_hbm, dspp_ref, osem.at[2]),
    ]
    for c in gets:
        c.start()
    raw_in.start()
    loads = [pltpu.make_async_copy(ins[k], part_s[k], psem.at[k]) for k in range(12)]
    for c in loads:
        c.start()
    loss_ref[...] = loss_in[...]

    for c in gets:
        c.wait()
    extra_p = ext_ref[32:40, :]
    e_hi = extra_p.astype(BF16).astype(F32)
    uw_p = jnp.concatenate([uw_ref[768:960, :].astype(F32), e_hi, extra_p - e_hi], 0).astype(BF16)
    keep = []
    for t in range(2):
        for m in range(4):
            cols = slice(256 * m, 256 * m + 256)
            k = t * 4 + m
            if k >= 2:
                keep[k - 2].wait()
            if t == 0:
                dx_s[k % 2] = dot_tn(dspq_ref[:, cols], uw_ref[0:768, :])
                for c in range(8):
                    dx_s[k % 2, 32 * c:32 * c + 1, :] += ext_ref[8 * m + c:8 * m + c + 1, :]
            else:
                colr = iota((8, 256), 1) + 256 * m
                rowr = iota((8, 256), 0)
                start = jnp.zeros((8, 256), jnp.int32)
                for r in range(2):
                    at = jnp.int32(r * 512)
                    for c in range(4):
                        start = jnp.where(rowr == r * 4 + c, at, start)
                        at = at + lens_ref[r, c]
                sel = jnp.where(colr == start, 1.0, 0.0)
                sel2 = jnp.concatenate([sel, sel], 0).astype(BF16)
                lhs = jnp.concatenate([dspp_ref[:, cols], sel2], 0)
                dx_s[k % 2] = dot_tn(lhs, uw_p)
            c = pltpu.make_async_copy(dx_s.at[k % 2], (dxq_hbm, dxp_hbm)[t].at[cols], dsem.at[k % 2])
            c.start()
            keep.append(c)
            if k == 1:
                raw_in.wait()
                for c in raw_out:
                    c.start()

    stores = []
    for k in range(4):
        loads[k].wait()
        loads[6 + k].wait()
        sum_s[k][...] = part_s[k][...].astype(F32) + part_s[6 + k][...].astype(F32)
        c = pltpu.make_async_copy(sum_s[k], outs[k], ssem.at[k])
        c.start()
        stores.append(c)
    for k in (4, 5, 10, 11):
        loads[k].wait()
    shift = lax.rem(768 - 48 * me, 768)
    for t in range(2):
        sums = pltpu.roll(part_s[4][t] + part_s[10][t], shift, 1)[:, 0:48]
        outs[4][t] = sums[0:2]
        for j in range(6):
            outs[5][j, t:t + 1, :] = sums[2 + j:3 + j]
    ffb = part_s[5][...] + part_s[11][...]
    wide = jnp.concatenate([ffb, jnp.zeros((6, 3072), F32)], 0)
    outs[6][...] = pltpu.roll(wide, lax.rem(3072 - 192 * me, 3072), 1)[0:2, 0:192]
    for c in keep[6:] + stores + raw_out:
        c.wait()


def finish(lengths, loss, dspq, dspp, uw, ext, raw, parts):
    sds = jax.ShapeDtypeStruct
    tokens = dspq.shape[1]
    vm = pl.BlockSpec(memory_space=pltpu.VMEM)
    hb = pl.BlockSpec(memory_space=pl.ANY)
    return pl.pallas_call(
        finish_kernel,
        out_shape=[sds(p.shape, F32) for p in parts[:4]]
        + [sds((2, 2, 48), F32), sds((6, 2, 48), F32), sds((2, 192), F32)]
        + [sds((1, 32), F32), sds((tokens, 768), BF16), sds((tokens, 768), BF16)]
        + [sds((tokens, 768), F32), sds((tokens, 768), F32)],
        in_specs=[pl.BlockSpec(memory_space=pltpu.SMEM)] + [vm] * 2 + [hb] * 16,
        out_specs=[hb] * 4 + [vm] * 4 + [hb] * 4,
        scratch_shapes=[pltpu.VMEM(p.shape, p.dtype) for p in parts]
        + [pltpu.VMEM((2, tokens, 768), BF16)]
        + [pltpu.VMEM(p.shape, F32) for p in parts[:4]]
        + [pltpu.VMEM((2, 256, 768), F32), pltpu.VMEM((768, tokens), BF16)]
        + [pltpu.VMEM((192, tokens), BF16), pltpu.VMEM((960, 768), BF16)]
        + [pltpu.SemaphoreType.DMA((n,)) for n in (12, 3, 4, 2, 3)],
        compiler_params=pltpu.CompilerParams(vmem_limit_bytes=VMEM_LIMIT),
        name="finish",
    )(lengths, loss, ext, dspq, dspp, uw, raw, *parts)


def fast_shards(query_tokens, passage_tokens, lengths, labels, *weights):
    xq = query_tokens.reshape(-1, 768)
    xp = passage_tokens.reshape(-1, 768)
    weights = weights[:5] + (weights[5].transpose(1, 0, 2), weights[6])
    raw, uw, dspq, dspp, *parts, loss, ext = run_forward(xq, xp, lengths, labels, weights)
    win, wout, fin, fout, gains, biases, ffb, loss, outq, outp, dxq, dxp = finish(
        lengths, loss, dspq, dspp, uw, ext, raw, parts
    )
    return (
        loss.reshape(-1),
        outq.reshape(query_tokens.shape),
        outp.reshape(passage_tokens.shape),
        dxq.reshape(query_tokens.shape),
        dxp.reshape(passage_tokens.shape),
        win, wout, fin, fout, gains, biases.transpose(1, 0, 2), ffb,
    )


def layer_norm(residual, gain_vec, shift_vec):
    centre = residual - jnp.mean(residual, -1, keepdims=True)
    inverse = lax.rsqrt(jnp.mean(centre * centre, -1, keepdims=True) + EPSILON)
    return centre * inverse * gain_vec + shift_vec


def plain_norm_back(residual, gain_vec, upstream):
    centre = residual - jnp.mean(residual, -1, keepdims=True)
    inverse = lax.rsqrt(jnp.mean(centre * centre, -1, keepdims=True) + EPSILON)
    normed = centre * inverse
    scaled = upstream * gain_vec
    grad_res = inverse * (
        scaled
        - jnp.mean(scaled, -1, keepdims=True)
        - normed * jnp.mean(scaled * normed, -1, keepdims=True)
    )
    return (grad_res, jnp.sum(upstream * normed, 0), jnp.sum(upstream, 0))


def cls_index(starts, seq_len):
    return (jnp.arange(starts.shape[0], dtype=jnp.int32)[:, None] * seq_len + starts).reshape(-1)


def forward(tokens, segment, starts, params):
    attn_in, attn_out, ffn_in, ffn_out, gains, biases, ffn_bias = params
    batch_size, seq_len, feature = tokens.shape
    head_count = feature // HEAD_DIM
    flat_tokens = tokens.reshape(batch_size * seq_len, feature)
    zeros_vec = jnp.zeros_like(biases[0])
    joined = jnp.dot(flat_tokens, attn_in, preferred_element_type=jnp.float32) + jnp.concatenate(
        [biases[0], zeros_vec, biases[1]]
    )
    joined = joined.astype(jnp.bfloat16)
    shaped = joined.reshape(batch_size, seq_len, 3, head_count, HEAD_DIM)
    scores = (
        jnp.einsum(
            "bqhd,bkhd->bhqk", shaped[:, :, 0], shaped[:, :, 1], preferred_element_type=jnp.float32
        )
        * KEY_SCALE
    )
    same_seg = segment[:, :, None] == segment[:, None, :]
    scores = jnp.where(same_seg[:, None], scores, -1000000000.0)
    attention = jax.nn.softmax(scores, -1).astype(jnp.bfloat16)
    mixed = jnp.einsum(
        "bhqk,bkhd->bqhd", attention, shaped[:, :, 2], preferred_element_type=jnp.float32
    )
    mixed = mixed.reshape(batch_size * seq_len, feature).astype(jnp.bfloat16)
    first_sum = flat_tokens.astype(jnp.float32) + (
        jnp.dot(mixed, attn_out, preferred_element_type=jnp.float32) + biases[2]
    )
    hidden = layer_norm(first_sum, gains[0], biases[3]).astype(jnp.bfloat16)
    inner = jnp.dot(hidden, ffn_in, preferred_element_type=jnp.float32) + ffn_bias
    active = jax.nn.gelu(inner).astype(jnp.bfloat16)
    second_sum = hidden.astype(jnp.float32) + (
        jnp.dot(active, ffn_out, preferred_element_type=jnp.float32) + biases[4]
    )
    output = layer_norm(second_sum, gains[1], biases[5]).astype(jnp.bfloat16)
    picked = cls_index(starts, seq_len)
    kept = (
        flat_tokens,
        joined,
        mixed[picked],
        first_sum[picked],
        hidden[picked],
        inner[picked],
        active[picked],
        second_sum[picked],
    )
    return (output, picked, kept)


def backward(kept, segment, starts, params, upstream):
    attn_in, attn_out, ffn_in, ffn_out, gains, biases, ffn_bias = params
    flat_tokens, joined, mixed_cls, first_cls, hidden_cls, inner_cls, active_cls, second_cls = kept
    batch_size, seq_len = segment.shape
    per_row = starts.shape[1]
    feature = flat_tokens.shape[1]
    head_count = feature // HEAD_DIM
    grad_second, gain_two, shift_two = plain_norm_back(second_cls, gains[1], upstream)
    grad_ffn = grad_second.astype(jnp.bfloat16)
    grad_down = jnp.dot(active_cls.T, grad_ffn, preferred_element_type=jnp.float32)
    grad_active = jnp.dot(grad_ffn, ffn_out.T, preferred_element_type=jnp.float32)
    grad_inner = jax.vjp(jax.nn.gelu, inner_cls)[1](grad_active)[0].astype(jnp.bfloat16)
    grad_up = jnp.dot(hidden_cls.T, grad_inner, preferred_element_type=jnp.float32)
    grad_hidden = grad_second + jnp.dot(grad_inner, ffn_in.T, preferred_element_type=jnp.float32)
    grad_first, gain_one, shift_one = plain_norm_back(first_cls, gains[0], grad_hidden)
    grad_attn = grad_first.astype(jnp.bfloat16)
    grad_outproj = jnp.dot(mixed_cls.T, grad_attn, preferred_element_type=jnp.float32)
    grad_mixed = jnp.dot(grad_attn, attn_out.T, preferred_element_type=jnp.float32).astype(
        jnp.bfloat16
    )
    grad_mixed = grad_mixed.reshape(batch_size, per_row, head_count, HEAD_DIM)
    shaped = joined.reshape(batch_size, seq_len, 3, head_count, HEAD_DIM)
    key_part = shaped[:, :, 1]
    value_part = shaped[:, :, 2]
    picked = cls_index(starts, seq_len)
    query_cls = joined[picked, :feature].reshape(batch_size, per_row, head_count, HEAD_DIM)
    own_seg = jnp.take_along_axis(segment, starts, 1)
    scores = (
        jnp.einsum("bchd,bkhd->bhck", query_cls, key_part, preferred_element_type=jnp.float32)
        * KEY_SCALE
    )
    scores = jnp.where((own_seg[:, :, None] == segment[:, None, :])[:, None], scores, -1000000000.0)
    attention = jax.nn.softmax(scores, -1)
    grad_attention = jnp.einsum(
        "bchd,bkhd->bhck", grad_mixed, value_part, preferred_element_type=jnp.float32
    )
    grad_scores = attention * (
        grad_attention - jnp.sum(attention * grad_attention, -1, keepdims=True)
    )
    grad_scores = grad_scores.astype(jnp.bfloat16)
    grad_query = (
        jnp.einsum("bhck,bkhd->bchd", grad_scores, key_part, preferred_element_type=jnp.float32)
        * KEY_SCALE
    ).astype(jnp.bfloat16)
    grad_key = (
        jnp.einsum("bhck,bchd->bkhd", grad_scores, query_cls, preferred_element_type=jnp.float32)
        * KEY_SCALE
    ).astype(jnp.bfloat16)
    grad_value = jnp.einsum(
        "bhck,bchd->bkhd",
        attention.astype(jnp.bfloat16),
        grad_mixed,
        preferred_element_type=jnp.float32,
    ).astype(jnp.bfloat16)
    places = jnp.arange(seq_len, dtype=jnp.int32)
    selector = (starts[:, :, None] == places[None, None, :]).astype(jnp.bfloat16)
    grad_query_full = jnp.einsum(
        "bcl,bchd->blhd", selector, grad_query, preferred_element_type=jnp.float32
    ).astype(jnp.bfloat16)
    grad_joined = jnp.stack([grad_query_full, grad_key, grad_value], 2).reshape(
        batch_size * seq_len, 3 * feature
    )
    grad_inproj = jnp.dot(flat_tokens.T, grad_joined, preferred_element_type=jnp.float32)
    grad_tokens = (
        jnp.dot(grad_joined, attn_in.T, preferred_element_type=jnp.float32)
        .at[picked]
        .add(grad_first)
    )
    bias_grads = jnp.stack(
        [
            jnp.sum(grad_query.astype(jnp.float32), (0, 1)).reshape(feature),
            jnp.sum(grad_value.astype(jnp.float32), (0, 1)).reshape(feature),
            jnp.sum(grad_attn.astype(jnp.float32), 0),
            shift_one,
            jnp.sum(grad_ffn.astype(jnp.float32), 0),
            shift_two,
        ]
    )
    gain_grads = jnp.stack([gain_one, gain_two])
    hidden_bias = jnp.sum(grad_inner.astype(jnp.float32), 0)
    grads = (grad_inproj, grad_outproj, grad_up, grad_down, gain_grads, bias_grads, hidden_bias)
    row_data = (hidden_cls, grad_inner, active_cls, grad_ffn)
    return (grads, grad_tokens.reshape(batch_size, seq_len, feature), row_data)


def shards(
    query_tokens,
    passage_tokens,
    lengths,
    labels,
    attn_in,
    attn_out,
    ffn_in,
    ffn_out,
    gains,
    biases,
    ffn_bias,
):
    layers = (attn_in, attn_out, ffn_in, ffn_out, gains, biases, ffn_bias)
    query_params = tuple((matrix[0] for matrix in layers))
    passage_params = tuple((matrix[1] for matrix in layers))
    query_count, query_len, feature = query_tokens.shape
    passage_len = passage_tokens.shape[1]
    query_segment = jnp.zeros((query_count, query_len), jnp.int32)
    query_starts = jnp.zeros((query_count, 1), jnp.int32)
    ends = jnp.cumsum(lengths, -1)
    passage_starts = ends - lengths
    places = jnp.arange(passage_len, dtype=jnp.int32)
    passage_segment = jnp.sum((places[None, :, None] >= ends[:, None, :]).astype(jnp.int32), -1)
    query_out, query_pick, query_kept = forward(
        query_tokens, query_segment, query_starts, query_params
    )
    passage_out, passage_pick, passage_kept = forward(
        passage_tokens, passage_segment, passage_starts, passage_params
    )
    query_vec = query_out[query_pick]
    passage_vec = passage_out[passage_pick]
    passage_count = passage_vec.shape[0]
    float_labels = labels.astype(jnp.float32)
    group_vec = lax.all_gather(passage_vec, "grp", axis=0, tiled=True)
    portion = lax.all_gather(group_vec, "blk", axis=0, tiled=True)
    running_max = jnp.full((query_count,), -1e30, jnp.float32)
    score_block = SCORE_SCALE * jnp.dot(query_vec, portion.T, preferred_element_type=jnp.float32)
    column_ids = jnp.arange(portion.shape[0], dtype=jnp.int32)
    new_max = jnp.maximum(running_max, jnp.max(score_block, -1))
    running_sum = jnp.sum(jnp.exp(score_block - new_max[:, None]), -1)
    hits = column_ids[None, :] == labels[:, None]
    positive = jnp.sum(jnp.where(hits, score_block, 0.0), -1)
    running_max, running_sum, positive = (new_max, running_sum, positive)
    norm_log = running_max + jnp.log(running_sum)
    portion = lax.all_gather(group_vec, "blk", axis=0, tiled=True)
    score_block = SCORE_SCALE * jnp.dot(query_vec, portion.T, preferred_element_type=jnp.float32)
    column_ids = jnp.arange(portion.shape[0], dtype=jnp.int32)
    hits = (column_ids[None, :] == labels[:, None]).astype(jnp.float32)
    grad_block = (jnp.exp(score_block - norm_log[:, None]) - hits).astype(jnp.bfloat16)
    query_up = SCORE_SCALE * jnp.dot(grad_block, portion, preferred_element_type=jnp.float32)
    own_ids = (
        lax.axis_index(("blk", "grp")) * passage_count + jnp.arange(passage_count, dtype=jnp.int32)
    ).astype(jnp.float32)
    remote_vec = lax.all_gather(query_vec.astype(jnp.float32), ("blk", "grp"), axis=0, tiled=True)
    remote_log = lax.all_gather(norm_log, ("blk", "grp"), axis=0, tiled=True)
    remote_label = lax.all_gather(float_labels, ("blk", "grp"), axis=0, tiled=True)
    remote_low = remote_vec.astype(jnp.bfloat16)
    score_block = SCORE_SCALE * jnp.dot(
        remote_low, passage_vec.T, preferred_element_type=jnp.float32
    )
    hits = (remote_label[:, None] == own_ids[None, :]).astype(jnp.float32)
    grad_block = (jnp.exp(score_block - remote_log[:, None]) - hits).astype(jnp.bfloat16)
    passage_up = SCORE_SCALE * jnp.dot(grad_block.T, remote_low, preferred_element_type=jnp.float32)
    query_losses = norm_log - positive
    query_grads, query_back, query_rows = backward(
        query_kept, query_segment, query_starts, query_params, query_up
    )
    passage_grads, passage_back, passage_rows = backward(
        passage_kept, passage_segment, passage_starts, passage_params, passage_up
    )
    stacked = tuple(
        (
            jnp.stack([first_part, second_part])
            for first_part, second_part in zip(query_grads, passage_grads)
        )
    )
    grad_win, grad_wout, grad_up, grad_down, grad_gain, grad_bias, grad_hidden_bias = stacked
    shares = (
        lax.psum_scatter(
            grad_win.astype(jnp.bfloat16), "blk", scatter_dimension=1, tiled=True
        ).astype(jnp.float32),
        lax.psum_scatter(
            grad_wout.astype(jnp.bfloat16), "blk", scatter_dimension=1, tiled=True
        ).astype(jnp.float32),
        lax.psum_scatter(
            grad_up.astype(jnp.bfloat16), "blk", scatter_dimension=1, tiled=True
        ).astype(jnp.float32),
        lax.psum_scatter(
            grad_down.astype(jnp.bfloat16), "blk", scatter_dimension=1, tiled=True
        ).astype(jnp.float32),
        lax.psum_scatter(
            grad_gain.astype(jnp.bfloat16), "blk", scatter_dimension=2, tiled=True
        ).astype(jnp.float32),
        lax.psum_scatter(
            grad_bias.astype(jnp.bfloat16), "blk", scatter_dimension=2, tiled=True
        ).astype(jnp.float32),
        lax.psum_scatter(
            grad_hidden_bias.astype(jnp.bfloat16), "blk", scatter_dimension=1, tiled=True
        ).astype(jnp.float32),
    )
    grad_win, grad_wout, grad_up, grad_down, grad_gain, grad_bias, grad_hidden_bias = (
        lax.psum(shares[0].astype(jnp.bfloat16), "grp").astype(jnp.float32),
        lax.psum(shares[1].astype(jnp.bfloat16), "grp").astype(jnp.float32),
        lax.psum(shares[2].astype(jnp.bfloat16), "grp").astype(jnp.float32),
        lax.psum(shares[3].astype(jnp.bfloat16), "grp").astype(jnp.float32),
        lax.psum(shares[4].astype(jnp.bfloat16), "grp").astype(jnp.float32),
        lax.psum(shares[5].astype(jnp.bfloat16), "grp").astype(jnp.float32),
        lax.psum(shares[6].astype(jnp.bfloat16), "grp").astype(jnp.float32),
    )
    query_shaped = query_out.reshape(query_count, query_len, feature)
    passage_shaped = passage_out.reshape(passage_tokens.shape)
    return (
        query_losses,
        query_shaped,
        passage_shaped,
        query_back,
        passage_back,
        grad_win,
        grad_wout,
        grad_up,
        grad_down,
        grad_gain,
        grad_bias,
        grad_hidden_bias,
    )


def solution(mesh):
    placed = (
        P(("blk", "grp"), None, None),
        P(("blk", "grp"), None, None),
        P(("blk", "grp"), None),
        P(("blk", "grp")),
        P(),
        P(),
        P(),
        P(),
        P(),
        P(),
        P(),
    )
    small = dict(mesh.shape) == {"blk": 16, "grp": 2}
    return jax.shard_map(
        fast_shards if small else shards,
        mesh=mesh,
        in_specs=placed,
        out_specs=(
            P(("blk", "grp")),
            P(("blk", "grp"), None, None),
            P(("blk", "grp"), None, None),
            P(("blk", "grp"), None, None),
            P(("blk", "grp"), None, None),
            P(None, "blk", None),
            P(None, "blk", None),
            P(None, "blk", None),
            P(None, "blk", None),
            P(None, None, "blk"),
            P(None, None, "blk"),
            P(None, "blk"),
        ),
        check_vma=False,
    )
```

```python
import functools
import jax
import jax.numpy as jnp
from jax import lax
from jax.experimental import pallas as pl
from jax.experimental.pallas import tpu as pltpu
from jax.sharding import PartitionSpec as P

MESH = pl.DeviceIdType.MESH
HEAD_DIM = 64
HEADS = 12
EPSILON = 1e-05
SCORE_SCALE = 0.08
KEY_SCALE = 0.125
NEG = -1000000000.0
GELU_A = 0.7978845608028654
GELU_B = 0.044715 * GELU_A
F32 = jnp.float32
BF16 = jnp.bfloat16
VMEM_LIMIT = 60 * 1024 * 1024


def dot(a, b):
    return lax.dot_general(a, b, (((1,), (0,)), ((), ())), preferred_element_type=F32)


def dot_nt(a, b):
    return lax.dot_general(a, b, (((1,), (1,)), ((), ())), preferred_element_type=F32)


def dot_tn(a, b):
    return lax.dot_general(a, b, (((0,), (0,)), ((), ())), preferred_element_type=F32)


def iota(shape, dim):
    return lax.broadcasted_iota(jnp.int32, shape, dim)


def head_row(h):
    return iota((1, 768), 1) // HEAD_DIM == h


def expand_heads(rows, h0=0, heads=HEADS):
    return jnp.concatenate(
        [jnp.where(head_row(h0 + h), rows, 0.0) for h in range(heads)], 0
    )


def fold_heads(rows, count, h0=0, heads=HEADS):
    out = jnp.where(head_row(h0), rows[:count], 0.0)
    for h in range(1, heads):
        out = out + jnp.where(head_row(h0 + h), rows[h * count:(h + 1) * count], 0.0)
    return out


def norm_stats(residual):
    centre = residual - jnp.mean(residual, -1, keepdims=True)
    inverse = lax.rsqrt(jnp.mean(centre * centre, -1, keepdims=True) + EPSILON)
    return centre * inverse, inverse


def gelu(v):
    half = 0.5 + 0.5 * jnp.tanh(v * (GELU_A + GELU_B * (v * v)))
    return v * half


def split3(v):
    hi = v.astype(BF16).astype(F32)
    rest = v - hi
    mid = rest.astype(BF16).astype(F32)
    return hi, mid, rest - mid


def lane_pack(columns, count):
    lane = iota((count, 128), 1)
    out = jnp.zeros((count, 128), F32)
    for j, column in enumerate(columns):
        out = jnp.where(lane == j, column, out)
    return out


def norm_back(up, gain, normed, inverse):
    u = up * gain
    return inverse * (
        u - jnp.mean(u, -1, keepdims=True) - normed * jnp.mean(u * normed, -1, keepdims=True)
    )


def gelu_pair(v):
    sq = v * v
    half = 0.5 + 0.5 * jnp.tanh(v * (GELU_A + GELU_B * sq))
    value = v * half
    return value, half + (value - value * half) * (2.0 * GELU_A + 6.0 * GELU_B * sq)


def decode_inv(ext):
    return ext[:, 0:1] + ext[:, 1:2] + ext[:, 2:3], ext[:, 3:4] + ext[:, 4:5] + ext[:, 5:6]


def ext_rows(block):
    e_p = block[:, :, 0:128].reshape(128, 128)
    e_q = jnp.concatenate([block[:, :, 128 * a:128 * a + 128] for a in range(1, 5)], 1)
    return e_p, e_q.reshape(512, 128)


def place():
    return lax.axis_index("blk"), lax.axis_index("grp")


def remote(src, dst, send, recv, peer):
    return pltpu.make_async_remote_copy(
        src_ref=src, dst_ref=dst, send_sem=send, recv_sem=recv, device_id=peer, device_id_type=MESH
    )


def greet(me, g):
    barrier = pltpu.get_barrier_semaphore()
    for i in range(1, 16):
        pl.semaphore_signal(barrier, inc=1, device_id=(lax.rem(me + i, 16), g), device_id_type=MESH)
    pl.semaphore_signal(barrier, inc=1, device_id=(me, 1 - g), device_id_type=MESH)


def greeted():
    pl.semaphore_wait(pltpu.get_barrier_semaphore(), 16)


def gather_phases(me, g, pay, ga, ss, rs, base, lo, hi):
    z, yx = me // 4, lax.rem(me, 4)
    xpeer = me + 1 - 2 * lax.rem(me, 2)
    ypeer = me + 2 - 4 * (lax.rem(me, 4) // 2)
    yx_x, yx_y = lax.rem(xpeer, 4), lax.rem(ypeer, 4)
    rows = slice(lo, hi)
    first, second, third = [], [], []

    def add(phase, src, dst, k, peer):
        phase.append(remote(src, dst, ss.at[base + k], rs.at[base + k], (peer, g)))

    for d in range(1, 4):
        peer = lax.rem(z + d, 4) * 4 + yx
        add(first, pay.at[rows], ga.at[z, yx, rows], d - 1, peer)
    add(second, ga.at[:, yx, rows], ga.at[:, yx, rows], 3, xpeer)
    add(second, ga.at[:, yx, rows], ga.at[:, yx, rows], 4, ypeer)
    add(third, ga.at[0:2, yx_x, rows], ga.at[0:2, yx_x, rows], 5, ypeer)
    add(third, ga.at[2:4, yx_y, rows], ga.at[2:4, yx_y, rows], 6, xpeer)
    return first, second, third


QR, PR = 512, 128


def forward_kernel(
    lens_ref, labels_ref, gains_ref, biases_ref, ffnb_ref,
    xq_hbm, xp_hbm, win_hbm, wout_hbm, fin_hbm, fout_hbm,
    out_hbm, uw_hbm, dspq_hbm, dspp_hbm,
    pwin_hbm, pwout_hbm, pfin_hbm, pfout_hbm, psum_hbm, pffb_hbm,
    swin_hbm, swout_hbm, sfin_hbm, sfout_hbm, ssum_hbm, sffb_hbm,
    loss_ref, ext_ref,
    x_s, q_s, kv_s, win_s, wout_s, fin_s, fout_s, pq_s, pp_s, out_s, mix_s, bias_s,
    pay_s, swap_s, ga_ref, gs_ref, rsw_ref, innq_ref, innp_ref, invq_ref, invp_ref, qq_ref, zq_ref,
    grad_s, upp_s, gq_s, rgq_s, yt_s, ryt_s, sib_s, r1_s, s2_s, r2_s,
    pwin_s, pwout_s, pfin_s, pfout_s, psum_s, pffb_s, acc_s,
    sem, lsem, osem, ss, rs, as_, ar, xs, xr, ks, kr, psem,
):
    me, g = place()
    z, yx = me // 4, lax.rem(me, 4)
    greet(me, g)
    copies = []
    for t, x_hbm in enumerate((xq_hbm, xp_hbm)):
        copies.append([
            pltpu.make_async_copy(x_hbm, x_s.at[t], sem.at[t, 0]),
            pltpu.make_async_copy(win_hbm.at[t], win_s.at[t], sem.at[t, 1]),
            pltpu.make_async_copy(wout_hbm.at[t], wout_s.at[t], sem.at[t, 2]),
            pltpu.make_async_copy(fin_hbm.at[t], fin_s.at[t], sem.at[t, 3]),
            pltpu.make_async_copy(fout_hbm.at[t], fout_s.at[t], sem.at[t, 4]),
        ])
    for c in copies[0][:2] + copies[1][:2] + copies[0][2:] + copies[1][2:]:
        c.start()
    a1, b1, c1 = gather_phases(me, g, pay_s, ga_ref, ss, rs, 0, 0, 64)
    a2, b2, c2 = gather_phases(me, g, pay_s, ga_ref, ss, rs, 7, 64, 96)
    last_hop = [remote(ga_ref.at[:, :, 0:64], gs_ref, ss.at[14], rs.at[14], (me, 1 - g))]
    swaps = []
    for i in range(1, 16):
        peer = lax.rem(me + i, 16)
        swaps.append(remote(swap_s.at[peer], rsw_ref.at[me], as_.at[i], ar.at[i], (peer, g)))
    own_copy = [
        pltpu.make_async_copy(pay_s, ga_ref.at[z, yx], lsem.at[0]),
        pltpu.make_async_copy(swap_s.at[me], rsw_ref.at[me], lsem.at[1]),
    ]

    tokens = x_s.shape[1]
    col_q = iota((32, tokens), 1)
    row_q = iota((32, tokens), 0)
    sel_q = col_q == row_q * 32
    own_q = col_q // 32 == row_q
    col_p = iota((8, tokens), 1)
    row_p = iota((8, tokens), 0)
    lo = jnp.zeros((8, tokens), jnp.int32)
    hi = jnp.zeros((8, tokens), jnp.int32)
    for r in range(2):
        acc = jnp.int32(r * 512)
        for c in range(4):
            length = lens_ref[r, c]
            lo = jnp.where(row_p == r * 4 + c, acc, lo)
            acc = acc + length
            hi = jnp.where(row_p == r * 4 + c, acc, hi)
    sel_p = col_p == lo
    own_p = (col_p >= lo) & (col_p < hi)

    picks = []
    for t, sel in enumerate((sel_q, sel_p)):
        copies[t][0].wait()
        copies[t][1].wait()
        query_bias = biases_ref[0, t:t + 1, :]
        value_bias = biases_ref[1, t:t + 1, :]

        def kv_step(m, _, t=t, query_bias=query_bias, value_bias=value_bias):
            rows = pl.ds(pl.multiple_of(m * 512, 512), 512)
            x = x_s[t, rows, :]
            kv_s[t, rows, 0:768] = dot(x, win_s[t, :, 768:1536]).astype(BF16)
            kv_s[t, rows, 768:1536] = (dot(x, win_s[t, :, 1536:2304]) + value_bias).astype(BF16)
            q_s[t, rows, :] = (dot(x, win_s[t, :, 0:768]) + query_bias).astype(BF16)
            return 0

        lax.fori_loop(0, tokens // 512, kv_step, 0)
        pick = jnp.where(sel, 1.0, 0.0).astype(BF16)
        picks.append((dot(pick, x_s[t]), dot(pick, q_s[t])))

    done = []
    for t, (own, count, p_s, inn_ref, inv_ref) in enumerate((
        (own_q, 32, pq_s, innq_ref, invq_ref), (own_p, 8, pp_s, innp_ref, invp_ref),
    )):
        xc, qc = picks[t]
        mixed = jnp.zeros((count, 768), F32)
        heads = 4 if t == 0 else HEADS
        mask = jnp.concatenate([jnp.where(own, 0.0, NEG)] * heads, 0)
        for h0 in range(0, HEADS, heads):
            span = slice(h0 * count, (h0 + heads) * count)
            spread = expand_heads(qc, h0, heads).astype(BF16)
            scores = dot_nt(spread, kv_s[t, :, 0:768]) * KEY_SCALE + mask
            weight = jnp.exp(scores - jnp.max(scores, -1, keepdims=True))
            soft = weight * (1.0 / jnp.sum(weight, -1, keepdims=True))
            p_s[span, :] = soft
            soft16 = soft.astype(BF16)
            mixed = mixed + fold_heads(dot(soft16, kv_s[t, :, 768:1536]), count, h0, heads)
            zsum = dot(soft16, x_s[t])
            if t == 0:
                zq_ref[span, :] = zsum.astype(BF16)
            else:
                wide = jnp.concatenate([zsum, jnp.zeros((32, 768), F32)], 0)
                swap_s[:, 48:96, :] = wide.T.astype(BF16).reshape(16, 48, 128)
        mixed = mixed.astype(BF16)
        copies[t][2].wait()
        first = xc + (dot(mixed, wout_s[t]) + biases_ref[2, t:t + 1, :])
        n1, inv1 = norm_stats(first)
        hidden = (n1 * gains_ref[t, 0:1, :] + biases_ref[3, t:t + 1, :]).astype(BF16)
        copies[t][3].wait()
        inner = dot(hidden, fin_s[t]) + ffnb_ref[t:t + 1, :]
        inn_ref[...] = inner
        active = gelu(inner).astype(BF16)
        copies[t][4].wait()
        second = hidden.astype(F32) + (dot(active, fout_s[t]) + biases_ref[4, t:t + 1, :])
        n2, inv2 = norm_stats(second)
        vec = (n2 * gains_ref[t, 1:2, :] + biases_ref[5, t:t + 1, :]).astype(BF16)
        inv_ref[...] = lane_pack([inv1, inv2], count)
        done.append((xc, qc, mixed, hidden, vec, inv1, inv2))

    xq, qq, mq, hq, vq, i1q, i2q = done[0]
    xp, qp, mp, hp, vp, i1p, i2p = done[1]
    lab = labels_ref[...].astype(F32)
    eye = iota((32, 32), 0) == iota((32, 32), 1)
    lab_col = jnp.sum(jnp.where(eye, lab, 0.0), 1, keepdims=True)
    lab_hi = jnp.floor(lab_col * (1.0 / 256.0))
    lab_lo = lab_col - 256.0 * lab_hi
    ext_q = lane_pack([*split3(i1q), *split3(i2q), lab_hi, lab_lo], 32)
    ext_p = lane_pack([*split3(i1p), *split3(i2p)], 8)
    ext = jnp.concatenate(
        [ext_p] + [ext_q[8 * a:8 * a + 8] for a in range(4)] + [jnp.zeros((8, 128), F32)], 1
    )
    pay_s[0:32, :] = vq
    pay_s[32:64, :] = jnp.concatenate([hp.astype(F32), vp.astype(F32), qp, ext], 0).astype(BF16)
    pay_s[64:96, :] = hq
    qq_ref[...] = qq.astype(BF16)
    greeted()
    own_copy[0].start()
    for c in a1 + a2:
        c.start()
    m48 = jnp.concatenate([mq.astype(F32), mp.astype(F32), jnp.zeros((8, 768), F32)], 0)
    x48 = jnp.concatenate([xq, xp, jnp.zeros((8, 768), F32)], 0)
    swap_s[:, 0:48, :] = jnp.zeros((16, 48, 128), BF16)
    for b in range(16):
        swap_s[b, 0:48, 0:48] = m48[:, 48 * b:48 * b + 48].astype(BF16)
        swap_s[b, 0:48, 64:112] = x48[:, 48 * b:48 * b + 48].astype(BF16)
    for c in own_copy[1:]:
        c.start()

    low_half = iota((1, 128), 1) < HEAD_DIM

    def tile(step, _):
        tower = step // 4
        rows = pl.ds(pl.multiple_of(lax.rem(step, 4) * 256, 256), 256)

        def on(k, waits, starts):
            @pl.when(step == k)
            def _():
                for c in waits:
                    c.wait()
                for c in starts:
                    c.start()

        on(2, own_copy[0:1] + a1, b1)
        on(3, a2, b2)
        on(4, b1, c1 + swaps)
        on(5, b2, c2)
        on(6, c1, last_hop)

        @pl.when(step < 4)
        def _():
            same = iota((128, 128), 0) // 32 == iota((128, 128), 1) // 32
            mask = jnp.where(same, 0.0, NEG)
            mask2 = jnp.concatenate([mask, mask], 0)
            for part in range(2):
                at = pl.ds(pl.multiple_of(lax.rem(step, 4) * 256 + part * 128, 128), 128)
                for j in range(HEADS // 2):
                    lanes = slice(128 * j, 128 * j + 128)
                    q = q_s[0, at, lanes] * KEY_SCALE
                    k = kv_s[0, at, lanes]
                    v = kv_s[0, at, 768 + 128 * j:768 + 128 * j + 128]
                    zero = jnp.zeros_like(q)
                    q2 = jnp.concatenate([jnp.where(low_half, q, zero), jnp.where(low_half, zero, q)], 0)
                    s = dot_nt(q2, k) + mask2
                    e = jnp.exp(s - jnp.max(s, -1, keepdims=True))
                    total = jnp.sum(e, -1, keepdims=True)
                    o = dot(e.astype(BF16), v) * (1.0 / total)
                    mix_s[part * 128:part * 128 + 128, lanes] = jnp.where(low_half, o[:128], o[128:]).astype(BF16)

        @pl.when(step >= 4)
        def _():
            row = (step - 4) // 2
            base = lax.rem(step, 2) * 256
            keys = pl.ds(pl.multiple_of(row * 512, 512), 512)
            qpos = iota((256, 512), 0) + base
            kpos = iota((256, 512), 1)
            qseg = jnp.zeros((256, 512), jnp.int32)
            kseg = jnp.zeros((256, 512), jnp.int32)
            end = jnp.int32(0)
            for c in range(3):
                end = end + lens_ref[row, c]
                qseg = qseg + jnp.where(qpos >= end, 1, 0)
                kseg = kseg + jnp.where(kpos >= end, 1, 0)
            mask = jnp.where(qseg == kseg, 0.0, NEG)
            bias_s[...] = mask
            for j in range(HEADS // 2):
                lanes = slice(128 * j, 128 * j + 128)
                q = q_s[1, rows, lanes] * KEY_SCALE
                k = kv_s[1, keys, lanes]
                v = kv_s[1, keys, 768 + 128 * j:768 + 128 * j + 128]
                zero = jnp.zeros_like(q)
                halves = []
                for part in (jnp.where(low_half, q, zero), jnp.where(low_half, zero, q)):
                    s = dot_nt(part, k) + bias_s[...]
                    e = jnp.exp(s - jnp.max(s, -1, keepdims=True))
                    total = jnp.sum(e, -1, keepdims=True)
                    halves.append(dot(e.astype(BF16), v) * (1.0 / total))
                mix_s[:, lanes] = jnp.where(low_half, halves[0], halves[1]).astype(BF16)

        first_sum = x_s[tower, rows, :].astype(F32) + (
            dot(mix_s[...], wout_s[tower]) + biases_ref[2, pl.ds(tower, 1), :]
        )
        n1, _ = norm_stats(first_sum)
        hidden = (n1 * gains_ref[tower, 0:1, :] + biases_ref[3, pl.ds(tower, 1), :]).astype(BF16)
        second_sum = hidden.astype(F32) + biases_ref[4, pl.ds(tower, 1), :]
        for c in range(4):
            cols = slice(768 * c, 768 * c + 768)
            inner = dot(hidden, fin_s[tower, :, cols]) + ffnb_ref[pl.ds(tower, 1), cols]
            second_sum = second_sum + dot(gelu(inner).astype(BF16), fout_s[tower, cols, :])
        n2, _ = norm_stats(second_sum)
        slot = lax.rem(step, 2)

        @pl.when(step >= 2)
        def _():
            pltpu.make_async_copy(out_s.at[slot], out_hbm.at[tower, rows], osem.at[slot]).wait()

        out_s[slot] = (
            n2 * gains_ref[tower, 1:2, :] + biases_ref[5, pl.ds(tower, 1), :]
        ).astype(BF16)
        pltpu.make_async_copy(out_s.at[slot], out_hbm.at[tower, rows], osem.at[slot]).start()
        return 0

    lax.fori_loop(0, 8, tile, 0)
    for c in c2 + last_hop + swaps + own_copy[1:]:
        c.wait()
    for i in range(2):
        pltpu.make_async_copy(out_s.at[i], out_hbm.at[1, 0:256], osem.at[i]).wait()
    ga = ga_ref.reshape(16, 96, 768)
    gs = gs_ref.reshape(16, 64, 768)

    sib = (me, 1 - g)
    pair = [remote(q_s.at[1 - g, 0:768], sib_s, ks.at[0], kr.at[0], sib)]
    save_dsp = [
        pltpu.make_async_copy(kv_s.at[0, 0:768, 0:tokens], dspq_hbm, osem.at[5]),
        pltpu.make_async_copy(kv_s.at[1, 0:192, 0:tokens], dspp_hbm, osem.at[6]),
    ]
    save_uw = pltpu.make_async_copy(x_s.at[0, 0:960], uw_hbm, osem.at[4])

    pv_own = ga[:, 32:48].astype(F32)[:, 8:16].reshape(128, 768)
    pv_sib = gs[:, 32:48].astype(F32)[:, 8:16].reshape(128, 768)
    pv = jnp.concatenate([pv_own, pv_sib], 0).astype(BF16)
    col = iota((1, 256), 1)
    within = lax.rem(col, 128)
    side = jnp.where(col < 128, g, 1 - g)
    ids = (within // 8) * 16 + side * 8 + lax.rem(within, 8)
    for half, src in enumerate((ga, gs)):
        _, eq = ext_rows(src[:, 48:64].astype(F32)[:, 8:16])
        label = (eq[:, 6:7] * 256.0 + eq[:, 7:8]).astype(jnp.int32)
        logits = SCORE_SCALE * dot_nt(src[:, 0:32].reshape(512, 768), pv)
        top = jnp.max(logits, -1, keepdims=True)
        norm_log = top + jnp.log(jnp.sum(jnp.exp(logits - top), -1, keepdims=True))
        hit = label == ids
        grad = (jnp.exp(logits - norm_log) - jnp.where(hit, 1.0, 0.0)).astype(BF16)
        part = SCORE_SCALE * dot_tn(grad[:, 0:128], src[:, 0:32].reshape(512, 768))
        if half == 0:
            positive = jnp.sum(jnp.where(hit, logits, 0.0), -1, keepdims=True)
            loss = jnp.where(iota((512, 1), 0) // 32 == me, norm_log - positive, 0.0)
            diagonal = lax.rem(iota((512, 32), 0), 32) == iota((512, 32), 1)
            loss_ref[...] = jnp.sum(jnp.where(diagonal, loss, 0.0), 0, keepdims=True)
            grad_s[...] = grad
            upp_s[...] = part
        else:
            upp_s[...] += part
    mix_s[...] = pv

    def query_up(rows):
        return SCORE_SCALE * dot(grad_s[rows, :], mix_s[...])

    mine = ga[me]
    low = mine[32:64].astype(F32)
    gq_rows, keep = [], []
    for t, (count, up, hidden, vec, q, inn_ref, inv_ref, p_s) in enumerate((
        (32, query_up(pl.ds(pl.multiple_of(me * 32, 32), 32)), mine[64:96].astype(F32),
         mine[0:32].astype(F32), qq_ref[...].astype(F32), innq_ref, invq_ref, pq_s),
        (8, upp_s[pl.ds(pl.multiple_of(me * 8, 8), 8), :], low[0:8], low[8:16], low[16:24],
         innp_ref, invp_ref, pp_s),
    )):
        g0, g1 = gains_ref[t, 0:1, :], gains_ref[t, 1:2, :]
        n2 = (vec - biases_ref[5, t:t + 1, :]) / g1
        n1 = (hidden - biases_ref[3, t:t + 1, :]) / g0
        grad_second = norm_back(up, g1, n2, inv_ref[:, 1:2])
        grad_ffn = grad_second.astype(BF16)
        grad_active = dot_nt(grad_ffn, fout_s[t])
        _, slope = gelu_pair(inn_ref[...])
        grad_inner = (grad_active * slope).astype(BF16)
        grad_hidden = grad_second + dot_nt(grad_inner, fin_s[t])
        grad_first = norm_back(grad_hidden, g0, n1, inv_ref[:, 0:1])
        gm = dot_nt(grad_first.astype(BF16), wout_s[t]).astype(BF16)
        n = HEADS * count
        heads = 4 if t == 0 else HEADS
        gq = jnp.zeros((count, 768), F32)
        slopes = []
        rows_y = out_s.reshape(512, 768)
        for h0 in range(0, HEADS, heads):
            span = slice(h0 * count, (h0 + heads) * count)
            wide = expand_heads(gm.astype(F32), h0, heads).astype(BF16)
            dp = dot_nt(wide, kv_s[t, :, 768:1536])
            soft = p_s[span, :]
            ds = (soft * (dp - jnp.sum(soft * dp, -1, keepdims=True))).astype(BF16)
            slopes.append(ds)
            gq = gq + fold_heads(dot(ds, kv_s[t, :, 0:768]), count, h0, heads)
            y = dot(ds, x_s[t]) * KEY_SCALE
            if t == 0:
                rows_y[span, :] = y.astype(BF16)
            else:
                yt_s[...] = jnp.concatenate(
                    [y, jnp.zeros((32, 768), F32)], 0
                ).T.astype(BF16).reshape(16, 48, 128)
        gq = gq * KEY_SCALE
        gq_rows.append(gq)
        wide = expand_heads(gm.astype(F32)).astype(BF16)
        spread = expand_heads(q).astype(BF16)
        if t == 0:
            for lo in range(0, 768, 256):
                q_s[0, lo:lo + 256, :] = dot_tn(rows_y[0:384, lo:lo + 256], spread).astype(BF16)
            for lo in range(0, 768, 256):
                q_s[1, lo:lo + 256, :] = dot_tn(zq_ref[:, lo:lo + 256], wide).astype(BF16)
            for c in pair:
                c.start()
        for i, ds in enumerate(slopes):
            span = slice(i * heads * count, (i + 1) * heads * count)
            kv_s[t, span, 0:tokens] = ds
        kv_s[t, n:2 * n, 0:tokens] = p_s[...].astype(BF16)
        save_dsp[t].start()
        at = 768 * t
        for lo in range(0, n, 128):
            hi = min(lo + 128, n)
            u = dot_nt(spread[lo:hi], win_s[t, :, 768:1536]) * KEY_SCALE
            x_s[0, at + lo:at + hi, :] = u.astype(BF16)
            x_s[0, at + n + lo:at + n + hi, :] = dot_nt(wide[lo:hi], win_s[t, :, 1536:2304]).astype(BF16)
        extra = dot_nt(gq.astype(BF16), win_s[t, :, 0:768]) + grad_first
        ext_ref[32 * t:32 * t + count, :] = extra
    gq_s[...] = jnp.concatenate(gq_rows + [jnp.zeros((8, 768), F32)], 0).astype(BF16)
    save_uw.start()
    for c in save_dsp:
        c.wait()

    first, second, third = gather_phases(me, g, gq_s, rgq_s, ss, rs, 15, 0, 48)
    rows_swap = []
    for i in range(1, 16):
        peer = lax.rem(me + i, 16)
        rows_swap.append(remote(yt_s.at[peer], ryt_s.at[me], as_.at[16 + i], ar.at[16 + i], (peer, g)))
    own = [
        pltpu.make_async_copy(gq_s, rgq_s.at[z, yx], lsem.at[2]),
        pltpu.make_async_copy(yt_s.at[me], ryt_s.at[me], lsem.at[3]),
    ]
    xpeer = me + 1 - 2 * lax.rem(me, 2)
    ypeer = me + 2 - 4 * (lax.rem(me, 4) // 2)
    dpeer = xpeer + 2 - 4 * (lax.rem(xpeer, 4) // 2)
    plane = []
    for k, peer in enumerate((dpeer, xpeer, ypeer)):
        for zz in range(4):
            at = pl.multiple_of(48 * (4 * zz + lax.rem(peer, 4)), 16)
            n = 1 + 4 * k + zz
            plane.append(remote(
                q_s.at[g, pl.ds(at, 48)], r1_s.at[k, zz], ks.at[n], kr.at[n], (peer, g)
            ))
    column = [
        remote(s2_s.at[lax.rem(z + d, 4)], r2_s.at[d - 1], ks.at[12 + d], kr.at[12 + d],
               (lax.rem(z + d, 4) * 4 + yx, g))
        for d in range(1, 4)
    ]

    def add_pair():
        def one(i, _):
            at = pl.ds(pl.multiple_of(48 * i, 16), 48)
            q_s[g, at, :] = (q_s[g, at, :].astype(F32) + sib_s[at, :].astype(F32)).astype(BF16)
            return 0

        lax.fori_loop(0, 16, one, 0)

    def add_plane():
        def one(i, _):
            at = pl.ds(pl.multiple_of(48 * (4 * i + yx), 16), 48)
            s2_s[i] = (
                q_s[g, at, :].astype(F32) + r1_s[0, i].astype(F32)
                + r1_s[1, i].astype(F32) + r1_s[2, i].astype(F32)
            ).astype(BF16)
            return 0

        lax.fori_loop(0, 4, one, 0)

    shares = [(pwout_s, pwout_hbm, swout_hbm), (pfin_s, pfin_hbm, sfin_hbm), (pffb_s, pffb_hbm, sffb_hbm)]
    shares += [
        (pfout_s.at[t], pfout_hbm.at[t], sfout_hbm.at[t]) for t in range(2)
    ]
    shares += [(pwin_s, pwin_hbm, swin_hbm), (psum_s, psum_hbm, ssum_hbm)]
    sends = [remote(a, c, xs.at[n], xr.at[n], sib) for n, (a, b, c) in enumerate(shares)]
    saves = [pltpu.make_async_copy(a, b, psem.at[n]) for n, (a, b, c) in enumerate(shares)]
    early, late = sends[:5] + saves[:5], sends[5:] + saves[5:]
    for c in own + first + rows_swap:
        c.start()
    for c in pair:
        c.wait()
    add_pair()
    for c in plane:
        c.start()

    psum_s[...] = jnp.zeros(psum_s.shape, F32)
    pffb_s[...] = jnp.zeros(pffb_s.shape, F32)

    def chain(t, up, hidden, vec, inv1, inv2, rows, count):
        g0, g1 = gains_ref[t, 0:1, :], gains_ref[t, 1:2, :]
        total = lambda v: jnp.sum(v, 0, keepdims=True)
        n2 = (vec.astype(F32) - biases_ref[5, t:t + 1, :]) / g1
        grad_second = norm_back(up, g1, n2, inv2)
        grad_ffn = grad_second.astype(BF16)
        x_s[1, rows, :] = grad_ffn
        psum_s[t, 1:2, :] += total(up * n2)
        psum_s[t, 6:7, :] += total(grad_ffn.astype(F32))
        psum_s[t, 7:8, :] += total(up)
        grad_hidden = grad_second
        for c in range(4):
            cols = slice(768 * c, 768 * c + 768)
            inner = dot(hidden, fin_s[t, :, cols]) + ffnb_ref[t:t + 1, cols]
            active, slope = gelu_pair(inner)
            half = slice(768 * (c % 2), 768 * (c % 2) + 768)
            kept = active if c == 0 else jnp.where(me // 4 == c, active, kept)
            grad_inner = (dot_nt(grad_ffn, fout_s[t, cols, :]) * slope).astype(BF16)
            kv_s[c // 2, rows, half] = grad_inner
            pffb_s[t:t + 1, cols] += jnp.sum(grad_inner.astype(F32), 0, keepdims=True)
            grad_hidden = grad_hidden + dot_nt(grad_inner, fin_s[t, :, cols])
        win_s[0, rows, 1536:2304] = kept.astype(BF16)
        n1 = (hidden.astype(F32) - biases_ref[3, t:t + 1, :]) / g0
        psum_s[t, 0:1, :] += total(grad_hidden * n1)
        psum_s[t, 5:6, :] += total(grad_hidden)
        grad_attn = norm_back(grad_hidden, g0, n1, inv1).astype(BF16)
        win_s[0, rows, 0:768] = grad_attn
        psum_s[t, 4:5, :] += total(grad_attn.astype(F32))
        gm = dot_nt(grad_attn, wout_s[t]).astype(BF16)
        win_s[0, rows, 768:1536] = gm
        psum_s[t, 3:4, :] += total(gm.astype(F32))

    def query_block(blk, _):
        src = pl.ds(pl.multiple_of(8 * blk, 8), 8)
        rows = pl.ds(pl.multiple_of(256 * blk, 256), 256)
        block = ga[src, 48:64].astype(F32)[:, 8:16]
        ext_q = jnp.concatenate([block[:, :, 128 * a:128 * a + 128] for a in range(1, 5)], 1)
        i1q, i2q = decode_inv(ext_q.reshape(256, 128))
        chain(
            0, query_up(rows), ga[src, 64:96].reshape(256, 768), ga[src, 0:32].reshape(256, 768),
            i1q, i2q, rows, 256,
        )

        @pl.when(blk == 0)
        def _():
            own[0].wait()
            for c in first:
                c.wait()
            for c in second:
                c.start()

        return 0

    lax.fori_loop(0, 2, query_block, 0)
    i1p, i2p = decode_inv(ga[:, 48:64].astype(F32)[:, 8:16, 0:128].reshape(128, 128))
    hv = ga[:, 32:48].astype(F32)
    chain(
        1, upp_s[...], hv[:, 0:8].reshape(128, 768).astype(BF16),
        hv[:, 8:16].reshape(128, 768).astype(BF16), i1p, i2p, slice(QR, QR + PR), 128,
    )
    for c in plane:
        c.wait()
    add_plane()
    for c in column:
        c.start()
    for c in second:
        c.wait()
    for c in third:
        c.start()

    for t, rows in enumerate((slice(0, QR), slice(QR, QR + PR))):
        count = rows.stop - rows.start
        fo_at = pl.multiple_of(1536 + lax.rem(me // 2, 2) * 384, 128)
        win_s[1, 0:384, 0:count] = win_s[0, rows, pl.ds(fo_at, 384)].astype(F32).T.astype(BF16)
        fo_row = pl.multiple_of(lax.rem(me, 2) * 192, 16)
        pfout_s[t] = dot(win_s[1, pl.ds(fo_row, 192), 0:count], x_s[1, rows, :]).astype(BF16)
        fi_at = pl.multiple_of((me // 8) * 384, 128)
        if t == 0:
            hid = ga[:, 64:96, pl.ds(fi_at, 384)].reshape(QR, 384)
        else:
            hid = ga[:, 32:48, pl.ds(fi_at, 384)].astype(F32)[:, 0:8].reshape(PR, 384)
        win_s[1, 0:384, 768:768 + count] = hid.astype(F32).T.astype(BF16)
        fi_row = pl.multiple_of(lax.rem(me, 8) * 48, 16)
        lhs = win_s[1, pl.ds(fi_row, 48), 768:768 + count]
        for h in range(2):
            pfin_s[t, :, 1536 * h:1536 * h + 1536] = dot(lhs, kv_s[h, rows, :]).astype(BF16)
        if t == 0:
            mx = rsw_ref[:, 0:32].reshape(QR, 128)
        else:
            mx = rsw_ref[:, 32:48].astype(F32)[:, 0:8].reshape(PR, 128).astype(BF16)
        pwout_s[t] = dot_tn(mx, win_s[0, rows, 0:768])[0:48].astype(BF16)
    for c in early:
        c.start()

    def low_rank(read_t, read_p, out_col):
        acc_s[...] = jnp.zeros(acc_s.shape, F32)
        pad = jnp.zeros((32, 768), F32)

        def source(i, _):
            total = acc_s[...]
            for j in (2 * i, 2 * i + 1):
                even, odd = read_p(j)
                wide = jnp.concatenate([expand_heads(even), pad, expand_heads(odd), pad], 0)
                left = jnp.concatenate([read_t(2 * j), read_t(2 * j + 1)], 1)
                total = total + dot(left, wide.astype(BF16))
            acc_s[...] = total
            return 0

        lax.fori_loop(0, 4, source, 0)
        pwin_s[1, :, out_col:out_col + 768] = acc_s[...].astype(BF16)

    def gm_p(j):
        both = win_s[0, pl.ds(pl.multiple_of(QR + j * 16, 16), 16), 768:1536].astype(F32)
        return both[0:8], both[8:16]

    low_rank(lambda i: rsw_ref[i, 48:96, :], gm_p, 1536)

    for c in third:
        c.wait()
    for c in rows_swap:
        c.wait()
    own[1].wait()

    def q_p(j):
        return tuple(ga[2 * j + u, 48:64, :].astype(F32)[0:8] for u in range(2))

    low_rank(lambda i: ryt_s[i], q_p, 768)
    rg_q = rgq_s[:, :, 0:32].reshape(QR, 768)
    rg_p = rgq_s[:, :, 32:48].astype(F32)[:, :, 0:8].reshape(PR, 768)
    pwin_s[0, :, 0:768] = dot_tn(rsw_ref[:, 0:32].reshape(QR, 128), rg_q)[64:112].astype(BF16)
    x_p = rsw_ref[:, 32:48].astype(F32)[:, 0:8].reshape(PR, 128).astype(BF16)
    pwin_s[1, :, 0:768] = dot_tn(x_p, rg_p.astype(BF16))[64:112].astype(BF16)
    for c in column:
        c.wait()
    pwin_s[0, :, pl.ds(pl.multiple_of(768 + 768 * g, 128), 768)] = (
        s2_s[z].astype(F32) + r2_s[0].astype(F32) + r2_s[1].astype(F32) + r2_s[2].astype(F32)
    ).astype(BF16)
    pwin_s[0, :, pl.ds(pl.multiple_of(1536 - 768 * g, 128), 768)] = jnp.zeros((48, 768), BF16)
    psum_s[0, 2:3, :] = jnp.sum(rg_q.astype(F32), 0, keepdims=True)
    psum_s[1, 2:3, :] = jnp.sum(rg_p, 0, keepdims=True)
    for c in late:
        c.start()
    for c in early + late:
        c.wait()
    save_uw.wait()


def run_forward(xq, xp, lengths, labels, weights):
    attn_in, attn_out, ffn_in, ffn_out, gains, biases, ffn_bias = weights
    tokens = xq.shape[0]
    vm = pl.BlockSpec(memory_space=pltpu.VMEM)
    hb = pl.BlockSpec(memory_space=pl.ANY)
    sds = jax.ShapeDtypeStruct
    parts = [
        sds((2, 48, 2304), BF16), sds((2, 48, 768), BF16), sds((2, 48, 3072), BF16),
        sds((2, 192, 768), BF16), sds((2, 8, 768), F32), sds((2, 3072), F32),
    ]
    return pl.pallas_call(
        forward_kernel,
        out_shape=[
            sds((2, tokens, 768), BF16), sds((960, 768), BF16),
            sds((768, tokens), BF16), sds((192, tokens), BF16),
        ] + parts + parts + [sds((1, 32), F32), sds((40, 768), F32)],
        in_specs=[pl.BlockSpec(memory_space=pltpu.SMEM), vm, vm, vm, vm] + [hb] * 6,
        out_specs=[hb] * 16 + [vm] * 2,
        scratch_shapes=[
            pltpu.VMEM((2, tokens, 768), BF16), pltpu.VMEM((2, tokens, 768), BF16),
            pltpu.VMEM((2, tokens, 1536), BF16),
            pltpu.VMEM((2, 768, 2304), BF16), pltpu.VMEM((2, 768, 768), BF16),
            pltpu.VMEM((2, 768, 3072), BF16), pltpu.VMEM((2, 3072, 768), BF16),
            pltpu.VMEM((384, tokens), F32), pltpu.VMEM((96, tokens), F32),
            pltpu.VMEM((2, 256, 768), BF16), pltpu.VMEM((256, 768), BF16),
            pltpu.VMEM((256, 512), F32),
            pltpu.VMEM((96, 768), BF16), pltpu.VMEM((16, 96, 128), BF16),
            pltpu.VMEM((4, 4, 96, 768), BF16), pltpu.VMEM((4, 4, 64, 768), BF16), pltpu.VMEM((16, 96, 128), BF16),
            pltpu.VMEM((32, 3072), F32), pltpu.VMEM((8, 3072), F32),
            pltpu.VMEM((32, 128), F32), pltpu.VMEM((8, 128), F32),
            pltpu.VMEM((32, 768), BF16), pltpu.VMEM((384, 768), BF16),
            pltpu.VMEM((512, 256), BF16), pltpu.VMEM((128, 768), F32),
            pltpu.VMEM((48, 768), BF16), pltpu.VMEM((4, 4, 48, 768), BF16),
            pltpu.VMEM((16, 48, 128), BF16), pltpu.VMEM((16, 48, 128), BF16),
            pltpu.VMEM((768, 768), BF16), pltpu.VMEM((3, 4, 48, 768), BF16),
            pltpu.VMEM((4, 48, 768), BF16), pltpu.VMEM((3, 48, 768), BF16),
            pltpu.VMEM((2, 48, 2304), BF16), pltpu.VMEM((2, 48, 768), BF16), pltpu.VMEM((2, 48, 3072), BF16),
            pltpu.VMEM((2, 192, 768), BF16),
            pltpu.VMEM((2, 8, 768), F32), pltpu.VMEM((2, 3072), F32), pltpu.VMEM((48, 768), F32),
            pltpu.SemaphoreType.DMA((2, 5)), pltpu.SemaphoreType.DMA((4,)), pltpu.SemaphoreType.DMA((7,)),
            pltpu.SemaphoreType.DMA((22,)), pltpu.SemaphoreType.DMA((22,)),
            pltpu.SemaphoreType.DMA((32,)), pltpu.SemaphoreType.DMA((32,)),
            pltpu.SemaphoreType.DMA((7,)), pltpu.SemaphoreType.DMA((7,)),
            pltpu.SemaphoreType.DMA((16,)), pltpu.SemaphoreType.DMA((16,)), pltpu.SemaphoreType.DMA((7,)),
        ],
        compiler_params=pltpu.CompilerParams(
            collective_id=1, has_side_effects=True, vmem_limit_bytes=65400 * 1024
        ),
        name="forward",
    )(lengths, labels.reshape(1, -1), gains, biases, ffn_bias, xq, xp, attn_in, attn_out, ffn_in, ffn_out)


def finish_kernel(
    lens_ref, loss_in, ext_ref, dspq_hbm, dspp_hbm, uw_hbm, raw_hbm, *refs,
):
    ins, outs, (loss_ref, outq_hbm, outp_hbm, dxq_hbm, dxp_hbm), scratch = (
        refs[:12], refs[12:19], refs[19:24], refs[24:]
    )
    part_s, raw_s, sum_s = scratch[:12], scratch[12], scratch[13:17]
    dx_s, dspq_ref, dspp_ref, uw_ref, psem, rsem, ssem, dsem, osem = scratch[17:]
    me, _ = place()
    raw_in = pltpu.make_async_copy(raw_hbm, raw_s, rsem.at[2])
    raw_out = [pltpu.make_async_copy(raw_s.at[t], (outq_hbm, outp_hbm)[t], rsem.at[t]) for t in range(2)]
    gets = [
        pltpu.make_async_copy(uw_hbm, uw_ref, osem.at[0]),
        pltpu.make_async_copy(dspq_hbm, dspq_ref, osem.at[1]),
        pltpu.make_async_copy(dspp_hbm, dspp_ref, osem.at[2]),
    ]
    for c in gets:
        c.start()
    raw_in.start()
    loads = [pltpu.make_async_copy(ins[k], part_s[k], psem.at[k]) for k in range(12)]
    for c in loads:
        c.start()
    loss_ref[...] = loss_in[...]

    for c in gets:
        c.wait()
    extra_p = ext_ref[32:40, :]
    e_hi = extra_p.astype(BF16).astype(F32)
    uw_p = jnp.concatenate([uw_ref[768:960, :].astype(F32), e_hi, extra_p - e_hi], 0).astype(BF16)
    keep = []
    for t in range(2):
        for m in range(4):
            cols = slice(256 * m, 256 * m + 256)
            k = t * 4 + m
            if k >= 2:
                keep[k - 2].wait()
            if t == 0:
                dx_s[k % 2] = dot_tn(dspq_ref[:, cols], uw_ref[0:768, :])
                for c in range(8):
                    dx_s[k % 2, 32 * c:32 * c + 1, :] += ext_ref[8 * m + c:8 * m + c + 1, :]
            else:
                colr = iota((8, 256), 1) + 256 * m
                rowr = iota((8, 256), 0)
                start = jnp.zeros((8, 256), jnp.int32)
                for r in range(2):
                    at = jnp.int32(r * 512)
                    for c in range(4):
                        start = jnp.where(rowr == r * 4 + c, at, start)
                        at = at + lens_ref[r, c]
                sel = jnp.where(colr == start, 1.0, 0.0)
                sel2 = jnp.concatenate([sel, sel], 0).astype(BF16)
                lhs = jnp.concatenate([dspp_ref[:, cols], sel2], 0)
                dx_s[k % 2] = dot_tn(lhs, uw_p)
            c = pltpu.make_async_copy(dx_s.at[k % 2], (dxq_hbm, dxp_hbm)[t].at[cols], dsem.at[k % 2])
            c.start()
            keep.append(c)
            if k == 1:
                raw_in.wait()
                for c in raw_out:
                    c.start()

    stores = []
    for k in range(4):
        loads[k].wait()
        loads[6 + k].wait()
        sum_s[k][...] = part_s[k][...].astype(F32) + part_s[6 + k][...].astype(F32)
        c = pltpu.make_async_copy(sum_s[k], outs[k], ssem.at[k])
        c.start()
        stores.append(c)
    for k in (4, 5, 10, 11):
        loads[k].wait()
    shift = lax.rem(768 - 48 * me, 768)
    for t in range(2):
        sums = pltpu.roll(part_s[4][t] + part_s[10][t], shift, 1)[:, 0:48]
        outs[4][t] = sums[0:2]
        for j in range(6):
            outs[5][j, t:t + 1, :] = sums[2 + j:3 + j]
    ffb = part_s[5][...] + part_s[11][...]
    wide = jnp.concatenate([ffb, jnp.zeros((6, 3072), F32)], 0)
    outs[6][...] = pltpu.roll(wide, lax.rem(3072 - 192 * me, 3072), 1)[0:2, 0:192]
    for c in keep[6:] + stores + raw_out:
        c.wait()


def finish(lengths, loss, dspq, dspp, uw, ext, raw, parts):
    sds = jax.ShapeDtypeStruct
    tokens = dspq.shape[1]
    vm = pl.BlockSpec(memory_space=pltpu.VMEM)
    hb = pl.BlockSpec(memory_space=pl.ANY)
    return pl.pallas_call(
        finish_kernel,
        out_shape=[sds(p.shape, F32) for p in parts[:4]]
        + [sds((2, 2, 48), F32), sds((6, 2, 48), F32), sds((2, 192), F32)]
        + [sds((1, 32), F32), sds((tokens, 768), BF16), sds((tokens, 768), BF16)]
        + [sds((tokens, 768), F32), sds((tokens, 768), F32)],
        in_specs=[pl.BlockSpec(memory_space=pltpu.SMEM)] + [vm] * 2 + [hb] * 16,
        out_specs=[hb] * 4 + [vm] * 4 + [hb] * 4,
        scratch_shapes=[pltpu.VMEM(p.shape, p.dtype) for p in parts]
        + [pltpu.VMEM((2, tokens, 768), BF16)]
        + [pltpu.VMEM(p.shape, F32) for p in parts[:4]]
        + [pltpu.VMEM((2, 256, 768), F32), pltpu.VMEM((768, tokens), BF16)]
        + [pltpu.VMEM((192, tokens), BF16), pltpu.VMEM((960, 768), BF16)]
        + [pltpu.SemaphoreType.DMA((n,)) for n in (12, 3, 4, 2, 3)],
        compiler_params=pltpu.CompilerParams(vmem_limit_bytes=VMEM_LIMIT),
        name="finish",
    )(lengths, loss, ext, dspq, dspp, uw, raw, *parts)


def fast_shards(query_tokens, passage_tokens, lengths, labels, *weights):
    xq = query_tokens.reshape(-1, 768)
    xp = passage_tokens.reshape(-1, 768)
    weights = weights[:5] + (weights[5].transpose(1, 0, 2), weights[6])
    raw, uw, dspq, dspp, *parts, loss, ext = run_forward(xq, xp, lengths, labels, weights)
    win, wout, fin, fout, gains, biases, ffb, loss, outq, outp, dxq, dxp = finish(
        lengths, loss, dspq, dspp, uw, ext, raw, parts
    )
    return (
        loss.reshape(-1),
        outq.reshape(query_tokens.shape),
        outp.reshape(passage_tokens.shape),
        dxq.reshape(query_tokens.shape),
        dxp.reshape(passage_tokens.shape),
        win, wout, fin, fout, gains, biases.transpose(1, 0, 2), ffb,
    )


def layer_norm(residual, gain_vec, shift_vec):
    centre = residual - jnp.mean(residual, -1, keepdims=True)
    inverse = lax.rsqrt(jnp.mean(centre * centre, -1, keepdims=True) + EPSILON)
    return centre * inverse * gain_vec + shift_vec


def plain_norm_back(residual, gain_vec, upstream):
    centre = residual - jnp.mean(residual, -1, keepdims=True)
    inverse = lax.rsqrt(jnp.mean(centre * centre, -1, keepdims=True) + EPSILON)
    normed = centre * inverse
    scaled = upstream * gain_vec
    grad_res = inverse * (
        scaled
        - jnp.mean(scaled, -1, keepdims=True)
        - normed * jnp.mean(scaled * normed, -1, keepdims=True)
    )
    return (grad_res, jnp.sum(upstream * normed, 0), jnp.sum(upstream, 0))


def cls_index(starts, seq_len):
    return (jnp.arange(starts.shape[0], dtype=jnp.int32)[:, None] * seq_len + starts).reshape(-1)


def forward(tokens, segment, starts, params):
    attn_in, attn_out, ffn_in, ffn_out, gains, biases, ffn_bias = params
    batch_size, seq_len, feature = tokens.shape
    head_count = feature // HEAD_DIM
    flat_tokens = tokens.reshape(batch_size * seq_len, feature)
    zeros_vec = jnp.zeros_like(biases[0])
    joined = jnp.dot(flat_tokens, attn_in, preferred_element_type=jnp.float32) + jnp.concatenate(
        [biases[0], zeros_vec, biases[1]]
    )
    joined = joined.astype(jnp.bfloat16)
    shaped = joined.reshape(batch_size, seq_len, 3, head_count, HEAD_DIM)
    scores = (
        jnp.einsum(
            "bqhd,bkhd->bhqk", shaped[:, :, 0], shaped[:, :, 1], preferred_element_type=jnp.float32
        )
        * KEY_SCALE
    )
    same_seg = segment[:, :, None] == segment[:, None, :]
    scores = jnp.where(same_seg[:, None], scores, -1000000000.0)
    attention = jax.nn.softmax(scores, -1).astype(jnp.bfloat16)
    mixed = jnp.einsum(
        "bhqk,bkhd->bqhd", attention, shaped[:, :, 2], preferred_element_type=jnp.float32
    )
    mixed = mixed.reshape(batch_size * seq_len, feature).astype(jnp.bfloat16)
    first_sum = flat_tokens.astype(jnp.float32) + (
        jnp.dot(mixed, attn_out, preferred_element_type=jnp.float32) + biases[2]
    )
    hidden = layer_norm(first_sum, gains[0], biases[3]).astype(jnp.bfloat16)
    inner = jnp.dot(hidden, ffn_in, preferred_element_type=jnp.float32) + ffn_bias
    active = jax.nn.gelu(inner).astype(jnp.bfloat16)
    second_sum = hidden.astype(jnp.float32) + (
        jnp.dot(active, ffn_out, preferred_element_type=jnp.float32) + biases[4]
    )
    output = layer_norm(second_sum, gains[1], biases[5]).astype(jnp.bfloat16)
    picked = cls_index(starts, seq_len)
    kept = (
        flat_tokens,
        joined,
        mixed[picked],
        first_sum[picked],
        hidden[picked],
        inner[picked],
        active[picked],
        second_sum[picked],
    )
    return (output, picked, kept)


def backward(kept, segment, starts, params, upstream):
    attn_in, attn_out, ffn_in, ffn_out, gains, biases, ffn_bias = params
    flat_tokens, joined, mixed_cls, first_cls, hidden_cls, inner_cls, active_cls, second_cls = kept
    batch_size, seq_len = segment.shape
    per_row = starts.shape[1]
    feature = flat_tokens.shape[1]
    head_count = feature // HEAD_DIM
    grad_second, gain_two, shift_two = plain_norm_back(second_cls, gains[1], upstream)
    grad_ffn = grad_second.astype(jnp.bfloat16)
    grad_down = jnp.dot(active_cls.T, grad_ffn, preferred_element_type=jnp.float32)
    grad_active = jnp.dot(grad_ffn, ffn_out.T, preferred_element_type=jnp.float32)
    grad_inner = jax.vjp(jax.nn.gelu, inner_cls)[1](grad_active)[0].astype(jnp.bfloat16)
    grad_up = jnp.dot(hidden_cls.T, grad_inner, preferred_element_type=jnp.float32)
    grad_hidden = grad_second + jnp.dot(grad_inner, ffn_in.T, preferred_element_type=jnp.float32)
    grad_first, gain_one, shift_one = plain_norm_back(first_cls, gains[0], grad_hidden)
    grad_attn = grad_first.astype(jnp.bfloat16)
    grad_outproj = jnp.dot(mixed_cls.T, grad_attn, preferred_element_type=jnp.float32)
    grad_mixed = jnp.dot(grad_attn, attn_out.T, preferred_element_type=jnp.float32).astype(
        jnp.bfloat16
    )
    grad_mixed = grad_mixed.reshape(batch_size, per_row, head_count, HEAD_DIM)
    shaped = joined.reshape(batch_size, seq_len, 3, head_count, HEAD_DIM)
    key_part = shaped[:, :, 1]
    value_part = shaped[:, :, 2]
    picked = cls_index(starts, seq_len)
    query_cls = joined[picked, :feature].reshape(batch_size, per_row, head_count, HEAD_DIM)
    own_seg = jnp.take_along_axis(segment, starts, 1)
    scores = (
        jnp.einsum("bchd,bkhd->bhck", query_cls, key_part, preferred_element_type=jnp.float32)
        * KEY_SCALE
    )
    scores = jnp.where((own_seg[:, :, None] == segment[:, None, :])[:, None], scores, -1000000000.0)
    attention = jax.nn.softmax(scores, -1)
    grad_attention = jnp.einsum(
        "bchd,bkhd->bhck", grad_mixed, value_part, preferred_element_type=jnp.float32
    )
    grad_scores = attention * (
        grad_attention - jnp.sum(attention * grad_attention, -1, keepdims=True)
    )
    grad_scores = grad_scores.astype(jnp.bfloat16)
    grad_query = (
        jnp.einsum("bhck,bkhd->bchd", grad_scores, key_part, preferred_element_type=jnp.float32)
        * KEY_SCALE
    ).astype(jnp.bfloat16)
    grad_key = (
        jnp.einsum("bhck,bchd->bkhd", grad_scores, query_cls, preferred_element_type=jnp.float32)
        * KEY_SCALE
    ).astype(jnp.bfloat16)
    grad_value = jnp.einsum(
        "bhck,bchd->bkhd",
        attention.astype(jnp.bfloat16),
        grad_mixed,
        preferred_element_type=jnp.float32,
    ).astype(jnp.bfloat16)
    places = jnp.arange(seq_len, dtype=jnp.int32)
    selector = (starts[:, :, None] == places[None, None, :]).astype(jnp.bfloat16)
    grad_query_full = jnp.einsum(
        "bcl,bchd->blhd", selector, grad_query, preferred_element_type=jnp.float32
    ).astype(jnp.bfloat16)
    grad_joined = jnp.stack([grad_query_full, grad_key, grad_value], 2).reshape(
        batch_size * seq_len, 3 * feature
    )
    grad_inproj = jnp.dot(flat_tokens.T, grad_joined, preferred_element_type=jnp.float32)
    grad_tokens = (
        jnp.dot(grad_joined, attn_in.T, preferred_element_type=jnp.float32)
        .at[picked]
        .add(grad_first)
    )
    bias_grads = jnp.stack(
        [
            jnp.sum(grad_query.astype(jnp.float32), (0, 1)).reshape(feature),
            jnp.sum(grad_value.astype(jnp.float32), (0, 1)).reshape(feature),
            jnp.sum(grad_attn.astype(jnp.float32), 0),
            shift_one,
            jnp.sum(grad_ffn.astype(jnp.float32), 0),
            shift_two,
        ]
    )
    gain_grads = jnp.stack([gain_one, gain_two])
    hidden_bias = jnp.sum(grad_inner.astype(jnp.float32), 0)
    grads = (grad_inproj, grad_outproj, grad_up, grad_down, gain_grads, bias_grads, hidden_bias)
    row_data = (hidden_cls, grad_inner, active_cls, grad_ffn)
    return (grads, grad_tokens.reshape(batch_size, seq_len, feature), row_data)


def shards(
    query_tokens,
    passage_tokens,
    lengths,
    labels,
    attn_in,
    attn_out,
    ffn_in,
    ffn_out,
    gains,
    biases,
    ffn_bias,
):
    layers = (attn_in, attn_out, ffn_in, ffn_out, gains, biases, ffn_bias)
    query_params = tuple((matrix[0] for matrix in layers))
    passage_params = tuple((matrix[1] for matrix in layers))
    query_count, query_len, feature = query_tokens.shape
    passage_len = passage_tokens.shape[1]
    query_segment = jnp.zeros((query_count, query_len), jnp.int32)
    query_starts = jnp.zeros((query_count, 1), jnp.int32)
    ends = jnp.cumsum(lengths, -1)
    passage_starts = ends - lengths
    places = jnp.arange(passage_len, dtype=jnp.int32)
    passage_segment = jnp.sum((places[None, :, None] >= ends[:, None, :]).astype(jnp.int32), -1)
    query_out, query_pick, query_kept = forward(
        query_tokens, query_segment, query_starts, query_params
    )
    passage_out, passage_pick, passage_kept = forward(
        passage_tokens, passage_segment, passage_starts, passage_params
    )
    query_vec = query_out[query_pick]
    passage_vec = passage_out[passage_pick]
    passage_count = passage_vec.shape[0]
    float_labels = labels.astype(jnp.float32)
    group_vec = lax.all_gather(passage_vec, "grp", axis=0, tiled=True)
    portion = lax.all_gather(group_vec, "blk", axis=0, tiled=True)
    running_max = jnp.full((query_count,), -1e30, jnp.float32)
    score_block = SCORE_SCALE * jnp.dot(query_vec, portion.T, preferred_element_type=jnp.float32)
    column_ids = jnp.arange(portion.shape[0], dtype=jnp.int32)
    new_max = jnp.maximum(running_max, jnp.max(score_block, -1))
    running_sum = jnp.sum(jnp.exp(score_block - new_max[:, None]), -1)
    hits = column_ids[None, :] == labels[:, None]
    positive = jnp.sum(jnp.where(hits, score_block, 0.0), -1)
    running_max, running_sum, positive = (new_max, running_sum, positive)
    norm_log = running_max + jnp.log(running_sum)
    portion = lax.all_gather(group_vec, "blk", axis=0, tiled=True)
    score_block = SCORE_SCALE * jnp.dot(query_vec, portion.T, preferred_element_type=jnp.float32)
    column_ids = jnp.arange(portion.shape[0], dtype=jnp.int32)
    hits = (column_ids[None, :] == labels[:, None]).astype(jnp.float32)
    grad_block = (jnp.exp(score_block - norm_log[:, None]) - hits).astype(jnp.bfloat16)
    query_up = SCORE_SCALE * jnp.dot(grad_block, portion, preferred_element_type=jnp.float32)
    own_ids = (
        lax.axis_index(("blk", "grp")) * passage_count + jnp.arange(passage_count, dtype=jnp.int32)
    ).astype(jnp.float32)
    remote_vec = lax.all_gather(query_vec.astype(jnp.float32), ("blk", "grp"), axis=0, tiled=True)
    remote_log = lax.all_gather(norm_log, ("blk", "grp"), axis=0, tiled=True)
    remote_label = lax.all_gather(float_labels, ("blk", "grp"), axis=0, tiled=True)
    remote_low = remote_vec.astype(jnp.bfloat16)
    score_block = SCORE_SCALE * jnp.dot(
        remote_low, passage_vec.T, preferred_element_type=jnp.float32
    )
    hits = (remote_label[:, None] == own_ids[None, :]).astype(jnp.float32)
    grad_block = (jnp.exp(score_block - remote_log[:, None]) - hits).astype(jnp.bfloat16)
    passage_up = SCORE_SCALE * jnp.dot(grad_block.T, remote_low, preferred_element_type=jnp.float32)
    query_losses = norm_log - positive
    query_grads, query_back, query_rows = backward(
        query_kept, query_segment, query_starts, query_params, query_up
    )
    passage_grads, passage_back, passage_rows = backward(
        passage_kept, passage_segment, passage_starts, passage_params, passage_up
    )
    stacked = tuple(
        (
            jnp.stack([first_part, second_part])
            for first_part, second_part in zip(query_grads, passage_grads)
        )
    )
    grad_win, grad_wout, grad_up, grad_down, grad_gain, grad_bias, grad_hidden_bias = stacked
    shares = (
        lax.psum_scatter(
            grad_win.astype(jnp.bfloat16), "blk", scatter_dimension=1, tiled=True
        ).astype(jnp.float32),
        lax.psum_scatter(
            grad_wout.astype(jnp.bfloat16), "blk", scatter_dimension=1, tiled=True
        ).astype(jnp.float32),
        lax.psum_scatter(
            grad_up.astype(jnp.bfloat16), "blk", scatter_dimension=1, tiled=True
        ).astype(jnp.float32),
        lax.psum_scatter(
            grad_down.astype(jnp.bfloat16), "blk", scatter_dimension=1, tiled=True
        ).astype(jnp.float32),
        lax.psum_scatter(
            grad_gain.astype(jnp.bfloat16), "blk", scatter_dimension=2, tiled=True
        ).astype(jnp.float32),
        lax.psum_scatter(
            grad_bias.astype(jnp.bfloat16), "blk", scatter_dimension=2, tiled=True
        ).astype(jnp.float32),
        lax.psum_scatter(
            grad_hidden_bias.astype(jnp.bfloat16), "blk", scatter_dimension=1, tiled=True
        ).astype(jnp.float32),
    )
    grad_win, grad_wout, grad_up, grad_down, grad_gain, grad_bias, grad_hidden_bias = (
        lax.psum(shares[0].astype(jnp.bfloat16), "grp").astype(jnp.float32),
        lax.psum(shares[1].astype(jnp.bfloat16), "grp").astype(jnp.float32),
        lax.psum(shares[2].astype(jnp.bfloat16), "grp").astype(jnp.float32),
        lax.psum(shares[3].astype(jnp.bfloat16), "grp").astype(jnp.float32),
        lax.psum(shares[4].astype(jnp.bfloat16), "grp").astype(jnp.float32),
        lax.psum(shares[5].astype(jnp.bfloat16), "grp").astype(jnp.float32),
        lax.psum(shares[6].astype(jnp.bfloat16), "grp").astype(jnp.float32),
    )
    query_shaped = query_out.reshape(query_count, query_len, feature)
    passage_shaped = passage_out.reshape(passage_tokens.shape)
    return (
        query_losses,
        query_shaped,
        passage_shaped,
        query_back,
        passage_back,
        grad_win,
        grad_wout,
        grad_up,
        grad_down,
        grad_gain,
        grad_bias,
        grad_hidden_bias,
    )


def solution(mesh):
    placed = (
        P(("blk", "grp"), None, None),
        P(("blk", "grp"), None, None),
        P(("blk", "grp"), None),
        P(("blk", "grp")),
        P(),
        P(),
        P(),
        P(),
        P(),
        P(),
        P(),
    )
    small = dict(mesh.shape) == {"blk": 16, "grp": 2}
    return jax.shard_map(
        fast_shards if small else shards,
        mesh=mesh,
        in_specs=placed,
        out_specs=(
            P(("blk", "grp")),
            P(("blk", "grp"), None, None),
            P(("blk", "grp"), None, None),
            P(("blk", "grp"), None, None),
            P(("blk", "grp"), None, None),
            P(None, "blk", None),
            P(None, "blk", None),
            P(None, "blk", None),
            P(None, "blk", None),
            P(None, None, "blk"),
            P(None, None, "blk"),
            P(None, "blk"),
        ),
        check_vma=False,
    )
```
